32 devices in a mesh: dp: 2 (over core), seq: 4 (over y, x), expert: 4 (over z).
Axes of the slice: x: 2, y: 2, z: 4, core: 2. Of those that a mesh axis runs over, the one named last changes fastest.
Arguments:
- query_in: bfloat16 [2, 512, 4096], P('dp', 'seq', 'expert'), may hold values from -21 to 21
- key_in: bfloat16 [2, 512, 1024], P('dp', 'seq', 'expert'), may hold values from -6 to 6
- value_in: bfloat16 [2, 512, 1024], P('dp', 'seq', 'expert'), may hold values from -6 to 6
- resid_in: bfloat16 [2, 512, 4096], P('dp', 'seq', 'expert'), may hold values from -6 to 6
- out_grad: bfloat16 [2, 512, 4096], P('dp', 'seq', 'expert'), may hold values from -6 to 6
- o_weight: bfloat16 [4096, 4096], P('expert', 'seq'), may hold values from -0.09375 to 0.09375
- router_weight: bfloat16 [4096, 4], P('expert'), may hold values from -0.09375 to 0.09375
- route_ids: int32 [2, 512, 2], P('dp', 'seq'), may hold values from 0 to 3, all different within a row; in each aligned block of 128 rows (0 to 127, 128 to 255, ..., all dimensions but the last counted through in order) at most 128 rows name the same one
- expert_out: bfloat16 [2, 2048, 4096], P('dp', ('seq', 'expert')), may hold values from -6 to 6
Outputs:
- query_grad: bfloat16 [2, 512, 4096], P('dp', 'seq', 'expert')
- key_grad: bfloat16 [2, 512, 1024], P('dp', 'seq', 'expert')
- value_grad: bfloat16 [2, 512, 1024], P('dp', 'seq', 'expert')
- router_grad: float32 [4096, 4], P('expert')
- expert_grad: bfloat16 [2, 2048, 4096], P('dp', ('seq', 'expert'))
The draws below stay inside these ranges and needn't reach their ends.
Inputs may be any that keep to these rules, and one draw needn't show every extreme that they name: `route_ids`: the two experts of a token differ; among the 128 tokens of one index of seq at most 128 name one expert, and some such group in every draw has exactly 128 naming one expert.
All inputs are finite; a program needn't handle non-finite values.
Results may differ from the reference program's by a relative error of at most 0.0078.
Values may be sent and summed in bfloat16 or wider, within the bound.
No kernel may reach another device: no remote copies, remote signals or barrier semaphores. Data moves between devices by JAX's collectives and lax.ppermute only.
A program may use at most 64 MiB of HBM per device.

```python
import math
import jax
import jax.numpy as jnp
import numpy as np
from jax import lax

HEADS = 32
KV_HEADS = 8
HEAD_DIM = 128
D = 4096
TOK_DEV = 128
EXPERTS = 4
CAP = 128
BATCH = 2
LEN = 512
SLOTS = 2048
N_SEQ = 4


def draw_key_in(key, part):
    draw_base = jnp.clip(jax.random.normal(jax.random.fold_in(key, 1), (BATCH, LEN, KV_HEADS, HEAD_DIM), jnp.float32), -6.0, 6.0)
    return draw_base.reshape(BATCH, LEN, KV_HEADS * HEAD_DIM).astype(jnp.bfloat16)


def draw_query_in(key, part):
    draw_base = jnp.clip(jax.random.normal(jax.random.fold_in(key, 2), (BATCH, LEN, HEADS, HEAD_DIM), jnp.float32), -6.0, 6.0)
    return draw_base.reshape(BATCH, LEN, HEADS * HEAD_DIM).astype(jnp.bfloat16)


def level_of(stream_key, dims, split, least, largest):
    def one(axis_at, blocks):
        steps = jax.random.uniform(jax.random.fold_in(jax.random.fold_in(stream_key, 6), axis_at), (blocks,), jnp.float32, least / len(split), largest / len(split))
        return jnp.repeat(jnp.exp(steps), dims[axis_at] // blocks).reshape((-1,) + (1,) * (len(dims) - axis_at - 1))

    factor_of = one(*split[0])
    for cut in split[1:]:
        factor_of = factor_of * one(*cut)
    return factor_of


def deal_out(key, own, number, rows, number_of, top, reach, slope):
    ranking = jax.random.permutation(key, number_of)
    heavy_load, common = portions_of(number_of, rows * top, reach, slope, True), portions_of(number_of, rows * top, reach, slope, False)
    places = jnp.arange(number_of)

    def named(lengths, rotation):
        used = int((lengths > 0).sum())
        fixed = max(1, used // 4)
        passed = fixed + (places - fixed + rotation * (used - fixed)) % max(1, number_of - fixed)
        return jnp.zeros((number_of,), jnp.int32).at[ranking[jnp.where(places < fixed, places, passed)]].set(jnp.asarray(lengths, jnp.int32))

    lengths = jnp.where(number % 4 == 0, named(heavy_load, number // 4), named(common, number - number // 4 - 1))
    mixed = jax.random.permutation(jax.random.fold_in(own, 3), number_of)
    source_of, sink = mixed[0:number_of // 2 * 2:2], mixed[1:number_of // 2 * 2:2]
    margin = jnp.minimum(lengths[source_of] - 1, reach - lengths[sink]) // 2
    margin = jnp.where((source_of == ranking[0]) | (sink == ranking[0]) | (lengths[sink] == 0), 0, jnp.maximum(margin, 0))
    passed = jax.random.randint(jax.random.fold_in(own, 4), (number_of // 2,), 0, 1 << 20) % (margin + 1)
    lengths = lengths.at[source_of].add(-passed).at[sink].add(passed)
    labels = jnp.searchsorted(jnp.cumsum(lengths), jnp.arange(rows * top), side="right").astype(jnp.int32)
    listing = labels.reshape(top, rows).T
    listing = listing[jax.random.permutation(jax.random.fold_in(own, 1), rows)]
    rotation = jax.random.randint(jax.random.fold_in(own, 2), (rows, 1), 0, top)
    return jnp.take_along_axis(listing, (jnp.arange(top)[None, :] + rotation) % top, axis=1)


def portions_of(count, total, reach, slope, full):
    portions = [(1 << 20) // math.isqrt(rank ** slope) + 1 for rank in range(1, count + 1)]
    largest = reach if full else min(reach, max(-(-total // count), total * portions[0] // sum(portions)))
    least = 1 if total - largest >= count - 1 else 0
    counts, rest = [largest] + [least] * (count - 1), total - largest - least * (count - 1)
    while rest > 0:
        free = [i for i in range(1, count) if counts[i] < largest] or [i for i in range(1, count) if counts[i] < reach]
        whole, budget = sum([portions[i] for i in free]), rest
        for i in free:
            extra = min(reach - counts[i], max(1, budget * portions[i] // whole), rest)
            counts[i] = counts[i] + extra
            rest = rest - extra
    return np.array(counts)


def scatter_about(key, shape, spread, reach, cuts=(), kind=jnp.bfloat16):
    level = level_of(key, shape, cuts, -0.22, 0.18) if cuts else 1.0
    result = jax.random.normal(key, shape, jnp.float32) * spread * level
    return jnp.minimum(jnp.maximum(result, -reach), reach).astype(kind)


def setup_inputs(seed: int = 0) -> dict:
    key_of = jax.random.split(jax.random.key(seed), 10)
    query_in = draw_query_in(jax.random.fold_in(key_of[9], 71), 0)
    key_in = draw_key_in(jax.random.fold_in(key_of[9], 71), 0)
    value_in = scatter_about(key_of[2], (BATCH, LEN, KV_HEADS * HEAD_DIM), 1.0, 6.0, ((0, 2), (1, 4), (2, 4)))
    resid_in = scatter_about(key_of[3], (BATCH, LEN, D), 1.0, 6.0, ((0, 2), (1, 4), (2, 4)))
    out_grad = scatter_about(key_of[4], (BATCH, LEN, D), 1.0, 6.0, ((0, 2), (1, 4), (2, 4)))
    o_weight = scatter_about(key_of[5], (D, D), D ** -0.5, 0.09375, ((0, 4), (1, 4)))
    router_weight = scatter_about(key_of[6], (D, EXPERTS), D ** -0.5, 0.09375, ((0, 4),))
    route_ids_keys = jax.random.split(jax.random.fold_in(key_of[7], 1), BATCH * LEN // TOK_DEV)
    route_ids_turns = jax.random.permutation(jax.random.fold_in(key_of[7], 3), BATCH * LEN // TOK_DEV)
    route_ids = jax.vmap(lambda own, number: deal_out(jax.random.fold_in(key_of[7], 2), own, number, TOK_DEV, EXPERTS, 2, CAP, 2))(route_ids_keys, route_ids_turns).reshape((BATCH, LEN, 2))
    expert_out = scatter_about(key_of[8], (BATCH, SLOTS, D), 1.0, 6.0, ((0, 2), (1, 16)))
    return {"query_in": query_in, "key_in": key_in, "value_in": value_in, "resid_in": resid_in, "out_grad": out_grad, "o_weight": o_weight, "router_weight": router_weight, "route_ids": route_ids, "expert_out": expert_out}


NEG_FILL = -1e+30
NORM_EPS = 1e-05

def attention_grads(query_seq, key_seq, value_seq, grad_seq):
    length = query_seq.shape[0]
    group_size = HEADS // KV_HEADS
    score_scale = HEAD_DIM ** (-0.5)
    query_heads = jnp.transpose(query_seq.reshape(length, KV_HEADS, group_size, HEAD_DIM), (1, 2, 0, 3))
    grad_heads = jnp.transpose(grad_seq.reshape(length, KV_HEADS, group_size, HEAD_DIM), (1, 2, 0, 3))
    key_heads = jnp.transpose(key_seq.reshape(length, KV_HEADS, HEAD_DIM), (1, 0, 2))
    value_heads = jnp.transpose(value_seq.reshape(length, KV_HEADS, HEAD_DIM), (1, 0, 2))
    token_pos = jnp.arange(length, dtype=jnp.int32)
    causal = token_pos[None, :] <= token_pos[:, None]

    def per_group(operands):
        query_group, grad_group, key_rows, value_rows = operands

        def per_head(carry_in, head_in):
            dk_acc, dv_acc = carry_in
            query_rows, grad_rows = head_in
            scores = jnp.dot(query_rows, key_rows.T, preferred_element_type=jnp.float32) * score_scale
            row_max = lax.optimization_barrier(jnp.max(jnp.where(causal, scores, NEG_FILL), axis=1))
            weights = jnp.exp(jnp.where(causal, scores - row_max[:, None], NEG_FILL))
            row_total = lax.optimization_barrier(jnp.sum(weights, axis=1))
            attn_out = jnp.dot(weights.astype(jnp.bfloat16), value_rows, preferred_element_type=jnp.float32) / row_total[:, None]
            log_norm = row_max + jnp.log(row_total)
            delta_row = lax.optimization_barrier(jnp.sum(grad_rows.astype(jnp.float32) * attn_out, axis=1))
            probs = jnp.exp(jnp.where(causal, scores - log_norm[:, None], NEG_FILL))
            dprobs = jnp.dot(grad_rows, value_rows.T, preferred_element_type=jnp.float32)
            dscores = (probs * (dprobs - delta_row[:, None])).astype(jnp.bfloat16)
            dq_rows = jnp.dot(dscores, key_rows, preferred_element_type=jnp.float32) * score_scale
            dk_acc = dk_acc + jnp.dot(dscores.T, query_rows, preferred_element_type=jnp.float32) * score_scale
            dv_acc = dv_acc + jnp.dot(probs.astype(jnp.bfloat16).T, grad_rows, preferred_element_type=jnp.float32)
            return ((dk_acc, dv_acc), dq_rows)
        zero_rows = jnp.zeros((length, HEAD_DIM), jnp.float32)
        (dk_acc, dv_acc), dq_heads = lax.scan(per_head, (zero_rows, zero_rows), (query_group, grad_group))
        return (dq_heads, dk_acc, dv_acc)
    dq_all, dk_all, dv_all = lax.map(per_group, (query_heads, grad_heads, key_heads, value_heads))
    query_grad = jnp.transpose(dq_all, (2, 0, 1, 3)).reshape(length, HEADS * HEAD_DIM).astype(jnp.bfloat16)
    key_grad = jnp.transpose(dk_all, (1, 0, 2)).reshape(length, KV_HEADS * HEAD_DIM).astype(jnp.bfloat16)
    value_grad = jnp.transpose(dv_all, (1, 0, 2)).reshape(length, KV_HEADS * HEAD_DIM).astype(jnp.bfloat16)
    return (query_grad, key_grad, value_grad)

def pick_rows(table, where_rows):
    return table[where_rows]

def place_rows(where_a, where_b, values_a, values_b):
    blank = jnp.zeros((SLOTS, D), jnp.bfloat16)
    return blank.at[where_a].set(values_a).at[where_b].set(values_b)

def reference(query_in, key_in, value_in, resid_in, out_grad, o_weight, router_weight, route_ids, expert_out):
    resid_f32 = resid_in.astype(jnp.float32)
    grad_f32 = out_grad.astype(jnp.float32)
    router_f32 = router_weight.astype(jnp.float32)
    raw_logits = jnp.einsum('bld,de->ble', resid_f32, router_f32, precision=lax.Precision.HIGHEST)
    inv_rms = lax.rsqrt(lax.optimization_barrier(jnp.sum(resid_f32 * resid_f32, axis=-1)) / D + NORM_EPS)
    logits = inv_rms[..., None] * raw_logits
    expert_iota = jnp.arange(EXPERTS, dtype=jnp.int32)
    first_mask = route_ids[..., 0:1].astype(jnp.int32) == expert_iota
    second_mask = route_ids[..., 1:2].astype(jnp.int32) == expert_iota
    choose_a = first_mask.astype(jnp.float32)
    choose_b = second_mask.astype(jnp.float32)
    logit_a = lax.optimization_barrier(jnp.sum(logits * choose_a, axis=-1))
    logit_b = lax.optimization_barrier(jnp.sum(logits * choose_b, axis=-1))
    gate_a = jax.nn.sigmoid(logit_a - logit_b)
    gate_b = jax.nn.sigmoid(logit_b - logit_a)
    member = (first_mask | second_mask).astype(jnp.int32)
    grouped = member.reshape(BATCH, N_SEQ, TOK_DEV, EXPERTS)
    slot_index = (jnp.cumsum(grouped, axis=2) - grouped).reshape(BATCH, LEN, EXPERTS).astype(jnp.int32)
    group_id = (jnp.arange(LEN, dtype=jnp.int32) // TOK_DEV).astype(jnp.int32)
    slot_row = ((group_id[None, :, None] * EXPERTS + expert_iota[None, None, :]) * CAP + slot_index).astype(jnp.int32)
    row_a = lax.optimization_barrier(jnp.sum(slot_row * first_mask.astype(jnp.int32), axis=-1)).astype(jnp.int32)
    row_b = lax.optimization_barrier(jnp.sum(slot_row * second_mask.astype(jnp.int32), axis=-1)).astype(jnp.int32)
    saved_a = jax.vmap(pick_rows)(expert_out, row_a).astype(jnp.float32)
    saved_b = jax.vmap(pick_rows)(expert_out, row_b).astype(jnp.float32)
    dgate_a = lax.optimization_barrier(jnp.sum(grad_f32 * saved_a, axis=-1))
    dgate_b = lax.optimization_barrier(jnp.sum(grad_f32 * saved_b, axis=-1))
    values_a = (gate_a[..., None] * grad_f32).astype(jnp.bfloat16)
    values_b = (gate_b[..., None] * grad_f32).astype(jnp.bfloat16)
    expert_grad = jax.vmap(place_rows)(row_a, row_b, values_a, values_b)
    dlogit_a = gate_a * gate_b * (dgate_a - dgate_b)
    dlogits = dlogit_a[..., None] * (choose_a - choose_b)
    back_proj = jnp.einsum('ble,de->bld', dlogits, router_f32, precision=lax.Precision.HIGHEST)
    along_raw = lax.optimization_barrier(jnp.sum(raw_logits * dlogits, axis=-1))
    resid_grad = grad_f32 + inv_rms[..., None] * back_proj - (along_raw * inv_rms ** 3 / D)[..., None] * resid_f32
    resid_grad = resid_grad.astype(jnp.bfloat16)
    router_grad = jnp.einsum('bld,ble->de', resid_f32, inv_rms[..., None] * dlogits, precision=lax.Precision.HIGHEST) / (BATCH * LEN)
    query_list = []
    key_list = []
    value_list = []
    for batch_row in range(BATCH):
        attn_grad = jnp.dot(resid_grad[batch_row], o_weight.T, preferred_element_type=jnp.float32).astype(jnp.bfloat16)
        grads = attention_grads(query_in[batch_row], key_in[batch_row], value_in[batch_row], attn_grad)
        query_list.append(grads[0])
        key_list.append(grads[1])
        value_list.append(grads[2])
    query_grad = jnp.stack(query_list)
    key_grad = jnp.stack(key_list)
    value_grad = jnp.stack(value_list)
    return (query_grad, key_grad, value_grad, router_grad, expert_grad)
```

```python
import math

import jax
import jax.numpy as jnp
from jax import lax
from jax.experimental import pallas as pl
from jax.experimental.pallas import tpu as pltpu
from jax.sharding import PartitionSpec as P

HEADS = 32
KV_HEADS = 8
HEAD_DIM = 128
D = 4096


NEG_FILL = -1e30
NORM_EPS = 1e-05


def head_rows(matrix, kv_count):
    tok_rows = matrix.shape[0]
    group_size = HEADS // KV_HEADS
    split_view = matrix.reshape(tok_rows, kv_count, group_size, HEAD_DIM)
    return jnp.transpose(split_view, (1, 2, 0, 3)).reshape(
        kv_count, group_size * tok_rows, HEAD_DIM
    )


def token_cols(matrix, tok_rows):
    kv_count = matrix.shape[0]
    group_size = matrix.shape[1] // tok_rows
    split_view = matrix.reshape(kv_count, group_size, tok_rows, HEAD_DIM)
    return jnp.transpose(split_view, (2, 0, 1, 3)).reshape(
        tok_rows, kv_count * group_size * HEAD_DIM
    )


def key_blocks(key_part, value_part):
    key_count = key_part.shape[0]
    block_len = math.gcd(key_count, 512)
    kv_count = key_part.shape[1] // HEAD_DIM
    steps_count = key_count // block_len
    key_stack = key_part.reshape(steps_count, block_len, kv_count, HEAD_DIM)
    value_stack = value_part.reshape(steps_count, block_len, kv_count, HEAD_DIM)
    offsets = block_len * jnp.arange(steps_count, dtype=jnp.int32)
    return (key_stack, value_stack, offsets, block_len)


def forward_fold(query_heads, query_pos):
    score_scale = HEAD_DIM ** (-0.5)

    def forward_fold_keys(carry_in, key_piece, start_row):
        key_stack, value_stack, offsets, block_len = key_blocks(key_piece[0], key_piece[1])

        def forward_one_block(carry_state, blocks):
            run_max, run_sum, run_out = carry_state
            key_block, value_block, block_start = blocks
            scores = (
                jnp.einsum(
                    "hrd,khd->hrk", query_heads, key_block, preferred_element_type=jnp.float32
                )
                * score_scale
            )
            key_pos = block_start + jnp.arange(block_len, dtype=jnp.int32)
            allowed = (key_pos[None, :] <= query_pos[:, None])[None]
            row_top = jnp.maximum(run_max, jnp.max(jnp.where(allowed, scores, NEG_FILL), axis=-1))
            weights = jnp.exp(jnp.where(allowed, scores - row_top[..., None], NEG_FILL))
            shrink = jnp.exp(run_max - row_top)
            run_sum = run_sum * shrink + jnp.sum(weights, axis=-1)
            run_out = run_out * shrink[..., None] + jnp.einsum(
                "hrk,khd->hrd",
                weights.astype(jnp.bfloat16),
                value_block,
                preferred_element_type=jnp.float32,
            )
            return ((row_top, run_sum, run_out), None)

        result, _ = lax.scan(forward_one_block, carry_in, (key_stack, value_stack, offsets))
        return result

    return forward_fold_keys


def backward_fold(query_heads, grad_heads, log_norm, delta_row, query_pos):
    score_scale = HEAD_DIM ** (-0.5)

    def backward_fold_keys(carry_in, key_piece, start_row):
        key_stack, value_stack, offsets, block_len = key_blocks(key_piece[0], key_piece[1])

        def backward_one_block(dq_acc, blocks):
            key_block, value_block, block_start = blocks
            scores = (
                jnp.einsum(
                    "hrd,khd->hrk", query_heads, key_block, preferred_element_type=jnp.float32
                )
                * score_scale
            )
            key_pos = block_start + jnp.arange(block_len, dtype=jnp.int32)
            allowed = (key_pos[None, :] <= query_pos[:, None])[None]
            probs = jnp.exp(jnp.where(allowed, scores - log_norm[..., None], NEG_FILL))
            dprobs = jnp.einsum(
                "hrd,khd->hrk", grad_heads, value_block, preferred_element_type=jnp.float32
            )
            dscores = (probs * (dprobs - delta_row[..., None])).astype(jnp.bfloat16)
            dq_acc = (
                dq_acc
                + jnp.einsum("hrk,khd->hrd", dscores, key_block, preferred_element_type=jnp.float32)
                * score_scale
            )
            dk_block = (
                jnp.einsum("hrk,hrd->khd", dscores, query_heads, preferred_element_type=jnp.float32)
                * score_scale
            )
            dv_block = jnp.einsum(
                "hrk,hrd->khd",
                probs.astype(jnp.bfloat16),
                grad_heads,
                preferred_element_type=jnp.float32,
            )
            return (dq_acc, (dk_block, dv_block))

        dq_acc, key_terms = lax.scan(
            backward_one_block, carry_in[0], (key_stack, value_stack, offsets)
        )
        key_count = key_piece[0].shape[0]
        dk_rows = key_terms[0].reshape(key_count, -1)
        dv_rows = key_terms[1].reshape(key_count, -1)
        return (dq_acc, dk_rows, dv_rows)

    return backward_fold_keys


def local(
    query_in, key_in, value_in, resid_in, out_grad, o_weight, router_weight, route_ids, expert_out
):
    query_loc = query_in[0]
    key_loc = key_in[0]
    value_loc = value_in[0]
    resid_loc = resid_in[0]
    grad_in = out_grad[0]
    route_loc = route_ids[0]
    tok_rows = query_loc.shape[0]
    expert_count = router_weight.shape[1]
    capacity = expert_out.shape[1]
    my_expert = lax.axis_index("expert")
    resid_f32 = resid_loc.astype(jnp.float32)
    raw_part = jnp.dot(resid_loc, router_weight, preferred_element_type=jnp.float32)
    square_part = jnp.sum(resid_f32 * resid_f32, axis=1)
    raw_logits, square_sums = lax.psum((raw_part, square_part), "expert")
    inv_rms = lax.rsqrt(square_sums / D + NORM_EPS)
    logits = inv_rms[:, None] * raw_logits
    expert_iota = jnp.arange(expert_count, dtype=jnp.int32)
    first_mask = route_loc[:, 0:1] == expert_iota[None, :]
    second_mask = route_loc[:, 1:2] == expert_iota[None, :]
    choose_a = first_mask.astype(jnp.float32)
    choose_b = second_mask.astype(jnp.float32)
    logit_a = jnp.sum(logits * choose_a, axis=1)
    logit_b = jnp.sum(logits * choose_b, axis=1)
    gate_a = jax.nn.sigmoid(logit_a - logit_b)
    gate_b = jax.nn.sigmoid(logit_b - logit_a)
    gate_table = gate_a[:, None] * choose_a + gate_b[:, None] * choose_b
    member = (first_mask | second_mask).astype(jnp.int32)
    slot_index = jnp.cumsum(member, axis=0) - member
    slot_iota = jnp.arange(capacity, dtype=jnp.int32)
    dispatch_mask = (member.T[:, None, :] == 1) & (
        slot_index.T[:, None, :] == slot_iota[None, :, None]
    )
    dispatch_f32 = dispatch_mask.astype(jnp.float32)
    outgoing = jnp.einsum(
        "ect,td->ecd",
        dispatch_mask.astype(jnp.bfloat16),
        grad_in,
        preferred_element_type=jnp.float32,
    ).astype(jnp.bfloat16)
    arrived = lax.all_to_all(outgoing, "expert", split_axis=0, concat_axis=2, tiled=True)
    slot_grads = arrived[0]
    saved_rows = expert_out[0]
    dgate_mine = jnp.einsum("cd,cd->c", slot_grads, saved_rows, preferred_element_type=jnp.float32)
    onehot_mine = (expert_iota == my_expert).astype(jnp.float32)
    place_mine = jnp.sum(dispatch_f32 * onehot_mine[:, None, None], axis=0)
    gate_column = jnp.sum(gate_table * onehot_mine[None, :], axis=1)
    gate_slot = jnp.sum(place_mine * gate_column[None, :], axis=1)
    expert_grad = (gate_slot[:, None] * slot_grads.astype(jnp.float32)).astype(jnp.bfloat16)
    dgate_all = lax.all_gather(dgate_mine, "expert", axis=0, tiled=True)
    dgate_tok = jnp.einsum(
        "ect,ec->te",
        dispatch_f32,
        dgate_all.reshape(expert_count, capacity),
        precision=lax.Precision.HIGHEST,
    )
    dgate_a = jnp.sum(dgate_tok * choose_a, axis=1)
    dgate_b = jnp.sum(dgate_tok * choose_b, axis=1)
    dlogit_a = gate_a * gate_b * (dgate_a - dgate_b)
    dlogits = dlogit_a[:, None] * (choose_a - choose_b)
    back_proj = jnp.dot(
        dlogits, router_weight.astype(jnp.float32).T, precision=lax.Precision.HIGHEST
    )
    along_raw = jnp.sum(raw_logits * dlogits, axis=1)
    resid_grad = (
        grad_in.astype(jnp.float32)
        + inv_rms[:, None] * back_proj
        - (along_raw * inv_rms**3 / D)[:, None] * resid_f32
    )
    resid_grad = resid_grad.astype(jnp.bfloat16)
    token_total = lax.axis_size("dp") * lax.axis_size("seq") * tok_rows
    router_part = (
        jnp.dot(resid_f32.T, inv_rms[:, None] * dlogits, precision=lax.Precision.HIGHEST)
        / token_total
    )
    router_grad = lax.psum(router_part, ("dp", "seq"))
    resid_whole = lax.all_gather(resid_grad, "expert", axis=1, tiled=True)
    attn_grad = lax.dot_general(
        resid_whole,
        lax.all_gather(o_weight, "seq", axis=1, tiled=True),
        (((1,), (1,)), ((), ())),
        preferred_element_type=jnp.float32,
    ).astype(jnp.bfloat16)
    kv_count = key_loc.shape[1] // HEAD_DIM
    group_size = HEADS // KV_HEADS
    query_heads = head_rows(query_loc, kv_count)
    grad_heads = head_rows(attn_grad, kv_count)
    seq_base = lax.axis_index("seq") * tok_rows
    query_pos = jnp.tile(seq_base + jnp.arange(tok_rows, dtype=jnp.int32), group_size)
    head_count = group_size * tok_rows
    initial = (
        jnp.full((kv_count, head_count), NEG_FILL, jnp.float32),
        jnp.zeros((kv_count, head_count), jnp.float32),
        jnp.zeros((kv_count, head_count, HEAD_DIM), jnp.float32),
    )
    fold_forward = forward_fold(query_heads, query_pos)
    every_key, every_value = (
        lax.all_gather(key_loc, "seq", axis=0, tiled=True),
        lax.all_gather(value_loc, "seq", axis=0, tiled=True),
    )
    run_max, run_sum, run_out = fold_forward(initial, (every_key, every_value), jnp.int32(0))
    log_norm = run_max + jnp.log(run_sum)
    attn_out = run_out / run_sum[..., None]
    delta_row = jnp.sum(grad_heads.astype(jnp.float32) * attn_out, axis=-1)
    zero_dq = jnp.zeros((kv_count, head_count, HEAD_DIM), jnp.float32)
    full_len = tok_rows * lax.axis_size("seq")
    zero_terms = jnp.zeros((full_len, kv_count * HEAD_DIM), jnp.float32)
    back_init = (zero_dq, zero_terms, zero_terms)
    fold_backward = backward_fold(query_heads, grad_heads, log_norm, delta_row, query_pos)
    back_out = fold_backward(back_init, (every_key, every_value), jnp.int32(0))
    query_grad = token_cols(back_out[0], tok_rows).astype(jnp.bfloat16)
    dk_rows, dv_rows = (
        lax.psum_scatter(back_out[1], "seq", scatter_dimension=0, tiled=True),
        lax.psum_scatter(back_out[2], "seq", scatter_dimension=0, tiled=True),
    )
    key_grad = dk_rows.astype(jnp.bfloat16)
    value_grad = dv_rows.astype(jnp.bfloat16)
    return (query_grad[None], key_grad[None], value_grad[None], router_grad, expert_grad[None])


ANY_VMEM = pltpu.VMEM
VMEM_LIMIT = 56 * 1024 * 1024
NT = (((1,), (1,)), ((), ()))
TN = (((0,), (0,)), ((), ()))
LANES = 128


def params():
    return pltpu.CompilerParams(vmem_limit_bytes=VMEM_LIMIT)


def partner(array, axis, count, distance):
    return lax.ppermute(array, axis, [(i, i ^ distance) for i in range(count)])


def iota(shape, axis):
    return lax.broadcasted_iota(jnp.int32, shape, axis)


def whole(shape):
    return pl.BlockSpec(shape, lambda *_: (0,) * len(shape))


def column(matrix, lane):
    lanes = iota(matrix.shape, 1)
    return jnp.sum(jnp.where(lanes == lane, matrix, 0.0), axis=1, keepdims=True)


def as_rows(matrix):
    return jnp.transpose(matrix)[0:8]


def as_columns(rows):
    count = rows.shape[1]
    return jnp.transpose(
        jnp.concatenate([rows, jnp.zeros((LANES - rows.shape[0], count), rows.dtype)], axis=0)
    )


def prepare_kernel(meta, route, router_pad, resid, saved, pack, place, saved_tok):
    my_expert = meta[2]
    tok_rows, feats = resid.shape
    capacity = saved.shape[0]
    experts = EXPERTS_ROW
    member = (route[:, 0:1] == my_expert) | (route[:, 1:2] == my_expert)
    earlier = (iota((tok_rows, tok_rows), 1) < iota((tok_rows, tok_rows), 0)).astype(
        jnp.float32
    ).astype(jnp.bfloat16)
    member_wide = jnp.broadcast_to(member.astype(jnp.float32), (tok_rows, capacity))
    slot = jnp.dot(earlier, member_wide.astype(jnp.bfloat16), preferred_element_type=jnp.float32)
    slot_lane = iota((tok_rows, capacity), 1).astype(jnp.float32)
    placed = jnp.where(slot == slot_lane, member_wide, 0.0).astype(jnp.bfloat16)
    place[...] = placed
    saved_tok[...] = jnp.dot(placed, saved[...], preferred_element_type=jnp.float32).astype(
        jnp.bfloat16
    )
    resid_f32 = resid[...].astype(jnp.float32)
    raw = jnp.dot(resid[...], router_pad[...], preferred_element_type=jnp.float32)
    square = jnp.sum(resid_f32 * resid_f32, axis=1, keepdims=True)
    lanes = iota(raw.shape, 1)
    pack[:, 0:feats] = as_rows(router_pad[...].astype(jnp.float32))
    pack[:, feats : feats + tok_rows] = as_rows(jnp.where(lanes == experts, square, raw))


def gate_grad_kernel(meta, route, saved_tok, g0, g1, g2, g3, terms):
    my_expert = meta[2]
    tok_rows, feats = g0.shape
    total = jnp.zeros((tok_rows, 1), jnp.float32)
    for k, grad in enumerate((g0, g1, g2, g3)):
        start = pl.multiple_of((my_expert ^ k) * feats, LANES)
        saved = saved_tok[:, pl.ds(start, feats)].astype(jnp.float32)
        total = total + jnp.sum(grad[...].astype(jnp.float32) * saved, axis=1, keepdims=True)
    first = (route[:, 0:1] == my_expert).astype(jnp.float32)
    second = (route[:, 1:2] == my_expert).astype(jnp.float32)
    terms[...] = as_rows(jnp.broadcast_to((first - second) * total, (tok_rows, LANES)))


def expert_grad_kernel(
    meta, route, p0, p1, p2, p3, place, g0, g1, g2, g3, expert_grad, columns
):
    my_expert = meta[2]
    tok_rows, feats = g0.shape
    experts = EXPERTS_ROW
    here = slice(feats, feats + tok_rows)
    sums = as_columns((p0[:, here] + p1[:, here]) + (p2[:, here] + p3[:, here]))
    lanes = iota(sums.shape, 1)
    inv_rms = lax.rsqrt(column(sums, experts) / D + NORM_EPS)
    logits = jnp.where(lanes < experts, sums * inv_rms, 0.0)
    first = route[:, 0:1]
    second = route[:, 1:2]
    logit_a = jnp.sum(jnp.where(lanes == first, logits, 0.0), axis=1, keepdims=True)
    logit_b = jnp.sum(jnp.where(lanes == second, logits, 0.0), axis=1, keepdims=True)
    gate_a = jax.nn.sigmoid(logit_a - logit_b)
    gate_b = jax.nn.sigmoid(logit_b - logit_a)
    gate = jnp.where(first == my_expert, gate_a, 0.0) + jnp.where(second == my_expert, gate_b, 0.0)
    columns[...] = jnp.where(
        lanes < experts, sums, jnp.where(lanes == experts, inv_rms, gate_a * gate_b)
    )
    for k, grad in enumerate((g0, g1, g2, g3)):
        start = pl.multiple_of((my_expert ^ k) * feats, LANES)
        value = (gate * grad[...].astype(jnp.float32)).astype(jnp.bfloat16)
        expert_grad[:, pl.ds(start, feats)] = lax.dot_general(
            place[...], value, TN, preferred_element_type=jnp.float32
        ).astype(jnp.bfloat16)


def router_kernel(total_tokens, route, t0, t1, t2, t3, columns, resid, dcolumns, router_part):
    experts = EXPERTS_ROW
    rows = (t0[...] + t1[...]) + (t2[...] + t3[...])
    delta = column(as_columns(rows), 0)
    cols = columns[...]
    lanes = iota(cols.shape, 1)
    inv_rms = column(cols, experts)
    dlogit_a = column(cols, experts + 1) * delta
    dlogits = jnp.where(lanes == route[:, 0:1], dlogit_a, 0.0) - jnp.where(
        lanes == route[:, 1:2], dlogit_a, 0.0
    )
    along_raw = jnp.sum(jnp.where(lanes < experts, cols, 0.0) * dlogits, axis=1, keepdims=True)
    scaled = inv_rms * dlogits
    dcolumns[...] = jnp.where(lanes == experts, along_raw * inv_rms * inv_rms * inv_rms / D, scaled)
    router_part[...] = (
        jnp.dot(
            as_rows(scaled),
            resid[...].astype(jnp.float32),
            precision=lax.Precision.HIGHEST,
            preferred_element_type=jnp.float32,
        )
        / total_tokens
    )


def resid_grad_kernel(
    meta, dcolumns, p0, p1, p2, p3, g0, g1, g2, g3, r0, r1, r2, r3, resid_grad
):
    my_expert = meta[2]
    tok_rows, feats = g0.shape
    cols = dcolumns[...]
    weights = [column(cols, e) for e in range(EXPERTS_ROW)]
    along = column(cols, EXPERTS_ROW)
    groups = ((p0, g0, r0), (p1, g1, r1), (p2, g2, r2), (p3, g3, r3))
    for k, (pack, grad, resid) in enumerate(groups):
        start = pl.multiple_of((my_expert ^ k) * feats, LANES)
        back = weights[0] * pack[0:1, 0:feats]
        for e in range(1, EXPERTS_ROW):
            back = back + weights[e] * pack[e : e + 1, 0:feats]
        resid_grad[:, pl.ds(start, feats)] = (
            grad[...].astype(jnp.float32) + back - along * resid[...].astype(jnp.float32)
        ).astype(jnp.bfloat16)


def stacked(matrix, heads):
    return jnp.concatenate(
        [matrix[:, h * HEAD_DIM : (h + 1) * HEAD_DIM] for h in range(heads)], axis=0
    )


def forward_kernel(meta, query, v0, v1, v2, v3, probs, attn_out):
    my_seq = meta[1]
    tok_rows = query.shape[0]
    kv_count = v0.shape[1] // (2 * HEAD_DIM)
    group = query.shape[1] // (kv_count * HEAD_DIM)
    rows = group * tok_rows
    position = lax.rem(iota((rows, tok_rows), 0), tok_rows)
    key_at = iota((rows, tok_rows), 1)
    allowed = jnp.concatenate(
        [key_at + ((my_seq ^ k) - my_seq) * tok_rows <= position for k in range(4)], axis=1
    )
    for kv in range(kv_count):
        heads = stacked(query[:, kv * group * HEAD_DIM : (kv + 1) * group * HEAD_DIM], group)
        key_cols = slice(kv * HEAD_DIM, (kv + 1) * HEAD_DIM)
        value_cols = slice((kv_count + kv) * HEAD_DIM, (kv_count + kv + 1) * HEAD_DIM)
        keys = jnp.concatenate([v[:, key_cols] for v in (v0, v1, v2, v3)], axis=0)
        values = jnp.concatenate([v[:, value_cols] for v in (v0, v1, v2, v3)], axis=0)
        scores = lax.dot_general(heads, keys, NT, preferred_element_type=jnp.float32) * (
            HEAD_DIM ** (-0.5)
        )
        row_max = jnp.max(jnp.where(allowed, scores, NEG_FILL), axis=1, keepdims=True)
        weights = jnp.exp(jnp.where(allowed, scores - row_max, NEG_FILL))
        row_total = jnp.sum(weights, axis=1, keepdims=True)
        mixed = (
            jnp.dot(weights.astype(jnp.bfloat16), values, preferred_element_type=jnp.float32)
            / row_total
        )
        log_norm = row_max + jnp.log(row_total)
        probs[kv] = jnp.exp(jnp.where(allowed, scores - log_norm, NEG_FILL))
        for h in range(group):
            at = (kv * group + h) * HEAD_DIM
            attn_out[:, at : at + HEAD_DIM] = mixed[h * tok_rows : (h + 1) * tok_rows]


def backward_kernel(
    meta, resid_grad, w0, w1, w2, w3, query, probs, attn_out, *rest
):
    key_refs, value_refs, (dquery, d0, d1, d2, d3, total) = rest[0:4], rest[4:8], rest[8:]
    step = pl.program_id(0)
    my_seq = meta[1]
    tok_rows = query.shape[0]
    group = query.shape[1] // HEAD_DIM
    width = w0.shape[1]
    feats = width * pl.num_programs(0)

    @pl.when(step == 0)
    def _():
        total[...] = jnp.zeros_like(total)

    for k, weight in enumerate((w0, w1, w2, w3)):
        start = pl.multiple_of((my_seq ^ k) * feats + step * width, LANES)
        total[...] += lax.dot_general(
            resid_grad[:, pl.ds(start, width)], weight[...], NT, preferred_element_type=jnp.float32
        )

    @pl.when(step == pl.num_programs(0) - 1)
    def _():
        score_scale = HEAD_DIM ** (-0.5)
        attn_grad = total[...].astype(jnp.bfloat16)
        grads = stacked(attn_grad, group)
        heads = stacked(query[...], group)
        mixed = stacked(attn_out[...], group)
        keys = jnp.concatenate([ref[...] for ref in key_refs], axis=0)
        values = jnp.concatenate([ref[...] for ref in value_refs], axis=0)
        delta = jnp.sum(grads.astype(jnp.float32) * mixed, axis=1, keepdims=True)
        dprobs = lax.dot_general(grads, values, NT, preferred_element_type=jnp.float32)
        chances = probs[0]
        dscores = (chances * (dprobs - delta)).astype(jnp.bfloat16)
        dheads = (
            jnp.dot(dscores, keys, preferred_element_type=jnp.float32) * score_scale
        ).astype(jnp.bfloat16)
        for h in range(group):
            dquery[:, h * HEAD_DIM : (h + 1) * HEAD_DIM] = dheads[h * tok_rows : (h + 1) * tok_rows]
        dkeys = lax.dot_general(dscores, heads, TN, preferred_element_type=jnp.float32) * score_scale
        dvalues = lax.dot_general(
            chances.astype(jnp.bfloat16), grads, TN, preferred_element_type=jnp.float32
        )
        for k, out in enumerate((d0, d1, d2, d3)):
            here = slice(k * tok_rows, (k + 1) * tok_rows)
            out[:, 0:HEAD_DIM] = dkeys[here].astype(out.dtype)
            out[:, HEAD_DIM : 2 * HEAD_DIM] = dvalues[here].astype(out.dtype)


def finish_kernel(meta, a0, a1, a2, a3, b0, b1, b2, b3, qa, qb, key_grad, value_grad, query_grad):
    my_core = meta[0]
    wide = qa.shape[1]
    for half, parts, dquery in ((0, (a0, a1, a2, a3), qa), (1, (b0, b1, b2, b3), qb)):
        total = parts[0][...]
        for part in parts[1:]:
            total = total + part[...].astype(jnp.float32)
        total = total.astype(jnp.bfloat16)
        head = my_core ^ half
        start = pl.multiple_of(head * HEAD_DIM, LANES)
        key_grad[:, pl.ds(start, HEAD_DIM)] = total[:, 0:HEAD_DIM]
        value_grad[:, pl.ds(start, HEAD_DIM)] = total[:, HEAD_DIM : 2 * HEAD_DIM]
        query_grad[:, pl.ds(pl.multiple_of(head * wide, LANES), wide)] = dquery[...]


EXPERTS_ROW = 4


def call(kernel, meta, args, outs):
    shapes = [jax.ShapeDtypeStruct(s, t) for s, t in outs]
    return pl.pallas_call(
        kernel,
        out_shape=shapes,
        grid_spec=pltpu.PrefetchScalarGridSpec(
            num_scalar_prefetch=1,
            grid=(1,),
            in_specs=[whole(a.shape) for a in args],
            out_specs=[whole(s.shape) for s in shapes],
        ),
        compiler_params=params(),
    )(meta, *args)


def local_fast(
    query_in, key_in, value_in, resid_in, out_grad, o_weight, router_weight, route_ids, expert_out
):
    query = query_in[0]
    resid = resid_in[0]
    grad = out_grad[0]
    route = route_ids[0]
    saved = expert_out[0]
    tok_rows, feats = resid.shape
    capacity, width = saved.shape
    seq_n, expert_n, dp_n = lax.axis_size("seq"), lax.axis_size("expert"), lax.axis_size("dp")
    core = lax.axis_index("dp")
    meta = jnp.stack([core, lax.axis_index("seq"), lax.axis_index("expert")]).astype(jnp.int32)
    f32, bf16 = jnp.float32, jnp.bfloat16

    def over_expert(array):
        return [array] + [partner(array, "expert", expert_n, k) for k in range(1, expert_n)]

    def over_seq(array):
        return [partner(array, "seq", seq_n, k) for k in range(1, seq_n)]

    half_rows = o_weight.shape[0] // dp_n
    mine = lax.dynamic_slice_in_dim(o_weight, core * half_rows, half_rows, axis=0)
    weight_mine = over_seq(mine)
    weight_other = [partner(w, "dp", dp_n, 1) for w in weight_mine]

    grads = over_expert(grad)
    resids = over_expert(resid)
    pair = jnp.concatenate([key_in[0], value_in[0]], axis=1)
    pairs = [pair] + over_seq(pair)

    router_pad = jnp.pad(router_weight, ((0, 0), (0, LANES - router_weight.shape[1])))
    pack, place, saved_tok = call(
        prepare_kernel,
        meta,
        (route, router_pad, resid, saved),
        (
            ((8, feats + tok_rows), f32),
            ((tok_rows, capacity), bf16),
            ((tok_rows, width), bf16),
        ),
    )
    packs = over_expert(pack)
    (terms,) = call(
        gate_grad_kernel, meta, (route, saved_tok, *grads), (((8, tok_rows), f32),)
    )
    all_terms = over_expert(terms)
    expert_grad, columns = call(
        expert_grad_kernel,
        meta,
        (route, *packs, place, *grads),
        (((capacity, width), bf16), ((tok_rows, LANES), f32)),
    )
    total_tokens = dp_n * seq_n * tok_rows
    dcolumns, router_part = call(
        lambda meta, *refs: router_kernel(total_tokens, *refs),
        meta,
        (route, *all_terms, columns, resid),
        (((tok_rows, LANES), f32), ((8, feats), f32)),
    )
    router_pair = router_part + partner(router_part, "dp", dp_n, 1)
    r1, r2, r3 = over_seq(router_pair)
    router_sum = (router_pair + r1) + (r2 + r3)
    router_grad = router_sum[0 : router_weight.shape[1]].T

    kv_width = key_in.shape[2]
    kv_count = kv_width // HEAD_DIM
    group = query.shape[1] // kv_width
    probs, attn_out = call(
        forward_kernel,
        meta,
        (query, *pairs),
        (
            ((kv_count, group * tok_rows, seq_n * tok_rows), f32),
            (query.shape, f32),
        ),
    )
    (resid_grad,) = call(
        resid_grad_kernel,
        meta,
        (dcolumns, *packs, *grads, *resids),
        (((tok_rows, width), bf16),),
    )

    def backward(half, weights):
        steps = 4
        wide = group * HEAD_DIM
        head = lambda i, m: m[0] ^ half
        in_specs = [
            whole(resid_grad.shape),
            pl.BlockSpec((half_rows, feats // steps), lambda i, m: (head(i, m), i)),
        ]
        in_specs += [pl.BlockSpec((half_rows, feats // steps), lambda i, m: (0, i))] * 3
        in_specs += [
            pl.BlockSpec((tok_rows, wide), lambda i, m: (0, head(i, m))),
            pl.BlockSpec((1, group * tok_rows, seq_n * tok_rows), lambda i, m: (head(i, m), 0, 0)),
            pl.BlockSpec((tok_rows, wide), lambda i, m: (0, head(i, m))),
        ]
        in_specs += [pl.BlockSpec((tok_rows, HEAD_DIM), lambda i, m: (0, head(i, m)))] * 4
        in_specs += [
            pl.BlockSpec((tok_rows, HEAD_DIM), lambda i, m: (0, kv_count + head(i, m)))
        ] * 4
        term = (tok_rows, 2 * HEAD_DIM)
        shapes = [jax.ShapeDtypeStruct((tok_rows, wide), bf16), jax.ShapeDtypeStruct(term, f32)]
        shapes += [jax.ShapeDtypeStruct(term, bf16)] * 3
        return pl.pallas_call(
            backward_kernel,
            out_shape=shapes,
            grid_spec=pltpu.PrefetchScalarGridSpec(
                num_scalar_prefetch=1,
                grid=(steps,),
                in_specs=in_specs,
                out_specs=[whole(s.shape) for s in shapes],
                scratch_shapes=[pltpu.VMEM((tok_rows, wide), f32)],
            ),
            compiler_params=params(),
        )(meta, resid_grad, o_weight, *weights, query, probs, attn_out, *pairs, *pairs)

    def send_back(terms):
        return [
            lax.ppermute(
                terms[k - 1], "seq", [(i, i ^ k) for i in range(seq_n) if i > i ^ k]
            )
            for k in range(1, seq_n)
        ]

    dquery_a, own_a, *terms_a = backward(0, weight_mine)
    back_a = send_back(terms_a)
    dquery_b, own_b, *terms_b = backward(1, weight_other)
    back_b = send_back(terms_b)
    key_grad, value_grad, query_grad = call(
        finish_kernel,
        meta,
        (own_a, *back_a, own_b, *back_b, dquery_a, dquery_b),
        (
            ((tok_rows, kv_width), bf16),
            ((tok_rows, kv_width), bf16),
            ((tok_rows, query.shape[1]), bf16),
        ),
    )
    return (query_grad[None], key_grad[None], value_grad[None], router_grad, expert_grad[None])


def solution(mesh):
    placed = (
        P("dp", "seq", "expert"),
        P("dp", "seq", "expert"),
        P("dp", "seq", "expert"),
        P("dp", "seq", "expert"),
        P("dp", "seq", "expert"),
        P("expert", "seq"),
        P("expert", None),
        P("dp", "seq", None),
        P("dp", ("seq", "expert"), None),
    )
    four = mesh.shape["dp"] == 2 and mesh.shape["seq"] == 4 and mesh.shape["expert"] == 4
    return jax.shard_map(
        local_fast if four else local,
        mesh=mesh,
        in_specs=placed,
        out_specs=(
            P("dp", "seq", "expert"),
            P("dp", "seq", "expert"),
            P("dp", "seq", "expert"),
            P("expert", None),
            P("dp", ("seq", "expert"), None),
        ),
        check_vma=False,
    )
```

```python
import math

import jax
import jax.numpy as jnp
from jax import lax
from jax.experimental import pallas as pl
from jax.experimental.pallas import tpu as pltpu
from jax.sharding import PartitionSpec as P

HEADS = 32
KV_HEADS = 8
HEAD_DIM = 128
D = 4096


NEG_FILL = -1e30
NORM_EPS = 1e-05


def head_rows(matrix, kv_count):
    tok_rows = matrix.shape[0]
    group_size = HEADS // KV_HEADS
    split_view = matrix.reshape(tok_rows, kv_count, group_size, HEAD_DIM)
    return jnp.transpose(split_view, (1, 2, 0, 3)).reshape(
        kv_count, group_size * tok_rows, HEAD_DIM
    )


def token_cols(matrix, tok_rows):
    kv_count = matrix.shape[0]
    group_size = matrix.shape[1] // tok_rows
    split_view = matrix.reshape(kv_count, group_size, tok_rows, HEAD_DIM)
    return jnp.transpose(split_view, (2, 0, 1, 3)).reshape(
        tok_rows, kv_count * group_size * HEAD_DIM
    )


def key_blocks(key_part, value_part):
    key_count = key_part.shape[0]
    block_len = math.gcd(key_count, 512)
    kv_count = key_part.shape[1] // HEAD_DIM
    steps_count = key_count // block_len
    key_stack = key_part.reshape(steps_count, block_len, kv_count, HEAD_DIM)
    value_stack = value_part.reshape(steps_count, block_len, kv_count, HEAD_DIM)
    offsets = block_len * jnp.arange(steps_count, dtype=jnp.int32)
    return (key_stack, value_stack, offsets, block_len)


def forward_fold(query_heads, query_pos):
    score_scale = HEAD_DIM ** (-0.5)

    def forward_fold_keys(carry_in, key_piece, start_row):
        key_stack, value_stack, offsets, block_len = key_blocks(key_piece[0], key_piece[1])

        def forward_one_block(carry_state, blocks):
            run_max, run_sum, run_out = carry_state
            key_block, value_block, block_start = blocks
            scores = (
                jnp.einsum(
                    "hrd,khd->hrk", query_heads, key_block, preferred_element_type=jnp.float32
                )
                * score_scale
            )
            key_pos = block_start + jnp.arange(block_len, dtype=jnp.int32)
            allowed = (key_pos[None, :] <= query_pos[:, None])[None]
            row_top = jnp.maximum(run_max, jnp.max(jnp.where(allowed, scores, NEG_FILL), axis=-1))
            weights = jnp.exp(jnp.where(allowed, scores - row_top[..., None], NEG_FILL))
            shrink = jnp.exp(run_max - row_top)
            run_sum = run_sum * shrink + jnp.sum(weights, axis=-1)
            run_out = run_out * shrink[..., None] + jnp.einsum(
                "hrk,khd->hrd",
                weights.astype(jnp.bfloat16),
                value_block,
                preferred_element_type=jnp.float32,
            )
            return ((row_top, run_sum, run_out), None)

        result, _ = lax.scan(forward_one_block, carry_in, (key_stack, value_stack, offsets))
        return result

    return forward_fold_keys


def backward_fold(query_heads, grad_heads, log_norm, delta_row, query_pos):
    score_scale = HEAD_DIM ** (-0.5)

    def backward_fold_keys(carry_in, key_piece, start_row):
        key_stack, value_stack, offsets, block_len = key_blocks(key_piece[0], key_piece[1])

        def backward_one_block(dq_acc, blocks):
            key_block, value_block, block_start = blocks
            scores = (
                jnp.einsum(
                    "hrd,khd->hrk", query_heads, key_block, preferred_element_type=jnp.float32
                )
                * score_scale
            )
            key_pos = block_start + jnp.arange(block_len, dtype=jnp.int32)
            allowed = (key_pos[None, :] <= query_pos[:, None])[None]
            probs = jnp.exp(jnp.where(allowed, scores - log_norm[..., None], NEG_FILL))
            dprobs = jnp.einsum(
                "hrd,khd->hrk", grad_heads, value_block, preferred_element_type=jnp.float32
            )
            dscores = (probs * (dprobs - delta_row[..., None])).astype(jnp.bfloat16)
            dq_acc = (
                dq_acc
                + jnp.einsum("hrk,khd->hrd", dscores, key_block, preferred_element_type=jnp.float32)
                * score_scale
            )
            dk_block = (
                jnp.einsum("hrk,hrd->khd", dscores, query_heads, preferred_element_type=jnp.float32)
                * score_scale
            )
            dv_block = jnp.einsum(
                "hrk,hrd->khd",
                probs.astype(jnp.bfloat16),
                grad_heads,
                preferred_element_type=jnp.float32,
            )
            return (dq_acc, (dk_block, dv_block))

        dq_acc, key_terms = lax.scan(
            backward_one_block, carry_in[0], (key_stack, value_stack, offsets)
        )
        key_count = key_piece[0].shape[0]
        dk_rows = key_terms[0].reshape(key_count, -1)
        dv_rows = key_terms[1].reshape(key_count, -1)
        return (dq_acc, dk_rows, dv_rows)

    return backward_fold_keys


def local(
    query_in, key_in, value_in, resid_in, out_grad, o_weight, router_weight, route_ids, expert_out
):
    query_loc = query_in[0]
    key_loc = key_in[0]
    value_loc = value_in[0]
    resid_loc = resid_in[0]
    grad_in = out_grad[0]
    route_loc = route_ids[0]
    tok_rows = query_loc.shape[0]
    expert_count = router_weight.shape[1]
    capacity = expert_out.shape[1]
    my_expert = lax.axis_index("expert")
    resid_f32 = resid_loc.astype(jnp.float32)
    raw_part = jnp.dot(resid_loc, router_weight, preferred_element_type=jnp.float32)
    square_part = jnp.sum(resid_f32 * resid_f32, axis=1)
    raw_logits, square_sums = lax.psum((raw_part, square_part), "expert")
    inv_rms = lax.rsqrt(square_sums / D + NORM_EPS)
    logits = inv_rms[:, None] * raw_logits
    expert_iota = jnp.arange(expert_count, dtype=jnp.int32)
    first_mask = route_loc[:, 0:1] == expert_iota[None, :]
    second_mask = route_loc[:, 1:2] == expert_iota[None, :]
    choose_a = first_mask.astype(jnp.float32)
    choose_b = second_mask.astype(jnp.float32)
    logit_a = jnp.sum(logits * choose_a, axis=1)
    logit_b = jnp.sum(logits * choose_b, axis=1)
    gate_a = jax.nn.sigmoid(logit_a - logit_b)
    gate_b = jax.nn.sigmoid(logit_b - logit_a)
    gate_table = gate_a[:, None] * choose_a + gate_b[:, None] * choose_b
    member = (first_mask | second_mask).astype(jnp.int32)
    slot_index = jnp.cumsum(member, axis=0) - member
    slot_iota = jnp.arange(capacity, dtype=jnp.int32)
    dispatch_mask = (member.T[:, None, :] == 1) & (
        slot_index.T[:, None, :] == slot_iota[None, :, None]
    )
    dispatch_f32 = dispatch_mask.astype(jnp.float32)
    outgoing = jnp.einsum(
        "ect,td->ecd",
        dispatch_mask.astype(jnp.bfloat16),
        grad_in,
        preferred_element_type=jnp.float32,
    ).astype(jnp.bfloat16)
    arrived = lax.all_to_all(outgoing, "expert", split_axis=0, concat_axis=2, tiled=True)
    slot_grads = arrived[0]
    saved_rows = expert_out[0]
    dgate_mine = jnp.einsum("cd,cd->c", slot_grads, saved_rows, preferred_element_type=jnp.float32)
    onehot_mine = (expert_iota == my_expert).astype(jnp.float32)
    place_mine = jnp.sum(dispatch_f32 * onehot_mine[:, None, None], axis=0)
    gate_column = jnp.sum(gate_table * onehot_mine[None, :], axis=1)
    gate_slot = jnp.sum(place_mine * gate_column[None, :], axis=1)
    expert_grad = (gate_slot[:, None] * slot_grads.astype(jnp.float32)).astype(jnp.bfloat16)
    dgate_all = lax.all_gather(dgate_mine, "expert", axis=0, tiled=True)
    dgate_tok = jnp.einsum(
        "ect,ec->te",
        dispatch_f32,
        dgate_all.reshape(expert_count, capacity),
        precision=lax.Precision.HIGHEST,
    )
    dgate_a = jnp.sum(dgate_tok * choose_a, axis=1)
    dgate_b = jnp.sum(dgate_tok * choose_b, axis=1)
    dlogit_a = gate_a * gate_b * (dgate_a - dgate_b)
    dlogits = dlogit_a[:, None] * (choose_a - choose_b)
    back_proj = jnp.dot(
        dlogits, router_weight.astype(jnp.float32).T, precision=lax.Precision.HIGHEST
    )
    along_raw = jnp.sum(raw_logits * dlogits, axis=1)
    resid_grad = (
        grad_in.astype(jnp.float32)
        + inv_rms[:, None] * back_proj
        - (along_raw * inv_rms**3 / D)[:, None] * resid_f32
    )
    resid_grad = resid_grad.astype(jnp.bfloat16)
    token_total = lax.axis_size("dp") * lax.axis_size("seq") * tok_rows
    router_part = (
        jnp.dot(resid_f32.T, inv_rms[:, None] * dlogits, precision=lax.Precision.HIGHEST)
        / token_total
    )
    router_grad = lax.psum(router_part, ("dp", "seq"))
    resid_whole = lax.all_gather(resid_grad, "expert", axis=1, tiled=True)
    attn_grad = lax.dot_general(
        resid_whole,
        lax.all_gather(o_weight, "seq", axis=1, tiled=True),
        (((1,), (1,)), ((), ())),
        preferred_element_type=jnp.float32,
    ).astype(jnp.bfloat16)
    kv_count = key_loc.shape[1] // HEAD_DIM
    group_size = HEADS // KV_HEADS
    query_heads = head_rows(query_loc, kv_count)
    grad_heads = head_rows(attn_grad, kv_count)
    seq_base = lax.axis_index("seq") * tok_rows
    query_pos = jnp.tile(seq_base + jnp.arange(tok_rows, dtype=jnp.int32), group_size)
    head_count = group_size * tok_rows
    initial = (
        jnp.full((kv_count, head_count), NEG_FILL, jnp.float32),
        jnp.zeros((kv_count, head_count), jnp.float32),
        jnp.zeros((kv_count, head_count, HEAD_DIM), jnp.float32),
    )
    fold_forward = forward_fold(query_heads, query_pos)
    every_key, every_value = (
        lax.all_gather(key_loc, "seq", axis=0, tiled=True),
        lax.all_gather(value_loc, "seq", axis=0, tiled=True),
    )
    run_max, run_sum, run_out = fold_forward(initial, (every_key, every_value), jnp.int32(0))
    log_norm = run_max + jnp.log(run_sum)
    attn_out = run_out / run_sum[..., None]
    delta_row = jnp.sum(grad_heads.astype(jnp.float32) * attn_out, axis=-1)
    zero_dq = jnp.zeros((kv_count, head_count, HEAD_DIM), jnp.float32)
    full_len = tok_rows * lax.axis_size("seq")
    zero_terms = jnp.zeros((full_len, kv_count * HEAD_DIM), jnp.float32)
    back_init = (zero_dq, zero_terms, zero_terms)
    fold_backward = backward_fold(query_heads, grad_heads, log_norm, delta_row, query_pos)
    back_out = fold_backward(back_init, (every_key, every_value), jnp.int32(0))
    query_grad = token_cols(back_out[0], tok_rows).astype(jnp.bfloat16)
    dk_rows, dv_rows = (
        lax.psum_scatter(back_out[1], "seq", scatter_dimension=0, tiled=True),
        lax.psum_scatter(back_out[2], "seq", scatter_dimension=0, tiled=True),
    )
    key_grad = dk_rows.astype(jnp.bfloat16)
    value_grad = dv_rows.astype(jnp.bfloat16)
    return (query_grad[None], key_grad[None], value_grad[None], router_grad, expert_grad[None])


VMEM_LIMIT = 16 * 1024 * 1024
NT = (((1,), (1,)), ((), ()))
TN = (((0,), (0,)), ((), ()))
LANES = 128


def params():
    return pltpu.CompilerParams(vmem_limit_bytes=VMEM_LIMIT)


def partner(array, axis, count, distance):
    return lax.ppermute(array, axis, [(i, i ^ distance) for i in range(count)])


def iota(shape, axis):
    return lax.broadcasted_iota(jnp.int32, shape, axis)


def whole(shape):
    return pl.BlockSpec(shape, lambda *_: (0,) * len(shape))


def column(matrix, lane):
    lanes = iota(matrix.shape, 1)
    return jnp.sum(jnp.where(lanes == lane, matrix, 0.0), axis=1, keepdims=True)


def as_rows(matrix):
    return jnp.transpose(matrix)[0:8]


def as_columns(rows):
    count = rows.shape[1]
    return jnp.transpose(
        jnp.concatenate([rows, jnp.zeros((LANES - rows.shape[0], count), rows.dtype)], axis=0)
    )


def prepare_kernel(meta, route, router_pad, resid, saved, rows, place, saved_tok):
    my_expert = meta[2]
    tok_rows = resid.shape[0]
    capacity = saved.shape[0]
    member = (route[:, 0:1] == my_expert) | (route[:, 1:2] == my_expert)
    earlier = (iota((tok_rows, tok_rows), 1) < iota((tok_rows, tok_rows), 0)).astype(
        jnp.float32
    ).astype(jnp.bfloat16)
    member_wide = jnp.broadcast_to(member.astype(jnp.float32), (tok_rows, capacity))
    slot = jnp.dot(earlier, member_wide.astype(jnp.bfloat16), preferred_element_type=jnp.float32)
    slot_lane = iota((tok_rows, capacity), 1).astype(jnp.float32)
    placed = jnp.where(slot == slot_lane, member_wide, 0.0).astype(jnp.bfloat16)
    place[...] = placed
    saved_tok[...] = jnp.dot(placed, saved[...], preferred_element_type=jnp.float32).astype(
        jnp.bfloat16
    )
    resid_f32 = resid[...].astype(jnp.float32)
    raw = jnp.dot(resid[...], router_pad[...], preferred_element_type=jnp.float32)
    square = jnp.sum(resid_f32 * resid_f32, axis=1, keepdims=True)
    lanes = iota(raw.shape, 1)
    rows[...] = as_rows(jnp.where(lanes == EXPERTS_ROW, square, raw))


def gate_grad_kernel(meta, route, rows, saved_tok, g0, g1, g2, g3, terms):
    my_expert = meta[2]
    tok_rows, feats = g0.shape
    total = jnp.zeros((tok_rows, 1), jnp.float32)
    for k, grad in enumerate((g0, g1, g2, g3)):
        start = pl.multiple_of((my_expert ^ k) * feats, LANES)
        saved = saved_tok[:, pl.ds(start, feats)].astype(jnp.float32)
        total = total + jnp.sum(grad[...].astype(jnp.float32) * saved, axis=1, keepdims=True)
    first = (route[:, 0:1] == my_expert).astype(jnp.float32)
    second = (route[:, 1:2] == my_expert).astype(jnp.float32)
    signed = as_rows(jnp.broadcast_to((first - second) * total, (tok_rows, LANES)))
    terms[...] = jnp.where(iota(signed.shape, 0) == EXPERTS_ROW + 1, signed, rows[...])


def router_kernel(meta, total_tokens, route, t0, t1, t2, t3, resid, columns, router_part):
    my_expert = meta[2]
    experts = EXPERTS_ROW
    sums = as_columns((t0[...] + t1[...]) + (t2[...] + t3[...]))
    lanes = iota(sums.shape, 1)
    inv_rms = lax.rsqrt(column(sums, experts) / D + NORM_EPS)
    delta = column(sums, experts + 1)
    raw = jnp.where(lanes < experts, sums, 0.0)
    logits = raw * inv_rms
    first = route[:, 0:1]
    second = route[:, 1:2]
    logit_a = jnp.sum(jnp.where(lanes == first, logits, 0.0), axis=1, keepdims=True)
    logit_b = jnp.sum(jnp.where(lanes == second, logits, 0.0), axis=1, keepdims=True)
    gate_a = jax.nn.sigmoid(logit_a - logit_b)
    gate_b = jax.nn.sigmoid(logit_b - logit_a)
    gate = jnp.where(first == my_expert, gate_a, 0.0) + jnp.where(second == my_expert, gate_b, 0.0)
    dlogit_a = gate_a * gate_b * delta
    dlogits = jnp.where(lanes == first, dlogit_a, 0.0) - jnp.where(lanes == second, dlogit_a, 0.0)
    along_raw = jnp.sum(raw * dlogits, axis=1, keepdims=True)
    scaled = inv_rms * dlogits
    along = along_raw * inv_rms * inv_rms * inv_rms / D
    columns[...] = jnp.where(
        lanes < experts, scaled, jnp.where(lanes == experts, along, gate)
    )
    router_part[...] = (
        jnp.dot(
            as_rows(scaled),
            resid[...].astype(jnp.float32),
            precision=lax.Precision.HIGHEST,
            preferred_element_type=jnp.float32,
        )
        / total_tokens
    )


def expert_grad_kernel(meta, columns, place, g0, g1, g2, g3, expert_grad):
    my_expert = meta[2]
    feats = g0.shape[1]
    gate = column(columns[...], EXPERTS_ROW + 1)
    for k, grad in enumerate((g0, g1, g2, g3)):
        start = pl.multiple_of((my_expert ^ k) * feats, LANES)
        value = (gate * grad[...].astype(jnp.float32)).astype(jnp.bfloat16)
        expert_grad[:, pl.ds(start, feats)] = lax.dot_general(
            place[...], value, TN, preferred_element_type=jnp.float32
        ).astype(jnp.bfloat16)


def resid_grad_kernel(meta, columns, g0, g1, g2, g3, r0, r1, r2, r3, resid_grad):
    my_expert = meta[2]
    tok_rows, feats = g0.shape
    cols = columns[...]
    weights = [column(cols, e) for e in range(EXPERTS_ROW)]
    along = column(cols, EXPERTS_ROW)
    for k, (grad, resid) in enumerate(((g0, r0), (g1, r1), (g2, r2), (g3, r3))):
        start = pl.multiple_of((my_expert ^ k) * feats, LANES)
        router = resid[tok_rows : tok_rows + ROW_TILE].astype(jnp.float32)
        back = weights[0] * router[0:1]
        for e in range(1, EXPERTS_ROW):
            back = back + weights[e] * router[e : e + 1]
        resid_grad[:, pl.ds(start, feats)] = (
            grad[...].astype(jnp.float32) + back - along * resid[0:tok_rows].astype(jnp.float32)
        ).astype(jnp.bfloat16)


def stacked(matrix, heads):
    return jnp.concatenate(
        [matrix[:, h * HEAD_DIM : (h + 1) * HEAD_DIM] for h in range(heads)], axis=0
    )


def forward_kernel(meta, query, v0, v1, v2, v3, probs, attn_out):
    my_seq = meta[1]
    tok_rows = query.shape[0]
    kv_count = v0.shape[1] // (2 * HEAD_DIM)
    group = query.shape[1] // (kv_count * HEAD_DIM)
    rows = group * tok_rows
    position = lax.rem(iota((rows, tok_rows), 0), tok_rows)
    key_at = iota((rows, tok_rows), 1)
    allowed = jnp.concatenate(
        [key_at + ((my_seq ^ k) - my_seq) * tok_rows <= position for k in range(4)], axis=1
    )
    for kv in range(kv_count):
        heads = stacked(query[:, kv * group * HEAD_DIM : (kv + 1) * group * HEAD_DIM], group)
        key_cols = slice(kv * HEAD_DIM, (kv + 1) * HEAD_DIM)
        value_cols = slice((kv_count + kv) * HEAD_DIM, (kv_count + kv + 1) * HEAD_DIM)
        keys = jnp.concatenate([v[:, key_cols] for v in (v0, v1, v2, v3)], axis=0)
        values = jnp.concatenate([v[:, value_cols] for v in (v0, v1, v2, v3)], axis=0)
        scores = lax.dot_general(heads, keys, NT, preferred_element_type=jnp.float32) * (
            HEAD_DIM ** (-0.5)
        )
        row_max = jnp.max(jnp.where(allowed, scores, NEG_FILL), axis=1, keepdims=True)
        weights = jnp.exp(jnp.where(allowed, scores - row_max, NEG_FILL))
        row_total = jnp.sum(weights, axis=1, keepdims=True)
        mixed = (
            jnp.dot(weights.astype(jnp.bfloat16), values, preferred_element_type=jnp.float32)
            / row_total
        )
        log_norm = row_max + jnp.log(row_total)
        probs[kv] = jnp.exp(jnp.where(allowed, scores - log_norm, NEG_FILL))
        for h in range(group):
            at = (kv * group + h) * HEAD_DIM
            attn_out[:, at : at + HEAD_DIM] = mixed[h * tok_rows : (h + 1) * tok_rows]


def backward_kernel(
    meta, resid_grad, w0, w1, w2, w3, query, probs, attn_out, *rest
):
    key_refs, value_refs, (dquery, d0, d1, d2, d3, total) = rest[0:4], rest[4:8], rest[8:]
    step = pl.program_id(0)
    my_core = meta[0]
    my_seq = meta[1]
    tok_rows = query.shape[0]
    group = query.shape[1] // HEAD_DIM
    width = w0.shape[1]
    feats = width * pl.num_programs(0)

    @pl.when(step == 0)
    def _():
        total[...] = jnp.zeros_like(total)

    for k, weight in ((0, w0), (1 + my_core, w1), (2 - my_core, w2), (3, w3)):
        start = pl.multiple_of((my_seq ^ k) * feats + step * width, LANES)
        total[...] += lax.dot_general(
            resid_grad[:, pl.ds(start, width)], weight[...], NT, preferred_element_type=jnp.float32
        )

    @pl.when(step == pl.num_programs(0) - 1)
    def _():
        score_scale = HEAD_DIM ** (-0.5)
        attn_grad = total[...].astype(jnp.bfloat16)
        grads = stacked(attn_grad, group)
        heads = stacked(query[...], group)
        mixed = stacked(attn_out[...], group)
        keys = jnp.concatenate([ref[...] for ref in key_refs], axis=0)
        values = jnp.concatenate([ref[...] for ref in value_refs], axis=0)
        delta = jnp.sum(grads.astype(jnp.float32) * mixed, axis=1, keepdims=True)
        dprobs = lax.dot_general(grads, values, NT, preferred_element_type=jnp.float32)
        chances = probs[0]
        dscores = (chances * (dprobs - delta)).astype(jnp.bfloat16)
        dheads = (
            jnp.dot(dscores, keys, preferred_element_type=jnp.float32) * score_scale
        ).astype(jnp.bfloat16)
        for h in range(group):
            dquery[:, h * HEAD_DIM : (h + 1) * HEAD_DIM] = dheads[h * tok_rows : (h + 1) * tok_rows]
        dkeys = lax.dot_general(dscores, heads, TN, preferred_element_type=jnp.float32) * score_scale
        dvalues = lax.dot_general(
            chances.astype(jnp.bfloat16), grads, TN, preferred_element_type=jnp.float32
        )
        for k, out in enumerate((d0, d1, d2, d3)):
            here = slice(k * tok_rows, (k + 1) * tok_rows)
            out[:, 0:HEAD_DIM] = dkeys[here].astype(out.dtype)
            out[:, HEAD_DIM : 2 * HEAD_DIM] = dvalues[here].astype(out.dtype)


def finish_kernel(meta, a0, a1, a2, a3, b0, b1, b2, b3, qa, qb, key_grad, value_grad, query_grad):
    my_core = meta[0]
    wide = qa.shape[1]
    for half, parts, dquery in ((0, (a0, a1, a2, a3), qa), (1, (b0, b1, b2, b3), qb)):
        total = parts[0][...]
        for part in parts[1:]:
            total = total + part[...].astype(jnp.float32)
        total = total.astype(jnp.bfloat16)
        head = my_core ^ half
        start = pl.multiple_of(head * HEAD_DIM, LANES)
        key_grad[:, pl.ds(start, HEAD_DIM)] = total[:, 0:HEAD_DIM]
        value_grad[:, pl.ds(start, HEAD_DIM)] = total[:, HEAD_DIM : 2 * HEAD_DIM]
        query_grad[:, pl.ds(pl.multiple_of(head * wide, LANES), wide)] = dquery[...]


EXPERTS_ROW = 4
ROW_TILE = 16


def call(kernel, meta, args, outs):
    shapes = [jax.ShapeDtypeStruct(s, t) for s, t in outs]
    return pl.pallas_call(
        kernel,
        out_shape=shapes,
        in_specs=[pl.BlockSpec(memory_space=pltpu.SMEM)]
        + [pl.BlockSpec(memory_space=pltpu.VMEM)] * len(args),
        out_specs=[pl.BlockSpec(memory_space=pltpu.VMEM)] * len(shapes),
        compiler_params=params(),
    )(meta, *args)


def local_fast(
    query_in, key_in, value_in, resid_in, out_grad, o_weight, router_weight, route_ids, expert_out
):
    query = query_in[0]
    resid = resid_in[0]
    grad = out_grad[0]
    route = route_ids[0]
    saved = expert_out[0]
    tok_rows, feats = resid.shape
    capacity, width = saved.shape
    seq_n, expert_n, dp_n = lax.axis_size("seq"), lax.axis_size("expert"), lax.axis_size("dp")
    core = lax.axis_index("dp")
    meta = jnp.stack([core, lax.axis_index("seq"), lax.axis_index("expert")]).astype(jnp.int32)
    f32, bf16 = jnp.float32, jnp.bfloat16

    def over_expert(array):
        return [array] + [partner(array, "expert", expert_n, k) for k in range(1, expert_n)]

    def over_seq(array):
        return [partner(array, "seq", seq_n, k) for k in range(1, seq_n)]

    def over_both(array, step):
        pairs = [
            (c * seq_n + i, c * seq_n + (i ^ step(c))) for c in range(dp_n) for i in range(seq_n)
        ]
        return lax.ppermute(array, ("dp", "seq"), pairs)

    half_rows = o_weight.shape[0] // dp_n
    grads = over_expert(grad)
    weight_near = over_both(o_weight, lambda c: 1 + c)
    pair = jnp.concatenate([key_in[0], value_in[0]], axis=1)
    pairs = [pair] + over_seq(pair)
    resid_rows = jnp.concatenate(
        [resid, jnp.pad(router_weight.T, ((0, ROW_TILE - EXPERTS_ROW), (0, 0)))], axis=0
    )
    resids = over_expert(resid_rows)
    router_pad = jnp.pad(router_weight, ((0, 0), (0, LANES - router_weight.shape[1])))
    rows, place, saved_tok = call(
        prepare_kernel,
        meta,
        (route, router_pad, resid, saved),
        (
            ((8, tok_rows), f32),
            ((tok_rows, capacity), bf16),
            ((tok_rows, width), bf16),
        ),
    )
    weight_near, grads[1:], pairs[1:], resids[1], rows, place, saved_tok = lax.optimization_barrier(
        (weight_near, grads[1:], pairs[1:], resids[1], rows, place, saved_tok)
    )
    weight_far = partner(weight_near, "dp", dp_n, 1)
    across = lax.dynamic_slice_in_dim(weight_near, core * half_rows, half_rows, axis=0)
    across_mine = over_both(across, lambda c: 2 - c)

    (terms,) = call(
        gate_grad_kernel, meta, (route, rows, saved_tok, *grads), (((8, tok_rows), f32),)
    )
    total_tokens = dp_n * seq_n * tok_rows
    columns, router_part = call(
        lambda meta, *refs: router_kernel(meta, total_tokens, *refs),
        meta,
        (route, *over_expert(terms), resid),
        (((tok_rows, LANES), f32), ((8, feats), f32)),
    )
    (expert_grad,) = call(
        expert_grad_kernel, meta, (columns, place, *grads), (((capacity, width), bf16),)
    )
    router_pair = router_part + partner(router_part, "dp", dp_n, 1)
    r1, r2, r3 = over_seq(router_pair)
    router_sum = (router_pair + r1) + (r2 + r3)

    kv_width = key_in.shape[2]
    kv_count = kv_width // HEAD_DIM
    group = query.shape[1] // kv_width
    probs, attn_out = call(
        forward_kernel,
        meta,
        (query, *pairs),
        (
            ((kv_count, group * tok_rows, seq_n * tok_rows), f32),
            (query.shape, f32),
        ),
    )
    across_mine, weight_far, resids[2:], columns, expert_grad, probs, attn_out = (
        lax.optimization_barrier(
            (across_mine, weight_far, resids[2:], columns, expert_grad, probs, attn_out)
        )
    )
    across_other = partner(across_mine, "dp", dp_n, 1)
    router_grad = router_sum[0 : router_weight.shape[1]].T
    (resid_grad,) = call(
        resid_grad_kernel,
        meta,
        (columns, *grads, *resids),
        (((tok_rows, width), bf16),),
    )

    def backward(half, weights):
        steps = 4
        wide = group * HEAD_DIM
        head = lambda i, m: m[0] ^ half
        in_specs = [
            whole(resid_grad.shape),
            pl.BlockSpec((half_rows, feats // steps), lambda i, m: (head(i, m), i)),
        ]
        in_specs += [pl.BlockSpec((half_rows, feats // steps), lambda i, m: (head(i, m), i))] * 2
        in_specs += [pl.BlockSpec((half_rows, feats // steps), lambda i, m: (0, i))]
        in_specs += [
            pl.BlockSpec((tok_rows, wide), lambda i, m: (0, head(i, m))),
            pl.BlockSpec((1, group * tok_rows, seq_n * tok_rows), lambda i, m: (head(i, m), 0, 0)),
            pl.BlockSpec((tok_rows, wide), lambda i, m: (0, head(i, m))),
        ]
        in_specs += [pl.BlockSpec((tok_rows, HEAD_DIM), lambda i, m: (0, head(i, m)))] * 4
        in_specs += [
            pl.BlockSpec((tok_rows, HEAD_DIM), lambda i, m: (0, kv_count + head(i, m)))
        ] * 4
        term = (tok_rows, 2 * HEAD_DIM)
        shapes = [jax.ShapeDtypeStruct((tok_rows, wide), bf16), jax.ShapeDtypeStruct(term, f32)]
        shapes += [jax.ShapeDtypeStruct(term, bf16)] * 3
        return pl.pallas_call(
            backward_kernel,
            out_shape=shapes,
            grid_spec=pltpu.PrefetchScalarGridSpec(
                num_scalar_prefetch=1,
                grid=(steps,),
                in_specs=in_specs,
                out_specs=[whole(s.shape) for s in shapes],
                scratch_shapes=[pltpu.VMEM((tok_rows, wide), f32)],
            ),
            compiler_params=params(),
        )(meta, resid_grad, o_weight, *weights, query, probs, attn_out, *pairs, *pairs)

    def send_back(terms):
        return [
            lax.ppermute(
                terms[k - 1], "seq", [(i, i ^ k) for i in range(seq_n) if i > i ^ k]
            )
            for k in range(1, seq_n)
        ]

    dquery_a, own_a, *terms_a = backward(0, (weight_near, weight_far, across_mine))
    back_a = send_back(terms_a)
    dquery_b, own_b, *terms_b = backward(1, (weight_near, weight_far, across_other))
    back_b = send_back(terms_b)
    key_grad, value_grad, query_grad = call(
        finish_kernel,
        meta,
        (own_a, *back_a, own_b, *back_b, dquery_a, dquery_b),
        (
            ((tok_rows, kv_width), bf16),
            ((tok_rows, kv_width), bf16),
            ((tok_rows, query.shape[1]), bf16),
        ),
    )
    return (query_grad[None], key_grad[None], value_grad[None], router_grad, expert_grad[None])


def solution(mesh):
    placed = (
        P("dp", "seq", "expert"),
        P("dp", "seq", "expert"),
        P("dp", "seq", "expert"),
        P("dp", "seq", "expert"),
        P("dp", "seq", "expert"),
        P("expert", "seq"),
        P("expert", None),
        P("dp", "seq", None),
        P("dp", ("seq", "expert"), None),
    )
    four = mesh.shape["dp"] == 2 and mesh.shape["seq"] == 4 and mesh.shape["expert"] == 4
    return jax.shard_map(
        local_fast if four else local,
        mesh=mesh,
        in_specs=placed,
        out_specs=(
            P("dp", "seq", "expert"),
            P("dp", "seq", "expert"),
            P("dp", "seq", "expert"),
            P("expert", None),
            P("dp", ("seq", "expert"), None),
        ),
        check_vma=False,
    )
```

```python
import math

import jax
import jax.numpy as jnp
from jax import lax
from jax.experimental import pallas as pl
from jax.experimental.pallas import tpu as pltpu
from jax.sharding import PartitionSpec as P

HEADS = 32
KV_HEADS = 8
HEAD_DIM = 128
D = 4096


NEG_FILL = -1e30
NORM_EPS = 1e-05


def head_rows(matrix, kv_count):
    tok_rows = matrix.shape[0]
    group_size = HEADS // KV_HEADS
    split_view = matrix.reshape(tok_rows, kv_count, group_size, HEAD_DIM)
    return jnp.transpose(split_view, (1, 2, 0, 3)).reshape(
        kv_count, group_size * tok_rows, HEAD_DIM
    )


def token_cols(matrix, tok_rows):
    kv_count = matrix.shape[0]
    group_size = matrix.shape[1] // tok_rows
    split_view = matrix.reshape(kv_count, group_size, tok_rows, HEAD_DIM)
    return jnp.transpose(split_view, (2, 0, 1, 3)).reshape(
        tok_rows, kv_count * group_size * HEAD_DIM
    )


def key_blocks(key_part, value_part):
    key_count = key_part.shape[0]
    block_len = math.gcd(key_count, 512)
    kv_count = key_part.shape[1] // HEAD_DIM
    steps_count = key_count // block_len
    key_stack = key_part.reshape(steps_count, block_len, kv_count, HEAD_DIM)
    value_stack = value_part.reshape(steps_count, block_len, kv_count, HEAD_DIM)
    offsets = block_len * jnp.arange(steps_count, dtype=jnp.int32)
    return (key_stack, value_stack, offsets, block_len)


def forward_fold(query_heads, query_pos):
    score_scale = HEAD_DIM ** (-0.5)

    def forward_fold_keys(carry_in, key_piece, start_row):
        key_stack, value_stack, offsets, block_len = key_blocks(key_piece[0], key_piece[1])

        def forward_one_block(carry_state, blocks):
            run_max, run_sum, run_out = carry_state
            key_block, value_block, block_start = blocks
            scores = (
                jnp.einsum(
                    "hrd,khd->hrk", query_heads, key_block, preferred_element_type=jnp.float32
                )
                * score_scale
            )
            key_pos = block_start + jnp.arange(block_len, dtype=jnp.int32)
            allowed = (key_pos[None, :] <= query_pos[:, None])[None]
            row_top = jnp.maximum(run_max, jnp.max(jnp.where(allowed, scores, NEG_FILL), axis=-1))
            weights = jnp.exp(jnp.where(allowed, scores - row_top[..., None], NEG_FILL))
            shrink = jnp.exp(run_max - row_top)
            run_sum = run_sum * shrink + jnp.sum(weights, axis=-1)
            run_out = run_out * shrink[..., None] + jnp.einsum(
                "hrk,khd->hrd",
                weights.astype(jnp.bfloat16),
                value_block,
                preferred_element_type=jnp.float32,
            )
            return ((row_top, run_sum, run_out), None)

        result, _ = lax.scan(forward_one_block, carry_in, (key_stack, value_stack, offsets))
        return result

    return forward_fold_keys


def backward_fold(query_heads, grad_heads, log_norm, delta_row, query_pos):
    score_scale = HEAD_DIM ** (-0.5)

    def backward_fold_keys(carry_in, key_piece, start_row):
        key_stack, value_stack, offsets, block_len = key_blocks(key_piece[0], key_piece[1])

        def backward_one_block(dq_acc, blocks):
            key_block, value_block, block_start = blocks
            scores = (
                jnp.einsum(
                    "hrd,khd->hrk", query_heads, key_block, preferred_element_type=jnp.float32
                )
                * score_scale
            )
            key_pos = block_start + jnp.arange(block_len, dtype=jnp.int32)
            allowed = (key_pos[None, :] <= query_pos[:, None])[None]
            probs = jnp.exp(jnp.where(allowed, scores - log_norm[..., None], NEG_FILL))
            dprobs = jnp.einsum(
                "hrd,khd->hrk", grad_heads, value_block, preferred_element_type=jnp.float32
            )
            dscores = (probs * (dprobs - delta_row[..., None])).astype(jnp.bfloat16)
            dq_acc = (
                dq_acc
                + jnp.einsum("hrk,khd->hrd", dscores, key_block, preferred_element_type=jnp.float32)
                * score_scale
            )
            dk_block = (
                jnp.einsum("hrk,hrd->khd", dscores, query_heads, preferred_element_type=jnp.float32)
                * score_scale
            )
            dv_block = jnp.einsum(
                "hrk,hrd->khd",
                probs.astype(jnp.bfloat16),
                grad_heads,
                preferred_element_type=jnp.float32,
            )
            return (dq_acc, (dk_block, dv_block))

        dq_acc, key_terms = lax.scan(
            backward_one_block, carry_in[0], (key_stack, value_stack, offsets)
        )
        key_count = key_piece[0].shape[0]
        dk_rows = key_terms[0].reshape(key_count, -1)
        dv_rows = key_terms[1].reshape(key_count, -1)
        return (dq_acc, dk_rows, dv_rows)

    return backward_fold_keys


def local(
    query_in, key_in, value_in, resid_in, out_grad, o_weight, router_weight, route_ids, expert_out
):
    query_loc = query_in[0]
    key_loc = key_in[0]
    value_loc = value_in[0]
    resid_loc = resid_in[0]
    grad_in = out_grad[0]
    route_loc = route_ids[0]
    tok_rows = query_loc.shape[0]
    expert_count = router_weight.shape[1]
    capacity = expert_out.shape[1]
    my_expert = lax.axis_index("expert")
    resid_f32 = resid_loc.astype(jnp.float32)
    raw_part = jnp.dot(resid_loc, router_weight, preferred_element_type=jnp.float32)
    square_part = jnp.sum(resid_f32 * resid_f32, axis=1)
    raw_logits, square_sums = lax.psum((raw_part, square_part), "expert")
    inv_rms = lax.rsqrt(square_sums / D + NORM_EPS)
    logits = inv_rms[:, None] * raw_logits
    expert_iota = jnp.arange(expert_count, dtype=jnp.int32)
    first_mask = route_loc[:, 0:1] == expert_iota[None, :]
    second_mask = route_loc[:, 1:2] == expert_iota[None, :]
    choose_a = first_mask.astype(jnp.float32)
    choose_b = second_mask.astype(jnp.float32)
    logit_a = jnp.sum(logits * choose_a, axis=1)
    logit_b = jnp.sum(logits * choose_b, axis=1)
    gate_a = jax.nn.sigmoid(logit_a - logit_b)
    gate_b = jax.nn.sigmoid(logit_b - logit_a)
    gate_table = gate_a[:, None] * choose_a + gate_b[:, None] * choose_b
    member = (first_mask | second_mask).astype(jnp.int32)
    slot_index = jnp.cumsum(member, axis=0) - member
    slot_iota = jnp.arange(capacity, dtype=jnp.int32)
    dispatch_mask = (member.T[:, None, :] == 1) & (
        slot_index.T[:, None, :] == slot_iota[None, :, None]
    )
    dispatch_f32 = dispatch_mask.astype(jnp.float32)
    outgoing = jnp.einsum(
        "ect,td->ecd",
        dispatch_mask.astype(jnp.bfloat16),
        grad_in,
        preferred_element_type=jnp.float32,
    ).astype(jnp.bfloat16)
    arrived = lax.all_to_all(outgoing, "expert", split_axis=0, concat_axis=2, tiled=True)
    slot_grads = arrived[0]
    saved_rows = expert_out[0]
    dgate_mine = jnp.einsum("cd,cd->c", slot_grads, saved_rows, preferred_element_type=jnp.float32)
    onehot_mine = (expert_iota == my_expert).astype(jnp.float32)
    place_mine = jnp.sum(dispatch_f32 * onehot_mine[:, None, None], axis=0)
    gate_column = jnp.sum(gate_table * onehot_mine[None, :], axis=1)
    gate_slot = jnp.sum(place_mine * gate_column[None, :], axis=1)
    expert_grad = (gate_slot[:, None] * slot_grads.astype(jnp.float32)).astype(jnp.bfloat16)
    dgate_all = lax.all_gather(dgate_mine, "expert", axis=0, tiled=True)
    dgate_tok = jnp.einsum(
        "ect,ec->te",
        dispatch_f32,
        dgate_all.reshape(expert_count, capacity),
        precision=lax.Precision.HIGHEST,
    )
    dgate_a = jnp.sum(dgate_tok * choose_a, axis=1)
    dgate_b = jnp.sum(dgate_tok * choose_b, axis=1)
    dlogit_a = gate_a * gate_b * (dgate_a - dgate_b)
    dlogits = dlogit_a[:, None] * (choose_a - choose_b)
    back_proj = jnp.dot(
        dlogits, router_weight.astype(jnp.float32).T, precision=lax.Precision.HIGHEST
    )
    along_raw = jnp.sum(raw_logits * dlogits, axis=1)
    resid_grad = (
        grad_in.astype(jnp.float32)
        + inv_rms[:, None] * back_proj
        - (along_raw * inv_rms**3 / D)[:, None] * resid_f32
    )
    resid_grad = resid_grad.astype(jnp.bfloat16)
    token_total = lax.axis_size("dp") * lax.axis_size("seq") * tok_rows
    router_part = (
        jnp.dot(resid_f32.T, inv_rms[:, None] * dlogits, precision=lax.Precision.HIGHEST)
        / token_total
    )
    router_grad = lax.psum(router_part, ("dp", "seq"))
    resid_whole = lax.all_gather(resid_grad, "expert", axis=1, tiled=True)
    attn_grad = lax.dot_general(
        resid_whole,
        lax.all_gather(o_weight, "seq", axis=1, tiled=True),
        (((1,), (1,)), ((), ())),
        preferred_element_type=jnp.float32,
    ).astype(jnp.bfloat16)
    kv_count = key_loc.shape[1] // HEAD_DIM
    group_size = HEADS // KV_HEADS
    query_heads = head_rows(query_loc, kv_count)
    grad_heads = head_rows(attn_grad, kv_count)
    seq_base = lax.axis_index("seq") * tok_rows
    query_pos = jnp.tile(seq_base + jnp.arange(tok_rows, dtype=jnp.int32), group_size)
    head_count = group_size * tok_rows
    initial = (
        jnp.full((kv_count, head_count), NEG_FILL, jnp.float32),
        jnp.zeros((kv_count, head_count), jnp.float32),
        jnp.zeros((kv_count, head_count, HEAD_DIM), jnp.float32),
    )
    fold_forward = forward_fold(query_heads, query_pos)
    every_key, every_value = (
        lax.all_gather(key_loc, "seq", axis=0, tiled=True),
        lax.all_gather(value_loc, "seq", axis=0, tiled=True),
    )
    run_max, run_sum, run_out = fold_forward(initial, (every_key, every_value), jnp.int32(0))
    log_norm = run_max + jnp.log(run_sum)
    attn_out = run_out / run_sum[..., None]
    delta_row = jnp.sum(grad_heads.astype(jnp.float32) * attn_out, axis=-1)
    zero_dq = jnp.zeros((kv_count, head_count, HEAD_DIM), jnp.float32)
    full_len = tok_rows * lax.axis_size("seq")
    zero_terms = jnp.zeros((full_len, kv_count * HEAD_DIM), jnp.float32)
    back_init = (zero_dq, zero_terms, zero_terms)
    fold_backward = backward_fold(query_heads, grad_heads, log_norm, delta_row, query_pos)
    back_out = fold_backward(back_init, (every_key, every_value), jnp.int32(0))
    query_grad = token_cols(back_out[0], tok_rows).astype(jnp.bfloat16)
    dk_rows, dv_rows = (
        lax.psum_scatter(back_out[1], "seq", scatter_dimension=0, tiled=True),
        lax.psum_scatter(back_out[2], "seq", scatter_dimension=0, tiled=True),
    )
    key_grad = dk_rows.astype(jnp.bfloat16)
    value_grad = dv_rows.astype(jnp.bfloat16)
    return (query_grad[None], key_grad[None], value_grad[None], router_grad, expert_grad[None])


VMEM_LIMIT = 16 * 1024 * 1024
NT = (((1,), (1,)), ((), ()))
TN = (((0,), (0,)), ((), ()))
LANES = 128


def params():
    return pltpu.CompilerParams(vmem_limit_bytes=VMEM_LIMIT)


def partner(array, axis, count, distance):
    return lax.ppermute(array, axis, [(i, i ^ distance) for i in range(count)])


def iota(shape, axis):
    return lax.broadcasted_iota(jnp.int32, shape, axis)


def whole(shape):
    return pl.BlockSpec(shape, lambda *_: (0,) * len(shape))


def column(matrix, lane):
    lanes = iota(matrix.shape, 1)
    return jnp.sum(jnp.where(lanes == lane, matrix, 0.0), axis=1, keepdims=True)


def as_rows(matrix):
    return jnp.transpose(matrix)[0:8]


def as_columns(rows):
    count = rows.shape[1]
    return jnp.transpose(
        jnp.concatenate([rows, jnp.zeros((LANES - rows.shape[0], count), rows.dtype)], axis=0)
    )


def prepare_kernel(meta, route, router_pad, resid, saved, rows, place, saved_tok):
    my_expert = meta[2]
    tok_rows = resid.shape[0]
    capacity = saved.shape[0]
    member = (route[:, 0:1] == my_expert) | (route[:, 1:2] == my_expert)
    earlier = (iota((tok_rows, tok_rows), 1) < iota((tok_rows, tok_rows), 0)).astype(
        jnp.float32
    ).astype(jnp.bfloat16)
    member_wide = jnp.broadcast_to(member.astype(jnp.float32), (tok_rows, capacity))
    slot = jnp.dot(earlier, member_wide.astype(jnp.bfloat16), preferred_element_type=jnp.float32)
    slot_lane = iota((tok_rows, capacity), 1).astype(jnp.float32)
    placed = jnp.where(slot == slot_lane, member_wide, 0.0).astype(jnp.bfloat16)
    place[...] = placed
    saved_tok[...] = jnp.dot(placed, saved[...], preferred_element_type=jnp.float32).astype(
        jnp.bfloat16
    )
    resid_f32 = resid[...].astype(jnp.float32)
    raw = jnp.dot(resid[...], router_pad[...], preferred_element_type=jnp.float32)
    square = jnp.sum(resid_f32 * resid_f32, axis=1, keepdims=True)
    lanes = iota(raw.shape, 1)
    rows[...] = as_rows(jnp.where(lanes == EXPERTS_ROW, square, raw))


def spread(my_expert, refs, rows):
    for k, ref in enumerate(refs):
        yield my_expert ^ k, lambda ref=ref: ref[rows].astype(jnp.float32)


def gate_grad_kernel(meta, route, rows, saved_tok, *refs):
    blocks, terms = refs[:-1], refs[-1]
    my_expert = meta[2]
    tok_rows = route.shape[0]
    feats = blocks[0].shape[1]
    total = jnp.zeros((tok_rows, 1), jnp.float32)
    for index, grad in spread(my_expert, blocks, slice(0, tok_rows)):
        start = pl.multiple_of(index * feats, LANES)
        saved = saved_tok[:, pl.ds(start, feats)].astype(jnp.float32)
        total = total + jnp.sum(grad() * saved, axis=1, keepdims=True)
    first = (route[:, 0:1] == my_expert).astype(jnp.float32)
    second = (route[:, 1:2] == my_expert).astype(jnp.float32)
    signed = as_rows(jnp.broadcast_to((first - second) * total, (tok_rows, LANES)))
    terms[...] = jnp.where(iota(signed.shape, 0) == EXPERTS_ROW + 1, signed, rows[...])


def router_kernel(meta, total_tokens, route, t0, t1, t2, t3, resid, columns, router_part):
    my_expert = meta[2]
    experts = EXPERTS_ROW
    sums = as_columns((t0[...] + t1[...]) + (t2[...] + t3[...]))
    lanes = iota(sums.shape, 1)
    inv_rms = lax.rsqrt(column(sums, experts) / D + NORM_EPS)
    delta = column(sums, experts + 1)
    raw = jnp.where(lanes < experts, sums, 0.0)
    logits = raw * inv_rms
    first = route[:, 0:1]
    second = route[:, 1:2]
    logit_a = jnp.sum(jnp.where(lanes == first, logits, 0.0), axis=1, keepdims=True)
    logit_b = jnp.sum(jnp.where(lanes == second, logits, 0.0), axis=1, keepdims=True)
    gate_a = jax.nn.sigmoid(logit_a - logit_b)
    gate_b = jax.nn.sigmoid(logit_b - logit_a)
    gate = jnp.where(first == my_expert, gate_a, 0.0) + jnp.where(second == my_expert, gate_b, 0.0)
    dlogit_a = gate_a * gate_b * delta
    dlogits = jnp.where(lanes == first, dlogit_a, 0.0) - jnp.where(lanes == second, dlogit_a, 0.0)
    along_raw = jnp.sum(raw * dlogits, axis=1, keepdims=True)
    scaled = inv_rms * dlogits
    along = along_raw * inv_rms * inv_rms * inv_rms / D
    columns[...] = jnp.where(
        lanes < experts, scaled, jnp.where(lanes == experts, along, gate)
    )
    router_part[...] = (
        jnp.dot(
            as_rows(scaled),
            resid[...].astype(jnp.float32),
            precision=lax.Precision.HIGHEST,
            preferred_element_type=jnp.float32,
        )
        / total_tokens
    )


def expert_grad_kernel(meta, columns, place, *refs):
    blocks, expert_grad = refs[:-1], refs[-1]
    tok_rows = place.shape[0]
    feats = blocks[0].shape[1]
    gate = column(columns[...], EXPERTS_ROW + 1)
    for index, grad in spread(meta[2], blocks, slice(0, tok_rows)):
        start = pl.multiple_of(index * feats, LANES)
        value = (gate * grad()).astype(jnp.bfloat16)
        expert_grad[:, pl.ds(start, feats)] = lax.dot_general(
            place[...], value, TN, preferred_element_type=jnp.float32
        ).astype(jnp.bfloat16)


def project_kernel(meta, *refs):
    weights, grads, resids = refs[0:5], refs[5:9], refs[9:13]
    total, rows = refs[13:]
    my_core, my_seq, my_expert = meta[0], meta[1], meta[2]
    step = pl.program_id(0)
    tok_rows, feats = grads[0].shape
    width = weights[0].shape[1]
    half = weights[3].shape[0]

    @pl.when(step == 0)
    def _():
        total[...] = jnp.zeros_like(total)
        for k in range(4):
            rows[my_expert ^ k, 0:tok_rows] = grads[k][...]
            rows[my_expert ^ k, tok_rows:] = resids[k][...]

    columns = pl.ds(pl.multiple_of(step * width, LANES), width)
    for k, weight in ((0, weights[0]), (1 + my_core, weights[1]), (2 - my_core, weights[2])):
        total[...] += lax.dot_general(
            rows[my_seq ^ k, :, columns], weight[...], NT, preferred_element_type=jnp.float32
        )
    for part, weight in ((my_core, weights[3]), (1 - my_core, weights[4])):
        total[:, pl.ds(pl.multiple_of(part * half, LANES), half)] += lax.dot_general(
            rows[my_seq ^ 3, :, columns], weight[...], NT, preferred_element_type=jnp.float32
        )


def stacked(matrix, heads):
    return jnp.concatenate(
        [matrix[:, h * HEAD_DIM : (h + 1) * HEAD_DIM] for h in range(heads)], axis=0
    )


def forward_kernel(meta, query, v0, v1, v2, v3, probs, attn_out):
    my_seq = meta[1]
    tok_rows = query.shape[0]
    kv_count = v0.shape[1] // (2 * HEAD_DIM)
    group = query.shape[1] // (kv_count * HEAD_DIM)
    rows = group * tok_rows
    position = lax.rem(iota((rows, tok_rows), 0), tok_rows)
    key_at = iota((rows, tok_rows), 1)
    allowed = jnp.concatenate(
        [key_at + ((my_seq ^ k) - my_seq) * tok_rows <= position for k in range(4)], axis=1
    )
    for kv in range(kv_count):
        heads = stacked(query[:, kv * group * HEAD_DIM : (kv + 1) * group * HEAD_DIM], group)
        key_cols = slice(kv * HEAD_DIM, (kv + 1) * HEAD_DIM)
        value_cols = slice((kv_count + kv) * HEAD_DIM, (kv_count + kv + 1) * HEAD_DIM)
        keys = jnp.concatenate([v[:, key_cols] for v in (v0, v1, v2, v3)], axis=0)
        values = jnp.concatenate([v[:, value_cols] for v in (v0, v1, v2, v3)], axis=0)
        scores = lax.dot_general(heads, keys, NT, preferred_element_type=jnp.float32) * (
            HEAD_DIM ** (-0.5)
        )
        row_max = jnp.max(jnp.where(allowed, scores, NEG_FILL), axis=1, keepdims=True)
        weights = jnp.exp(jnp.where(allowed, scores - row_max, NEG_FILL))
        row_total = jnp.sum(weights, axis=1, keepdims=True)
        mixed = (
            jnp.dot(weights.astype(jnp.bfloat16), values, preferred_element_type=jnp.float32)
            / row_total
        )
        log_norm = row_max + jnp.log(row_total)
        probs[kv] = jnp.exp(jnp.where(allowed, scores - log_norm, NEG_FILL))
        for h in range(group):
            at = (kv * group + h) * HEAD_DIM
            attn_out[:, at : at + HEAD_DIM] = mixed[h * tok_rows : (h + 1) * tok_rows]


def backward_kernel(
    meta, columns, projected, router, query, probs, attn_out, v0, v1, v2, v3,
    dquery, d0, d1, d2, d3,
):
    tok_rows = query.shape[0]
    kv_count = v0.shape[1] // (2 * HEAD_DIM)
    group = query.shape[1] // (kv_count * HEAD_DIM)
    wide = group * HEAD_DIM
    score_scale = HEAD_DIM ** (-0.5)
    cols = columns[...]
    weights = [column(cols, e) for e in range(EXPERTS_ROW)]
    along = column(cols, EXPERTS_ROW)
    for kv in range(kv_count):
        here = slice(kv * wide, (kv + 1) * wide)
        attn_grad = projected[0:tok_rows, here] - along * projected[tok_rows : 2 * tok_rows, here]
        for e in range(EXPERTS_ROW):
            attn_grad = attn_grad + weights[e] * projected[2 * tok_rows + e : 2 * tok_rows + e + 1, here]
        grads = stacked(attn_grad.astype(jnp.bfloat16), group)
        heads = stacked(query[:, here], group)
        mixed = stacked(attn_out[:, here], group)
        key_cols = slice(kv * HEAD_DIM, (kv + 1) * HEAD_DIM)
        value_cols = slice((kv_count + kv) * HEAD_DIM, (kv_count + kv + 1) * HEAD_DIM)
        keys = jnp.concatenate([v[:, key_cols] for v in (v0, v1, v2, v3)], axis=0)
        values = jnp.concatenate([v[:, value_cols] for v in (v0, v1, v2, v3)], axis=0)
        delta = jnp.sum(grads.astype(jnp.float32) * mixed, axis=1, keepdims=True)
        dprobs = lax.dot_general(grads, values, NT, preferred_element_type=jnp.float32)
        chances = probs[kv]
        dscores = (chances * (dprobs - delta)).astype(jnp.bfloat16)
        dheads = (
            jnp.dot(dscores, keys, preferred_element_type=jnp.float32) * score_scale
        ).astype(jnp.bfloat16)
        for h in range(group):
            at = (kv * group + h) * HEAD_DIM
            dquery[:, at : at + HEAD_DIM] = dheads[h * tok_rows : (h + 1) * tok_rows]
        dkeys = lax.dot_general(dscores, heads, TN, preferred_element_type=jnp.float32) * score_scale
        dvalues = lax.dot_general(
            chances.astype(jnp.bfloat16), grads, TN, preferred_element_type=jnp.float32
        )
        for k, out in enumerate((d0, d1, d2, d3)):
            part = slice(k * tok_rows, (k + 1) * tok_rows)
            out[0:tok_rows, key_cols] = dkeys[part].astype(out.dtype)
            out[0:tok_rows, value_cols] = dvalues[part].astype(out.dtype)
    for out in (d1, d2, d3):
        out[tok_rows:] = router[...]


def router_pair_kernel(meta, mine, other, rows):
    part = mine[...] + other[...]
    width = rows.shape[1]
    high = part.astype(jnp.bfloat16).astype(jnp.float32)
    pieces = [
        half[0:EXPERTS_ROW, at : at + width]
        for half in (high, part - high)
        for at in range(0, part.shape[1], width)
    ]
    rows[...] = jnp.concatenate(pieces, axis=0).astype(jnp.bfloat16)


def finish_kernel(meta, router, own, t1, t2, t3, key_grad, value_grad, router_grad):
    tok_rows, kv_width = key_grad.shape
    total = own[...]
    for part in (t1, t2, t3):
        total = total + part[0:tok_rows].astype(jnp.float32)
    total = total.astype(jnp.bfloat16)
    key_grad[...] = total[:, 0:kv_width]
    value_grad[...] = total[:, kv_width:]
    sums = []
    for rows in (router[...], t1[tok_rows:], t2[tok_rows:], t3[tok_rows:]):
        rows = rows.astype(jnp.float32)
        count = rows.shape[0] // 2
        sums.append(rows[0:count] + rows[count:])
    total = (sums[0] + sums[1]) + (sums[2] + sums[3])
    width = total.shape[1]
    for piece in range(total.shape[0] // EXPERTS_ROW):
        router_grad[:, piece * width : (piece + 1) * width] = total[
            piece * EXPERTS_ROW : (piece + 1) * EXPERTS_ROW
        ]


EXPERTS_ROW = 4
ROW_TILE = 16


def call(kernel, meta, args, outs):
    shapes = [jax.ShapeDtypeStruct(s, t) for s, t in outs]
    return pl.pallas_call(
        kernel,
        out_shape=shapes,
        in_specs=[pl.BlockSpec(memory_space=pltpu.SMEM)]
        + [pl.BlockSpec(memory_space=pltpu.VMEM)] * len(args),
        out_specs=[pl.BlockSpec(memory_space=pltpu.VMEM)] * len(shapes),
        compiler_params=params(),
    )(meta, *args)


def local_fast(
    query_in, key_in, value_in, resid_in, out_grad, o_weight, router_weight, route_ids, expert_out
):
    query = query_in[0]
    resid = resid_in[0]
    grad = out_grad[0]
    route = route_ids[0]
    saved = expert_out[0]
    tok_rows, feats = resid.shape
    capacity, width = saved.shape
    seq_n, expert_n, dp_n = lax.axis_size("seq"), lax.axis_size("expert"), lax.axis_size("dp")
    core = lax.axis_index("dp")
    meta = jnp.stack([core, lax.axis_index("seq"), lax.axis_index("expert")]).astype(jnp.int32)
    f32, bf16 = jnp.float32, jnp.bfloat16

    def over_expert(array):
        return [array] + [partner(array, "expert", expert_n, k) for k in range(1, expert_n)]

    def over_seq(array):
        return [partner(array, "seq", seq_n, k) for k in range(1, seq_n)]

    def over_both(array, step):
        pairs = [
            (c * seq_n + i, c * seq_n + (i ^ step(c))) for c in range(dp_n) for i in range(seq_n)
        ]
        return lax.ppermute(array, ("dp", "seq"), pairs)

    half_rows = o_weight.shape[0] // dp_n
    router_rows = jnp.pad(router_weight.T, ((0, ROW_TILE - EXPERTS_ROW), (0, 0)))
    grads = over_expert(grad)
    resids = over_expert(jnp.concatenate([resid, router_rows], axis=0))
    pair = jnp.concatenate([key_in[0], value_in[0]], axis=1)
    weight_near = over_both(o_weight, lambda c: 1 + c)
    router_pad = jnp.pad(router_weight, ((0, 0), (0, LANES - router_weight.shape[1])))
    rows, place, saved_tok = call(
        prepare_kernel,
        meta,
        (route, router_pad, resid, saved),
        (
            ((8, tok_rows), f32),
            ((tok_rows, capacity), bf16),
            ((tok_rows, width), bf16),
        ),
    )
    grads[1:], resids[1], weight_near, rows, place, saved_tok, pair = lax.optimization_barrier(
        (grads[1:], resids[1], weight_near, rows, place, saved_tok, pair)
    )
    (terms,) = call(
        gate_grad_kernel, meta, (route, rows, saved_tok, *grads), (((8, tok_rows), f32),)
    )
    pairs = [pair] + over_seq(pair)
    weight_far = partner(weight_near, "dp", dp_n, 1)
    across = lax.dynamic_slice_in_dim(weight_near, core * half_rows, half_rows, axis=0)
    across_mine = over_both(across, lambda c: 2 - c)

    kv_width = key_in.shape[2]
    kv_count = kv_width // HEAD_DIM
    group = query.shape[1] // kv_width
    probs, attn_out = call(
        forward_kernel,
        meta,
        (query, *pairs),
        (
            ((kv_count, group * tok_rows, seq_n * tok_rows), f32),
            (query.shape, f32),
        ),
    )
    terms, across_mine, weight_far, resids[2:], probs, attn_out = lax.optimization_barrier(
        (terms, across_mine, weight_far, resids[2:], probs, attn_out)
    )
    across_other = partner(across_mine, "dp", dp_n, 1)
    total_tokens = dp_n * seq_n * tok_rows
    columns, router_part = call(
        lambda meta, *refs: router_kernel(meta, total_tokens, *refs),
        meta,
        (route, *over_expert(terms), resid),
        (((tok_rows, LANES), f32), ((8, feats), f32)),
    )
    term_width = 2 * kv_width
    (router_term,) = call(
        router_pair_kernel,
        meta,
        (router_part, partner(router_part, "dp", dp_n, 1)),
        (((2 * EXPERTS_ROW * feats // term_width, term_width), bf16),),
    )
    steps = 4
    model_rows = o_weight.shape[0]
    blocks = [(model_rows, feats // steps)] * 3 + [(half_rows, feats // steps)] * 2
    token_parts = (*grads, *resids)
    (projected,) = pl.pallas_call(
        project_kernel,
        out_shape=[jax.ShapeDtypeStruct((2 * tok_rows + ROW_TILE, model_rows), f32)],
        grid_spec=pltpu.PrefetchScalarGridSpec(
            num_scalar_prefetch=1,
            grid=(steps,),
            in_specs=[pl.BlockSpec(b, lambda i, m: (0, i)) for b in blocks]
            + [pl.BlockSpec(memory_space=pltpu.VMEM)] * len(token_parts),
            out_specs=[whole((2 * tok_rows + ROW_TILE, model_rows))],
            scratch_shapes=[pltpu.VMEM((expert_n, 2 * tok_rows + ROW_TILE, feats), bf16)],
        ),
        compiler_params=params(),
    )(meta, o_weight, weight_near, weight_far, across_mine, across_other, *token_parts)
    term = (tok_rows + router_term.shape[0], term_width)
    query_grad, own, *key_terms = call(
        backward_kernel,
        meta,
        (columns, projected, router_term, query, probs, attn_out, *pairs),
        ((query.shape, bf16), ((tok_rows, term_width), f32), *(((term, bf16),) * 3)),
    )
    back = [partner(key_terms[k - 1], "seq", seq_n, k) for k in range(1, seq_n)]
    columns, own = lax.optimization_barrier((columns, own))
    (expert_grad,) = call(
        expert_grad_kernel, meta, (columns, place, *grads), (((capacity, width), bf16),)
    )
    key_grad, value_grad, router_grad = call(
        finish_kernel,
        meta,
        (router_term, own, *back),
        (
            ((tok_rows, kv_width), bf16),
            ((tok_rows, kv_width), bf16),
            ((EXPERTS_ROW, feats), f32),
        ),
    )
    router_grad = router_grad.T
    return (query_grad[None], key_grad[None], value_grad[None], router_grad, expert_grad[None])


def solution(mesh):
    placed = (
        P("dp", "seq", "expert"),
        P("dp", "seq", "expert"),
        P("dp", "seq", "expert"),
        P("dp", "seq", "expert"),
        P("dp", "seq", "expert"),
        P("expert", "seq"),
        P("expert", None),
        P("dp", "seq", None),
        P("dp", ("seq", "expert"), None),
    )
    four = mesh.shape["dp"] == 2 and mesh.shape["seq"] == 4 and mesh.shape["expert"] == 4
    return jax.shard_map(
        local_fast if four else local,
        mesh=mesh,
        in_specs=placed,
        out_specs=(
            P("dp", "seq", "expert"),
            P("dp", "seq", "expert"),
            P("dp", "seq", "expert"),
            P("expert", None),
            P("dp", ("seq", "expert"), None),
        ),
        check_vma=False,
    )
```

```python
import math

import jax
import jax.numpy as jnp
from jax import lax
from jax.experimental import pallas as pl
from jax.experimental.pallas import tpu as pltpu
from jax.sharding import PartitionSpec as P

HEADS = 32
KV_HEADS = 8
HEAD_DIM = 128
D = 4096


NEG_FILL = -1e30
NORM_EPS = 1e-05


def head_rows(matrix, kv_count):
    tok_rows = matrix.shape[0]
    group_size = HEADS // KV_HEADS
    split_view = matrix.reshape(tok_rows, kv_count, group_size, HEAD_DIM)
    return jnp.transpose(split_view, (1, 2, 0, 3)).reshape(
        kv_count, group_size * tok_rows, HEAD_DIM
    )


def token_cols(matrix, tok_rows):
    kv_count = matrix.shape[0]
    group_size = matrix.shape[1] // tok_rows
    split_view = matrix.reshape(kv_count, group_size, tok_rows, HEAD_DIM)
    return jnp.transpose(split_view, (2, 0, 1, 3)).reshape(
        tok_rows, kv_count * group_size * HEAD_DIM
    )


def key_blocks(key_part, value_part):
    key_count = key_part.shape[0]
    block_len = math.gcd(key_count, 512)
    kv_count = key_part.shape[1] // HEAD_DIM
    steps_count = key_count // block_len
    key_stack = key_part.reshape(steps_count, block_len, kv_count, HEAD_DIM)
    value_stack = value_part.reshape(steps_count, block_len, kv_count, HEAD_DIM)
    offsets = block_len * jnp.arange(steps_count, dtype=jnp.int32)
    return (key_stack, value_stack, offsets, block_len)


def forward_fold(query_heads, query_pos):
    score_scale = HEAD_DIM ** (-0.5)

    def forward_fold_keys(carry_in, key_piece, start_row):
        key_stack, value_stack, offsets, block_len = key_blocks(key_piece[0], key_piece[1])

        def forward_one_block(carry_state, blocks):
            run_max, run_sum, run_out = carry_state
            key_block, value_block, block_start = blocks
            scores = (
                jnp.einsum(
                    "hrd,khd->hrk", query_heads, key_block, preferred_element_type=jnp.float32
                )
                * score_scale
            )
            key_pos = block_start + jnp.arange(block_len, dtype=jnp.int32)
            allowed = (key_pos[None, :] <= query_pos[:, None])[None]
            row_top = jnp.maximum(run_max, jnp.max(jnp.where(allowed, scores, NEG_FILL), axis=-1))
            weights = jnp.exp(jnp.where(allowed, scores - row_top[..., None], NEG_FILL))
            shrink = jnp.exp(run_max - row_top)
            run_sum = run_sum * shrink + jnp.sum(weights, axis=-1)
            run_out = run_out * shrink[..., None] + jnp.einsum(
                "hrk,khd->hrd",
                weights.astype(jnp.bfloat16),
                value_block,
                preferred_element_type=jnp.float32,
            )
            return ((row_top, run_sum, run_out), None)

        result, _ = lax.scan(forward_one_block, carry_in, (key_stack, value_stack, offsets))
        return result

    return forward_fold_keys


def backward_fold(query_heads, grad_heads, log_norm, delta_row, query_pos):
    score_scale = HEAD_DIM ** (-0.5)

    def backward_fold_keys(carry_in, key_piece, start_row):
        key_stack, value_stack, offsets, block_len = key_blocks(key_piece[0], key_piece[1])

        def backward_one_block(dq_acc, blocks):
            key_block, value_block, block_start = blocks
            scores = (
                jnp.einsum(
                    "hrd,khd->hrk", query_heads, key_block, preferred_element_type=jnp.float32
                )
                * score_scale
            )
            key_pos = block_start + jnp.arange(block_len, dtype=jnp.int32)
            allowed = (key_pos[None, :] <= query_pos[:, None])[None]
            probs = jnp.exp(jnp.where(allowed, scores - log_norm[..., None], NEG_FILL))
            dprobs = jnp.einsum(
                "hrd,khd->hrk", grad_heads, value_block, preferred_element_type=jnp.float32
            )
            dscores = (probs * (dprobs - delta_row[..., None])).astype(jnp.bfloat16)
            dq_acc = (
                dq_acc
                + jnp.einsum("hrk,khd->hrd", dscores, key_block, preferred_element_type=jnp.float32)
                * score_scale
            )
            dk_block = (
                jnp.einsum("hrk,hrd->khd", dscores, query_heads, preferred_element_type=jnp.float32)
                * score_scale
            )
            dv_block = jnp.einsum(
                "hrk,hrd->khd",
                probs.astype(jnp.bfloat16),
                grad_heads,
                preferred_element_type=jnp.float32,
            )
            return (dq_acc, (dk_block, dv_block))

        dq_acc, key_terms = lax.scan(
            backward_one_block, carry_in[0], (key_stack, value_stack, offsets)
        )
        key_count = key_piece[0].shape[0]
        dk_rows = key_terms[0].reshape(key_count, -1)
        dv_rows = key_terms[1].reshape(key_count, -1)
        return (dq_acc, dk_rows, dv_rows)

    return backward_fold_keys


def local(
    query_in, key_in, value_in, resid_in, out_grad, o_weight, router_weight, route_ids, expert_out
):
    query_loc = query_in[0]
    key_loc = key_in[0]
    value_loc = value_in[0]
    resid_loc = resid_in[0]
    grad_in = out_grad[0]
    route_loc = route_ids[0]
    tok_rows = query_loc.shape[0]
    expert_count = router_weight.shape[1]
    capacity = expert_out.shape[1]
    my_expert = lax.axis_index("expert")
    resid_f32 = resid_loc.astype(jnp.float32)
    raw_part = jnp.dot(resid_loc, router_weight, preferred_element_type=jnp.float32)
    square_part = jnp.sum(resid_f32 * resid_f32, axis=1)
    raw_logits, square_sums = lax.psum((raw_part, square_part), "expert")
    inv_rms = lax.rsqrt(square_sums / D + NORM_EPS)
    logits = inv_rms[:, None] * raw_logits
    expert_iota = jnp.arange(expert_count, dtype=jnp.int32)
    first_mask = route_loc[:, 0:1] == expert_iota[None, :]
    second_mask = route_loc[:, 1:2] == expert_iota[None, :]
    choose_a = first_mask.astype(jnp.float32)
    choose_b = second_mask.astype(jnp.float32)
    logit_a = jnp.sum(logits * choose_a, axis=1)
    logit_b = jnp.sum(logits * choose_b, axis=1)
    gate_a = jax.nn.sigmoid(logit_a - logit_b)
    gate_b = jax.nn.sigmoid(logit_b - logit_a)
    gate_table = gate_a[:, None] * choose_a + gate_b[:, None] * choose_b
    member = (first_mask | second_mask).astype(jnp.int32)
    slot_index = jnp.cumsum(member, axis=0) - member
    slot_iota = jnp.arange(capacity, dtype=jnp.int32)
    dispatch_mask = (member.T[:, None, :] == 1) & (
        slot_index.T[:, None, :] == slot_iota[None, :, None]
    )
    dispatch_f32 = dispatch_mask.astype(jnp.float32)
    outgoing = jnp.einsum(
        "ect,td->ecd",
        dispatch_mask.astype(jnp.bfloat16),
        grad_in,
        preferred_element_type=jnp.float32,
    ).astype(jnp.bfloat16)
    arrived = lax.all_to_all(outgoing, "expert", split_axis=0, concat_axis=2, tiled=True)
    slot_grads = arrived[0]
    saved_rows = expert_out[0]
    dgate_mine = jnp.einsum("cd,cd->c", slot_grads, saved_rows, preferred_element_type=jnp.float32)
    onehot_mine = (expert_iota == my_expert).astype(jnp.float32)
    place_mine = jnp.sum(dispatch_f32 * onehot_mine[:, None, None], axis=0)
    gate_column = jnp.sum(gate_table * onehot_mine[None, :], axis=1)
    gate_slot = jnp.sum(place_mine * gate_column[None, :], axis=1)
    expert_grad = (gate_slot[:, None] * slot_grads.astype(jnp.float32)).astype(jnp.bfloat16)
    dgate_all = lax.all_gather(dgate_mine, "expert", axis=0, tiled=True)
    dgate_tok = jnp.einsum(
        "ect,ec->te",
        dispatch_f32,
        dgate_all.reshape(expert_count, capacity),
        precision=lax.Precision.HIGHEST,
    )
    dgate_a = jnp.sum(dgate_tok * choose_a, axis=1)
    dgate_b = jnp.sum(dgate_tok * choose_b, axis=1)
    dlogit_a = gate_a * gate_b * (dgate_a - dgate_b)
    dlogits = dlogit_a[:, None] * (choose_a - choose_b)
    back_proj = jnp.dot(
        dlogits, router_weight.astype(jnp.float32).T, precision=lax.Precision.HIGHEST
    )
    along_raw = jnp.sum(raw_logits * dlogits, axis=1)
    resid_grad = (
        grad_in.astype(jnp.float32)
        + inv_rms[:, None] * back_proj
        - (along_raw * inv_rms**3 / D)[:, None] * resid_f32
    )
    resid_grad = resid_grad.astype(jnp.bfloat16)
    token_total = lax.axis_size("dp") * lax.axis_size("seq") * tok_rows
    router_part = (
        jnp.dot(resid_f32.T, inv_rms[:, None] * dlogits, precision=lax.Precision.HIGHEST)
        / token_total
    )
    router_grad = lax.psum(router_part, ("dp", "seq"))
    resid_whole = lax.all_gather(resid_grad, "expert", axis=1, tiled=True)
    attn_grad = lax.dot_general(
        resid_whole,
        lax.all_gather(o_weight, "seq", axis=1, tiled=True),
        (((1,), (1,)), ((), ())),
        preferred_element_type=jnp.float32,
    ).astype(jnp.bfloat16)
    kv_count = key_loc.shape[1] // HEAD_DIM
    group_size = HEADS // KV_HEADS
    query_heads = head_rows(query_loc, kv_count)
    grad_heads = head_rows(attn_grad, kv_count)
    seq_base = lax.axis_index("seq") * tok_rows
    query_pos = jnp.tile(seq_base + jnp.arange(tok_rows, dtype=jnp.int32), group_size)
    head_count = group_size * tok_rows
    initial = (
        jnp.full((kv_count, head_count), NEG_FILL, jnp.float32),
        jnp.zeros((kv_count, head_count), jnp.float32),
        jnp.zeros((kv_count, head_count, HEAD_DIM), jnp.float32),
    )
    fold_forward = forward_fold(query_heads, query_pos)
    every_key, every_value = (
        lax.all_gather(key_loc, "seq", axis=0, tiled=True),
        lax.all_gather(value_loc, "seq", axis=0, tiled=True),
    )
    run_max, run_sum, run_out = fold_forward(initial, (every_key, every_value), jnp.int32(0))
    log_norm = run_max + jnp.log(run_sum)
    attn_out = run_out / run_sum[..., None]
    delta_row = jnp.sum(grad_heads.astype(jnp.float32) * attn_out, axis=-1)
    zero_dq = jnp.zeros((kv_count, head_count, HEAD_DIM), jnp.float32)
    full_len = tok_rows * lax.axis_size("seq")
    zero_terms = jnp.zeros((full_len, kv_count * HEAD_DIM), jnp.float32)
    back_init = (zero_dq, zero_terms, zero_terms)
    fold_backward = backward_fold(query_heads, grad_heads, log_norm, delta_row, query_pos)
    back_out = fold_backward(back_init, (every_key, every_value), jnp.int32(0))
    query_grad = token_cols(back_out[0], tok_rows).astype(jnp.bfloat16)
    dk_rows, dv_rows = (
        lax.psum_scatter(back_out[1], "seq", scatter_dimension=0, tiled=True),
        lax.psum_scatter(back_out[2], "seq", scatter_dimension=0, tiled=True),
    )
    key_grad = dk_rows.astype(jnp.bfloat16)
    value_grad = dv_rows.astype(jnp.bfloat16)
    return (query_grad[None], key_grad[None], value_grad[None], router_grad, expert_grad[None])


VMEM_LIMIT = 16 * 1024 * 1024
NT = (((1,), (1,)), ((), ()))
TN = (((0,), (0,)), ((), ()))
LANES = 128


def params():
    return pltpu.CompilerParams(vmem_limit_bytes=VMEM_LIMIT)


def partner(array, axis, count, distance):
    return lax.ppermute(array, axis, [(i, i ^ distance) for i in range(count)])


def iota(shape, axis):
    return lax.broadcasted_iota(jnp.int32, shape, axis)


def whole(shape):
    return pl.BlockSpec(shape, lambda *_: (0,) * len(shape))


def column(matrix, lane):
    lanes = iota(matrix.shape, 1)
    return jnp.sum(jnp.where(lanes == lane, matrix, 0.0), axis=1, keepdims=True)


def as_rows(matrix):
    return jnp.transpose(matrix)[0:8]


def as_columns(rows):
    count = rows.shape[1]
    return jnp.transpose(
        jnp.concatenate([rows, jnp.zeros((LANES - rows.shape[0], count), rows.dtype)], axis=0)
    )


def prepare_kernel(meta, route, router_pad, resid, saved, rows, place, saved_tok):
    my_expert = meta[2]
    tok_rows = resid.shape[0]
    capacity = saved.shape[0]
    member = (route[:, 0:1] == my_expert) | (route[:, 1:2] == my_expert)
    earlier = (iota((tok_rows, tok_rows), 1) < iota((tok_rows, tok_rows), 0)).astype(
        jnp.float32
    ).astype(jnp.bfloat16)
    member_wide = jnp.broadcast_to(member.astype(jnp.float32), (tok_rows, capacity))
    slot = jnp.dot(earlier, member_wide.astype(jnp.bfloat16), preferred_element_type=jnp.float32)
    slot_lane = iota((tok_rows, capacity), 1).astype(jnp.float32)
    placed = jnp.where(slot == slot_lane, member_wide, 0.0).astype(jnp.bfloat16)
    place[...] = placed
    saved_tok[...] = jnp.dot(placed, saved[...], preferred_element_type=jnp.float32).astype(
        jnp.bfloat16
    )
    resid_f32 = resid[...].astype(jnp.float32)
    raw = jnp.dot(resid[...], router_pad[...], preferred_element_type=jnp.float32)
    square = jnp.sum(resid_f32 * resid_f32, axis=1, keepdims=True)
    lanes = iota(raw.shape, 1)
    rows[...] = as_rows(jnp.where(lanes == EXPERTS_ROW, square, raw))


def spread(my_expert, refs, rows):
    for k, ref in enumerate(refs):
        yield my_expert ^ k, lambda ref=ref: ref[rows].astype(jnp.float32)


def gate_grad_kernel(meta, route, rows, saved_tok, *refs):
    blocks, terms = refs[:-1], refs[-1]
    my_expert = meta[2]
    tok_rows = route.shape[0]
    feats = blocks[0].shape[1]
    total = jnp.zeros((tok_rows, 1), jnp.float32)
    for index, grad in spread(my_expert, blocks, slice(0, tok_rows)):
        start = pl.multiple_of(index * feats, LANES)
        saved = saved_tok[:, pl.ds(start, feats)].astype(jnp.float32)
        total = total + jnp.sum(grad() * saved, axis=1, keepdims=True)
    first = (route[:, 0:1] == my_expert).astype(jnp.float32)
    second = (route[:, 1:2] == my_expert).astype(jnp.float32)
    signed = as_rows(jnp.broadcast_to((first - second) * total, (tok_rows, LANES)))
    terms[...] = jnp.where(iota(signed.shape, 0) == EXPERTS_ROW + 1, signed, rows[...])


def router_kernel(meta, total_tokens, route, t0, t1, t2, t3, resid, columns, router_part):
    my_expert = meta[2]
    experts = EXPERTS_ROW
    sums = as_columns((t0[...] + t1[...]) + (t2[...] + t3[...]))
    lanes = iota(sums.shape, 1)
    inv_rms = lax.rsqrt(column(sums, experts) / D + NORM_EPS)
    delta = column(sums, experts + 1)
    raw = jnp.where(lanes < experts, sums, 0.0)
    logits = raw * inv_rms
    first = route[:, 0:1]
    second = route[:, 1:2]
    logit_a = jnp.sum(jnp.where(lanes == first, logits, 0.0), axis=1, keepdims=True)
    logit_b = jnp.sum(jnp.where(lanes == second, logits, 0.0), axis=1, keepdims=True)
    gate_a = jax.nn.sigmoid(logit_a - logit_b)
    gate_b = jax.nn.sigmoid(logit_b - logit_a)
    gate = jnp.where(first == my_expert, gate_a, 0.0) + jnp.where(second == my_expert, gate_b, 0.0)
    dlogit_a = gate_a * gate_b * delta
    dlogits = jnp.where(lanes == first, dlogit_a, 0.0) - jnp.where(lanes == second, dlogit_a, 0.0)
    along_raw = jnp.sum(raw * dlogits, axis=1, keepdims=True)
    scaled = inv_rms * dlogits
    along = along_raw * inv_rms * inv_rms * inv_rms / D
    columns[...] = jnp.where(
        lanes < experts, scaled, jnp.where(lanes == experts, along, gate)
    )
    router_part[...] = (
        jnp.dot(
            as_rows(scaled),
            resid[...].astype(jnp.float32),
            precision=lax.Precision.HIGHEST,
            preferred_element_type=jnp.float32,
        )
        / total_tokens
    )


def expert_grad_kernel(meta, columns, place, *refs):
    blocks, expert_grad = refs[:-1], refs[-1]
    tok_rows = place.shape[0]
    feats = blocks[0].shape[1]
    gate = column(columns[...], EXPERTS_ROW + 1)
    for index, grad in spread(meta[2], blocks, slice(0, tok_rows)):
        start = pl.multiple_of(index * feats, LANES)
        value = (gate * grad()).astype(jnp.bfloat16)
        expert_grad[:, pl.ds(start, feats)] = lax.dot_general(
            place[...], value, TN, preferred_element_type=jnp.float32
        ).astype(jnp.bfloat16)


def project_kernel(meta, *refs):
    weights, grads, resids = refs[0:5], refs[5:9], refs[9:13]
    total, rows = refs[13:]
    my_core, my_seq, my_expert = meta[0], meta[1], meta[2]
    step = pl.program_id(0)
    tok_rows, feats = grads[0].shape
    width = weights[0].shape[1]
    half = weights[3].shape[0]

    @pl.when(step == 0)
    def _():
        total[...] = jnp.zeros_like(total)
        for k in range(4):
            rows[my_expert ^ k, 0:tok_rows] = grads[k][...]
            rows[my_expert ^ k, tok_rows:] = resids[k][...]

    columns = pl.ds(pl.multiple_of(step * width, LANES), width)
    for k, weight in ((0, weights[0]), (1 + my_core, weights[1]), (2 - my_core, weights[2])):
        total[...] += lax.dot_general(
            rows[my_seq ^ k, :, columns], weight[...], NT, preferred_element_type=jnp.float32
        )
    for part, weight in ((my_core, weights[3]), (1 - my_core, weights[4])):
        total[:, pl.ds(pl.multiple_of(part * half, LANES), half)] += lax.dot_general(
            rows[my_seq ^ 3, :, columns], weight[...], NT, preferred_element_type=jnp.float32
        )


def stacked(matrix, heads):
    return jnp.concatenate(
        [matrix[:, h * HEAD_DIM : (h + 1) * HEAD_DIM] for h in range(heads)], axis=0
    )


def four(pair, pair_x, pair_y):
    count = pair.shape[0]
    return pair[...], pair_x[...], pair_y[0:count], pair_y[count:]


def forward_kernel(meta, query, pair, pair_x, pair_y, probs, attn_out):
    my_seq = meta[1]
    tok_rows = query.shape[0]
    v0, v1, v2, v3 = four(pair, pair_x, pair_y)
    kv_count = v0.shape[1] // (2 * HEAD_DIM)
    group = query.shape[1] // (kv_count * HEAD_DIM)
    rows = group * tok_rows
    position = lax.rem(iota((rows, tok_rows), 0), tok_rows)
    key_at = iota((rows, tok_rows), 1)
    allowed = jnp.concatenate(
        [key_at + ((my_seq ^ k) - my_seq) * tok_rows <= position for k in range(4)], axis=1
    )
    for kv in range(kv_count):
        heads = stacked(query[:, kv * group * HEAD_DIM : (kv + 1) * group * HEAD_DIM], group)
        key_cols = slice(kv * HEAD_DIM, (kv + 1) * HEAD_DIM)
        value_cols = slice((kv_count + kv) * HEAD_DIM, (kv_count + kv + 1) * HEAD_DIM)
        keys = jnp.concatenate([v[:, key_cols] for v in (v0, v1, v2, v3)], axis=0)
        values = jnp.concatenate([v[:, value_cols] for v in (v0, v1, v2, v3)], axis=0)
        scores = lax.dot_general(heads, keys, NT, preferred_element_type=jnp.float32) * (
            HEAD_DIM ** (-0.5)
        )
        row_max = jnp.max(jnp.where(allowed, scores, NEG_FILL), axis=1, keepdims=True)
        weights = jnp.exp(jnp.where(allowed, scores - row_max, NEG_FILL))
        row_total = jnp.sum(weights, axis=1, keepdims=True)
        mixed = (
            jnp.dot(weights.astype(jnp.bfloat16), values, preferred_element_type=jnp.float32)
            / row_total
        )
        log_norm = row_max + jnp.log(row_total)
        probs[kv] = jnp.exp(jnp.where(allowed, scores - log_norm, NEG_FILL))
        for h in range(group):
            at = (kv * group + h) * HEAD_DIM
            attn_out[:, at : at + HEAD_DIM] = mixed[h * tok_rows : (h + 1) * tok_rows]


def backward_kernel(
    meta, columns, projected, router_a, router_b, query, probs, attn_out, pair, pair_x,
    pair_y, dquery, router, d0, d1, d2, d3,
):
    tok_rows = query.shape[0]
    v0, v1, v2, v3 = four(pair, pair_x, pair_y)
    kv_count = v0.shape[1] // (2 * HEAD_DIM)
    group = query.shape[1] // (kv_count * HEAD_DIM)
    wide = group * HEAD_DIM
    score_scale = HEAD_DIM ** (-0.5)
    cols = columns[...]
    weights = [column(cols, e) for e in range(EXPERTS_ROW)]
    along = column(cols, EXPERTS_ROW)
    for kv in range(kv_count):
        here = slice(kv * wide, (kv + 1) * wide)
        attn_grad = projected[0:tok_rows, here] - along * projected[tok_rows : 2 * tok_rows, here]
        for e in range(EXPERTS_ROW):
            attn_grad = attn_grad + weights[e] * projected[2 * tok_rows + e : 2 * tok_rows + e + 1, here]
        grads = stacked(attn_grad.astype(jnp.bfloat16), group)
        heads = stacked(query[:, here], group)
        mixed = stacked(attn_out[:, here], group)
        key_cols = slice(kv * HEAD_DIM, (kv + 1) * HEAD_DIM)
        value_cols = slice((kv_count + kv) * HEAD_DIM, (kv_count + kv + 1) * HEAD_DIM)
        keys = jnp.concatenate([v[:, key_cols] for v in (v0, v1, v2, v3)], axis=0)
        values = jnp.concatenate([v[:, value_cols] for v in (v0, v1, v2, v3)], axis=0)
        delta = jnp.sum(grads.astype(jnp.float32) * mixed, axis=1, keepdims=True)
        dprobs = lax.dot_general(grads, values, NT, preferred_element_type=jnp.float32)
        chances = probs[kv]
        dscores = (chances * (dprobs - delta)).astype(jnp.bfloat16)
        dheads = (
            jnp.dot(dscores, keys, preferred_element_type=jnp.float32) * score_scale
        ).astype(jnp.bfloat16)
        for h in range(group):
            at = (kv * group + h) * HEAD_DIM
            dquery[:, at : at + HEAD_DIM] = dheads[h * tok_rows : (h + 1) * tok_rows]
        dkeys = lax.dot_general(dscores, heads, TN, preferred_element_type=jnp.float32) * score_scale
        dvalues = lax.dot_general(
            chances.astype(jnp.bfloat16), grads, TN, preferred_element_type=jnp.float32
        )
        for k, out in enumerate((d0, d1, d2, d3)):
            part = slice(k * tok_rows, (k + 1) * tok_rows)
            out[0:tok_rows, key_cols] = dkeys[part].astype(out.dtype)
            out[0:tok_rows, value_cols] = dvalues[part].astype(out.dtype)
    halves = paired(router_a[...] + router_b[...], router.shape[1])
    router[...] = halves
    for out in (d1, d2, d3):
        out[tok_rows:] = halves


def paired(part, width):
    high = part.astype(jnp.bfloat16).astype(jnp.float32)
    pieces = [
        half[0:EXPERTS_ROW, at : at + width]
        for half in (high, part - high)
        for at in range(0, part.shape[1], width)
    ]
    return jnp.concatenate(pieces, axis=0).astype(jnp.bfloat16)


def finish_kernel(meta, router, own, t1, t2, t3, key_grad, value_grad, router_grad):
    tok_rows, kv_width = key_grad.shape
    total = own[...]
    for part in (t1, t2, t3):
        total = total + part[0:tok_rows].astype(jnp.float32)
    total = total.astype(jnp.bfloat16)
    key_grad[...] = total[:, 0:kv_width]
    value_grad[...] = total[:, kv_width:]
    sums = []
    for rows in (router[...], t1[tok_rows:], t2[tok_rows:], t3[tok_rows:]):
        rows = rows.astype(jnp.float32)
        count = rows.shape[0] // 2
        sums.append(rows[0:count] + rows[count:])
    total = (sums[0] + sums[1]) + (sums[2] + sums[3])
    width = total.shape[1]
    for piece in range(total.shape[0] // EXPERTS_ROW):
        router_grad[:, piece * width : (piece + 1) * width] = total[
            piece * EXPERTS_ROW : (piece + 1) * EXPERTS_ROW
        ]


EXPERTS_ROW = 4
ROW_TILE = 16


def call(kernel, meta, args, outs):
    shapes = [jax.ShapeDtypeStruct(s, t) for s, t in outs]
    return pl.pallas_call(
        kernel,
        out_shape=shapes,
        in_specs=[pl.BlockSpec(memory_space=pltpu.SMEM)]
        + [pl.BlockSpec(memory_space=pltpu.VMEM)] * len(args),
        out_specs=[pl.BlockSpec(memory_space=pltpu.VMEM)] * len(shapes),
        compiler_params=params(),
    )(meta, *args)


def local_fast(
    query_in, key_in, value_in, resid_in, out_grad, o_weight, router_weight, route_ids, expert_out
):
    query = query_in[0]
    resid = resid_in[0]
    grad = out_grad[0]
    route = route_ids[0]
    saved = expert_out[0]
    tok_rows, feats = resid.shape
    capacity, width = saved.shape
    seq_n, expert_n, dp_n = lax.axis_size("seq"), lax.axis_size("expert"), lax.axis_size("dp")
    core = lax.axis_index("dp")
    meta = jnp.stack([core, lax.axis_index("seq"), lax.axis_index("expert")]).astype(jnp.int32)
    f32, bf16 = jnp.float32, jnp.bfloat16

    def over_expert(array):
        return [array] + [partner(array, "expert", expert_n, k) for k in range(1, expert_n)]

    def over_seq(array):
        return [partner(array, "seq", seq_n, k) for k in range(1, seq_n)]

    def over_both(array, step):
        pairs = [
            (c * seq_n + i, c * seq_n + (i ^ step(c))) for c in range(dp_n) for i in range(seq_n)
        ]
        return lax.ppermute(array, ("dp", "seq"), pairs)

    half_rows = o_weight.shape[0] // dp_n
    router_rows = jnp.pad(router_weight.T, ((0, ROW_TILE - EXPERTS_ROW), (0, 0)))
    grads = over_expert(grad)
    pair = jnp.concatenate([key_in[0], value_in[0]], axis=1)
    pair_x = partner(pair, "seq", seq_n, 1)
    weight_near = over_both(o_weight, lambda c: 1 + c)
    router_pad = jnp.pad(router_weight, ((0, 0), (0, LANES - router_weight.shape[1])))
    rows, place, saved_tok = call(
        prepare_kernel,
        meta,
        (route, router_pad, resid, saved),
        (
            ((8, tok_rows), f32),
            ((tok_rows, capacity), bf16),
            ((tok_rows, width), bf16),
        ),
    )
    own_rows = jnp.concatenate([resid, router_rows], axis=0)
    grads[1:], weight_near, rows, place, saved_tok, pair_x, own_rows = lax.optimization_barrier(
        (grads[1:], weight_near, rows, place, saved_tok, pair_x, own_rows)
    )
    resids = over_expert(own_rows)
    (terms,) = call(
        gate_grad_kernel, meta, (route, rows, saved_tok, *grads), (((8, tok_rows), f32),)
    )
    pair_y = partner(jnp.concatenate([pair, pair_x], axis=0), "seq", seq_n, 2)
    pairs = (pair, pair_x, pair_y)
    across = lax.dynamic_slice_in_dim(weight_near, core * half_rows, half_rows, axis=0)
    across_mine = over_both(across, lambda c: 2 - c)

    kv_width = key_in.shape[2]
    kv_count = kv_width // HEAD_DIM
    group = query.shape[1] // kv_width
    probs, attn_out = call(
        forward_kernel,
        meta,
        (query, *pairs),
        (
            ((kv_count, group * tok_rows, seq_n * tok_rows), f32),
            (query.shape, f32),
        ),
    )
    steps = 4
    model_rows = o_weight.shape[0]
    all_rows = 2 * tok_rows + ROW_TILE
    terms, across_mine, resids[1:], probs, attn_out, weight_near = lax.optimization_barrier(
        (terms, across_mine, resids[1:], probs, attn_out, weight_near)
    )
    weight_far = partner(weight_near, "dp", dp_n, 1)
    across_other = partner(across_mine, "dp", dp_n, 1)
    weights = (o_weight, weight_near, weight_far, across_mine, across_other)
    token_parts = (*grads, *resids)
    projected = pl.pallas_call(
        project_kernel,
        out_shape=jax.ShapeDtypeStruct((all_rows, model_rows), f32),
        grid_spec=pltpu.PrefetchScalarGridSpec(
            num_scalar_prefetch=1,
            grid=(steps,),
            in_specs=[
                pl.BlockSpec((w.shape[0], feats // steps), lambda i, m: (0, i)) for w in weights
            ]
            + [pl.BlockSpec(memory_space=pltpu.VMEM)] * len(token_parts),
            out_specs=whole((all_rows, model_rows)),
            scratch_shapes=[pltpu.VMEM((expert_n, all_rows, feats), bf16)],
        ),
        compiler_params=params(),
    )(meta, *weights, *token_parts)
    all_terms = over_expert(terms)
    projected, all_terms[1:] = lax.optimization_barrier((projected, all_terms[1:]))
    total_tokens = dp_n * seq_n * tok_rows
    columns, router_part = call(
        lambda meta, *refs: router_kernel(meta, total_tokens, *refs),
        meta,
        (route, *all_terms, resid),
        (((tok_rows, LANES), f32), ((8, feats), f32)),
    )
    term_width = 2 * kv_width
    router_rows = 2 * EXPERTS_ROW * feats // term_width
    term = (tok_rows + router_rows, term_width)
    router_other = partner(router_part, "dp", dp_n, 1)
    query_grad, router_term, own, *key_terms = call(
        backward_kernel,
        meta,
        (columns, projected, router_part, router_other, query, probs, attn_out, *pairs),
        (
            (query.shape, bf16),
            ((router_rows, term_width), bf16),
            ((tok_rows, term_width), f32),
            *(((term, bf16),) * 3),
        ),
    )
    back = [partner(key_terms[k - 1], "seq", seq_n, k) for k in range(1, seq_n)]
    columns, own = lax.optimization_barrier((columns, own))
    (expert_grad,) = call(
        expert_grad_kernel, meta, (columns, place, *grads), (((capacity, width), bf16),)
    )
    key_grad, value_grad, router_grad = call(
        finish_kernel,
        meta,
        (router_term, own, *back),
        (
            ((tok_rows, kv_width), bf16),
            ((tok_rows, kv_width), bf16),
            ((EXPERTS_ROW, feats), f32),
        ),
    )
    router_grad = router_grad.T
    return (query_grad[None], key_grad[None], value_grad[None], router_grad, expert_grad[None])


def solution(mesh):
    placed = (
        P("dp", "seq", "expert"),
        P("dp", "seq", "expert"),
        P("dp", "seq", "expert"),
        P("dp", "seq", "expert"),
        P("dp", "seq", "expert"),
        P("expert", "seq"),
        P("expert", None),
        P("dp", "seq", None),
        P("dp", ("seq", "expert"), None),
    )
    four = mesh.shape["dp"] == 2 and mesh.shape["seq"] == 4 and mesh.shape["expert"] == 4
    return jax.shard_map(
        local_fast if four else local,
        mesh=mesh,
        in_specs=placed,
        out_specs=(
            P("dp", "seq", "expert"),
            P("dp", "seq", "expert"),
            P("dp", "seq", "expert"),
            P("expert", None),
            P("dp", ("seq", "expert"), None),
        ),
        check_vma=False,
    )
```

```python
import math

import jax
import jax.numpy as jnp
from jax import lax
from jax.experimental import pallas as pl
from jax.experimental.pallas import tpu as pltpu
from jax.sharding import PartitionSpec as P

HEADS = 32
KV_HEADS = 8
HEAD_DIM = 128
D = 4096


NEG_FILL = -1e30
NORM_EPS = 1e-05


def head_rows(matrix, kv_count):
    tok_rows = matrix.shape[0]
    group_size = HEADS // KV_HEADS
    split_view = matrix.reshape(tok_rows, kv_count, group_size, HEAD_DIM)
    return jnp.transpose(split_view, (1, 2, 0, 3)).reshape(
        kv_count, group_size * tok_rows, HEAD_DIM
    )


def token_cols(matrix, tok_rows):
    kv_count = matrix.shape[0]
    group_size = matrix.shape[1] // tok_rows
    split_view = matrix.reshape(kv_count, group_size, tok_rows, HEAD_DIM)
    return jnp.transpose(split_view, (2, 0, 1, 3)).reshape(
        tok_rows, kv_count * group_size * HEAD_DIM
    )


def key_blocks(key_part, value_part):
    key_count = key_part.shape[0]
    block_len = math.gcd(key_count, 512)
    kv_count = key_part.shape[1] // HEAD_DIM
    steps_count = key_count // block_len
    key_stack = key_part.reshape(steps_count, block_len, kv_count, HEAD_DIM)
    value_stack = value_part.reshape(steps_count, block_len, kv_count, HEAD_DIM)
    offsets = block_len * jnp.arange(steps_count, dtype=jnp.int32)
    return (key_stack, value_stack, offsets, block_len)


def forward_fold(query_heads, query_pos):
    score_scale = HEAD_DIM ** (-0.5)

    def forward_fold_keys(carry_in, key_piece, start_row):
        key_stack, value_stack, offsets, block_len = key_blocks(key_piece[0], key_piece[1])

        def forward_one_block(carry_state, blocks):
            run_max, run_sum, run_out = carry_state
            key_block, value_block, block_start = blocks
            scores = (
                jnp.einsum(
                    "hrd,khd->hrk", query_heads, key_block, preferred_element_type=jnp.float32
                )
                * score_scale
            )
            key_pos = block_start + jnp.arange(block_len, dtype=jnp.int32)
            allowed = (key_pos[None, :] <= query_pos[:, None])[None]
            row_top = jnp.maximum(run_max, jnp.max(jnp.where(allowed, scores, NEG_FILL), axis=-1))
            weights = jnp.exp(jnp.where(allowed, scores - row_top[..., None], NEG_FILL))
            shrink = jnp.exp(run_max - row_top)
            run_sum = run_sum * shrink + jnp.sum(weights, axis=-1)
            run_out = run_out * shrink[..., None] + jnp.einsum(
                "hrk,khd->hrd",
                weights.astype(jnp.bfloat16),
                value_block,
                preferred_element_type=jnp.float32,
            )
            return ((row_top, run_sum, run_out), None)

        result, _ = lax.scan(forward_one_block, carry_in, (key_stack, value_stack, offsets))
        return result

    return forward_fold_keys


def backward_fold(query_heads, grad_heads, log_norm, delta_row, query_pos):
    score_scale = HEAD_DIM ** (-0.5)

    def backward_fold_keys(carry_in, key_piece, start_row):
        key_stack, value_stack, offsets, block_len = key_blocks(key_piece[0], key_piece[1])

        def backward_one_block(dq_acc, blocks):
            key_block, value_block, block_start = blocks
            scores = (
                jnp.einsum(
                    "hrd,khd->hrk", query_heads, key_block, preferred_element_type=jnp.float32
                )
                * score_scale
            )
            key_pos = block_start + jnp.arange(block_len, dtype=jnp.int32)
            allowed = (key_pos[None, :] <= query_pos[:, None])[None]
            probs = jnp.exp(jnp.where(allowed, scores - log_norm[..., None], NEG_FILL))
            dprobs = jnp.einsum(
                "hrd,khd->hrk", grad_heads, value_block, preferred_element_type=jnp.float32
            )
            dscores = (probs * (dprobs - delta_row[..., None])).astype(jnp.bfloat16)
            dq_acc = (
                dq_acc
                + jnp.einsum("hrk,khd->hrd", dscores, key_block, preferred_element_type=jnp.float32)
                * score_scale
            )
            dk_block = (
                jnp.einsum("hrk,hrd->khd", dscores, query_heads, preferred_element_type=jnp.float32)
                * score_scale
            )
            dv_block = jnp.einsum(
                "hrk,hrd->khd",
                probs.astype(jnp.bfloat16),
                grad_heads,
                preferred_element_type=jnp.float32,
            )
            return (dq_acc, (dk_block, dv_block))

        dq_acc, key_terms = lax.scan(
            backward_one_block, carry_in[0], (key_stack, value_stack, offsets)
        )
        key_count = key_piece[0].shape[0]
        dk_rows = key_terms[0].reshape(key_count, -1)
        dv_rows = key_terms[1].reshape(key_count, -1)
        return (dq_acc, dk_rows, dv_rows)

    return backward_fold_keys


def local(
    query_in, key_in, value_in, resid_in, out_grad, o_weight, router_weight, route_ids, expert_out
):
    query_loc = query_in[0]
    key_loc = key_in[0]
    value_loc = value_in[0]
    resid_loc = resid_in[0]
    grad_in = out_grad[0]
    route_loc = route_ids[0]
    tok_rows = query_loc.shape[0]
    expert_count = router_weight.shape[1]
    capacity = expert_out.shape[1]
    my_expert = lax.axis_index("expert")
    resid_f32 = resid_loc.astype(jnp.float32)
    raw_part = jnp.dot(resid_loc, router_weight, preferred_element_type=jnp.float32)
    square_part = jnp.sum(resid_f32 * resid_f32, axis=1)
    raw_logits, square_sums = lax.psum((raw_part, square_part), "expert")
    inv_rms = lax.rsqrt(square_sums / D + NORM_EPS)
    logits = inv_rms[:, None] * raw_logits
    expert_iota = jnp.arange(expert_count, dtype=jnp.int32)
    first_mask = route_loc[:, 0:1] == expert_iota[None, :]
    second_mask = route_loc[:, 1:2] == expert_iota[None, :]
    choose_a = first_mask.astype(jnp.float32)
    choose_b = second_mask.astype(jnp.float32)
    logit_a = jnp.sum(logits * choose_a, axis=1)
    logit_b = jnp.sum(logits * choose_b, axis=1)
    gate_a = jax.nn.sigmoid(logit_a - logit_b)
    gate_b = jax.nn.sigmoid(logit_b - logit_a)
    gate_table = gate_a[:, None] * choose_a + gate_b[:, None] * choose_b
    member = (first_mask | second_mask).astype(jnp.int32)
    slot_index = jnp.cumsum(member, axis=0) - member
    slot_iota = jnp.arange(capacity, dtype=jnp.int32)
    dispatch_mask = (member.T[:, None, :] == 1) & (
        slot_index.T[:, None, :] == slot_iota[None, :, None]
    )
    dispatch_f32 = dispatch_mask.astype(jnp.float32)
    outgoing = jnp.einsum(
        "ect,td->ecd",
        dispatch_mask.astype(jnp.bfloat16),
        grad_in,
        preferred_element_type=jnp.float32,
    ).astype(jnp.bfloat16)
    arrived = lax.all_to_all(outgoing, "expert", split_axis=0, concat_axis=2, tiled=True)
    slot_grads = arrived[0]
    saved_rows = expert_out[0]
    dgate_mine = jnp.einsum("cd,cd->c", slot_grads, saved_rows, preferred_element_type=jnp.float32)
    onehot_mine = (expert_iota == my_expert).astype(jnp.float32)
    place_mine = jnp.sum(dispatch_f32 * onehot_mine[:, None, None], axis=0)
    gate_column = jnp.sum(gate_table * onehot_mine[None, :], axis=1)
    gate_slot = jnp.sum(place_mine * gate_column[None, :], axis=1)
    expert_grad = (gate_slot[:, None] * slot_grads.astype(jnp.float32)).astype(jnp.bfloat16)
    dgate_all = lax.all_gather(dgate_mine, "expert", axis=0, tiled=True)
    dgate_tok = jnp.einsum(
        "ect,ec->te",
        dispatch_f32,
        dgate_all.reshape(expert_count, capacity),
        precision=lax.Precision.HIGHEST,
    )
    dgate_a = jnp.sum(dgate_tok * choose_a, axis=1)
    dgate_b = jnp.sum(dgate_tok * choose_b, axis=1)
    dlogit_a = gate_a * gate_b * (dgate_a - dgate_b)
    dlogits = dlogit_a[:, None] * (choose_a - choose_b)
    back_proj = jnp.dot(
        dlogits, router_weight.astype(jnp.float32).T, precision=lax.Precision.HIGHEST
    )
    along_raw = jnp.sum(raw_logits * dlogits, axis=1)
    resid_grad = (
        grad_in.astype(jnp.float32)
        + inv_rms[:, None] * back_proj
        - (along_raw * inv_rms**3 / D)[:, None] * resid_f32
    )
    resid_grad = resid_grad.astype(jnp.bfloat16)
    token_total = lax.axis_size("dp") * lax.axis_size("seq") * tok_rows
    router_part = (
        jnp.dot(resid_f32.T, inv_rms[:, None] * dlogits, precision=lax.Precision.HIGHEST)
        / token_total
    )
    router_grad = lax.psum(router_part, ("dp", "seq"))
    resid_whole = lax.all_gather(resid_grad, "expert", axis=1, tiled=True)
    attn_grad = lax.dot_general(
        resid_whole,
        lax.all_gather(o_weight, "seq", axis=1, tiled=True),
        (((1,), (1,)), ((), ())),
        preferred_element_type=jnp.float32,
    ).astype(jnp.bfloat16)
    kv_count = key_loc.shape[1] // HEAD_DIM
    group_size = HEADS // KV_HEADS
    query_heads = head_rows(query_loc, kv_count)
    grad_heads = head_rows(attn_grad, kv_count)
    seq_base = lax.axis_index("seq") * tok_rows
    query_pos = jnp.tile(seq_base + jnp.arange(tok_rows, dtype=jnp.int32), group_size)
    head_count = group_size * tok_rows
    initial = (
        jnp.full((kv_count, head_count), NEG_FILL, jnp.float32),
        jnp.zeros((kv_count, head_count), jnp.float32),
        jnp.zeros((kv_count, head_count, HEAD_DIM), jnp.float32),
    )
    fold_forward = forward_fold(query_heads, query_pos)
    every_key, every_value = (
        lax.all_gather(key_loc, "seq", axis=0, tiled=True),
        lax.all_gather(value_loc, "seq", axis=0, tiled=True),
    )
    run_max, run_sum, run_out = fold_forward(initial, (every_key, every_value), jnp.int32(0))
    log_norm = run_max + jnp.log(run_sum)
    attn_out = run_out / run_sum[..., None]
    delta_row = jnp.sum(grad_heads.astype(jnp.float32) * attn_out, axis=-1)
    zero_dq = jnp.zeros((kv_count, head_count, HEAD_DIM), jnp.float32)
    full_len = tok_rows * lax.axis_size("seq")
    zero_terms = jnp.zeros((full_len, kv_count * HEAD_DIM), jnp.float32)
    back_init = (zero_dq, zero_terms, zero_terms)
    fold_backward = backward_fold(query_heads, grad_heads, log_norm, delta_row, query_pos)
    back_out = fold_backward(back_init, (every_key, every_value), jnp.int32(0))
    query_grad = token_cols(back_out[0], tok_rows).astype(jnp.bfloat16)
    dk_rows, dv_rows = (
        lax.psum_scatter(back_out[1], "seq", scatter_dimension=0, tiled=True),
        lax.psum_scatter(back_out[2], "seq", scatter_dimension=0, tiled=True),
    )
    key_grad = dk_rows.astype(jnp.bfloat16)
    value_grad = dv_rows.astype(jnp.bfloat16)
    return (query_grad[None], key_grad[None], value_grad[None], router_grad, expert_grad[None])


VMEM_LIMIT = 16 * 1024 * 1024
NT = (((1,), (1,)), ((), ()))
TN = (((0,), (0,)), ((), ()))
LANES = 128


def params():
    return pltpu.CompilerParams(vmem_limit_bytes=VMEM_LIMIT)


def partner(array, axis, count, distance):
    return lax.ppermute(array, axis, [(i, i ^ distance) for i in range(count)])


def iota(shape, axis):
    return lax.broadcasted_iota(jnp.int32, shape, axis)


def whole(shape):
    return pl.BlockSpec(shape, lambda *_: (0,) * len(shape))


def column(matrix, lane):
    lanes = iota(matrix.shape, 1)
    return jnp.sum(jnp.where(lanes == lane, matrix, 0.0), axis=1, keepdims=True)


def as_rows(matrix):
    return jnp.transpose(matrix)[0:8]


def as_columns(rows):
    count = rows.shape[1]
    return jnp.transpose(
        jnp.concatenate([rows, jnp.zeros((LANES - rows.shape[0], count), rows.dtype)], axis=0)
    )


def prepare_kernel(meta, route, router_pad, resid, saved, rows, place, saved_tok):
    my_expert = meta[2]
    tok_rows = resid.shape[0]
    capacity = saved.shape[0]
    member = (route[:, 0:1] == my_expert) | (route[:, 1:2] == my_expert)
    earlier = (iota((tok_rows, tok_rows), 1) < iota((tok_rows, tok_rows), 0)).astype(
        jnp.float32
    ).astype(jnp.bfloat16)
    member_wide = jnp.broadcast_to(member.astype(jnp.float32), (tok_rows, capacity))
    slot = jnp.dot(earlier, member_wide.astype(jnp.bfloat16), preferred_element_type=jnp.float32)
    slot_lane = iota((tok_rows, capacity), 1).astype(jnp.float32)
    placed = jnp.where(slot == slot_lane, member_wide, 0.0).astype(jnp.bfloat16)
    place[...] = placed
    saved_tok[...] = jnp.dot(placed, saved[...], preferred_element_type=jnp.float32).astype(
        jnp.bfloat16
    )
    resid_f32 = resid[...].astype(jnp.float32)
    raw = jnp.dot(resid[...], router_pad[...], preferred_element_type=jnp.float32)
    square = jnp.sum(resid_f32 * resid_f32, axis=1, keepdims=True)
    lanes = iota(raw.shape, 1)
    rows[...] = as_rows(jnp.where(lanes == EXPERTS_ROW, square, raw))


def spread(my_expert, refs, rows):
    for k, ref in enumerate(refs):
        yield my_expert ^ k, lambda ref=ref: ref[rows].astype(jnp.float32)


def flat(rows):
    return jnp.concatenate([rows[q : q + 1] for q in range(rows.shape[0])], axis=1)


def gate_grad_kernel(meta, route, rows, saved_tok, resid, router_rows, *refs):
    blocks, message = refs[:-1], refs[-1]
    my_expert = meta[2]
    tok_rows = route.shape[0]
    feats = blocks[0].shape[1]
    total = jnp.zeros((tok_rows, 1), jnp.float32)
    for index, grad in spread(my_expert, blocks, slice(0, tok_rows)):
        start = pl.multiple_of(index * feats, LANES)
        saved = saved_tok[:, pl.ds(start, feats)].astype(jnp.float32)
        total = total + jnp.sum(grad() * saved, axis=1, keepdims=True)
    first = (route[:, 0:1] == my_expert).astype(jnp.float32)
    second = (route[:, 1:2] == my_expert).astype(jnp.float32)
    signed = as_rows(jnp.broadcast_to((first - second) * total, (tok_rows, LANES)))
    rest = flat(jnp.where(iota(signed.shape, 0) == EXPERTS_ROW + 1, signed, rows[...]))
    tile = router_rows[...].astype(jnp.float32)
    at = iota(tile.shape, 0)
    for piece in range(3):
        part = rest.astype(jnp.bfloat16).astype(jnp.float32)
        tile = jnp.where(at == EXPERTS_ROW + piece, part, tile)
        rest = rest - part
    message[0:tok_rows] = resid[...]
    message[tok_rows:] = tile.astype(jnp.bfloat16)


def told(message):
    tok_rows = message.shape[0] - ROW_TILE
    tile = message[tok_rows:].astype(jnp.float32)
    one, two, three = (tile[EXPERTS_ROW + p : EXPERTS_ROW + p + 1] for p in range(3))
    line = (one + two) + three
    return jnp.concatenate(
        [line[:, at : at + tok_rows] for at in range(0, 8 * tok_rows, tok_rows)], axis=0
    )


def router_kernel(meta, total_tokens, route, m0, m1, m2, m3, columns, router_part):
    my_expert = meta[2]
    experts = EXPERTS_ROW
    sums = as_columns((told(m0) + told(m1)) + (told(m2) + told(m3)))
    resid = m0[0 : route.shape[0]]
    lanes = iota(sums.shape, 1)
    inv_rms = lax.rsqrt(column(sums, experts) / D + NORM_EPS)
    delta = column(sums, experts + 1)
    raw = jnp.where(lanes < experts, sums, 0.0)
    logits = raw * inv_rms
    first = route[:, 0:1]
    second = route[:, 1:2]
    logit_a = jnp.sum(jnp.where(lanes == first, logits, 0.0), axis=1, keepdims=True)
    logit_b = jnp.sum(jnp.where(lanes == second, logits, 0.0), axis=1, keepdims=True)
    gate_a = jax.nn.sigmoid(logit_a - logit_b)
    gate_b = jax.nn.sigmoid(logit_b - logit_a)
    gate = jnp.where(first == my_expert, gate_a, 0.0) + jnp.where(second == my_expert, gate_b, 0.0)
    dlogit_a = gate_a * gate_b * delta
    dlogits = jnp.where(lanes == first, dlogit_a, 0.0) - jnp.where(lanes == second, dlogit_a, 0.0)
    along_raw = jnp.sum(raw * dlogits, axis=1, keepdims=True)
    scaled = inv_rms * dlogits
    along = along_raw * inv_rms * inv_rms * inv_rms / D
    columns[...] = jnp.where(
        lanes < experts, scaled, jnp.where(lanes == experts, along, gate)
    )
    router_part[...] = (
        jnp.dot(
            as_rows(scaled),
            resid.astype(jnp.float32),
            precision=lax.Precision.HIGHEST,
            preferred_element_type=jnp.float32,
        )
        / total_tokens
    )


def expert_grad_kernel(meta, columns, place, *refs):
    blocks, expert_grad = refs[:-1], refs[-1]
    tok_rows = place.shape[0]
    feats = blocks[0].shape[1]
    gate = column(columns[...], EXPERTS_ROW + 1)
    for index, grad in spread(meta[2], blocks, slice(0, tok_rows)):
        start = pl.multiple_of(index * feats, LANES)
        value = (gate * grad()).astype(jnp.bfloat16)
        expert_grad[:, pl.ds(start, feats)] = lax.dot_general(
            place[...], value, TN, preferred_element_type=jnp.float32
        ).astype(jnp.bfloat16)


def times(rows, weight):
    return lax.dot_general(rows, weight, NT, preferred_element_type=jnp.float32)


def half_of(part, half):
    return pl.ds(pl.multiple_of(part * half, LANES), half)


def project_kernel(meta, own, near, across, *refs):
    grads, resids, total, rows = refs[0:4], refs[4:8], refs[8], refs[9]
    my_core, my_seq, my_expert = meta[0], meta[1], meta[2]
    step = pl.program_id(0)
    tok_rows = grads[0].shape[0]
    width = own.shape[1]

    @pl.when(step == 0)
    def _():
        total[...] = jnp.zeros_like(total)
        for k in range(4):
            rows[my_expert ^ k, 0:tok_rows] = grads[k][...]
            rows[my_expert ^ k, tok_rows:] = resids[k][...]

    columns = pl.ds(pl.multiple_of(step * width, LANES), width)
    total[...] += times(rows[my_seq, :, columns], own[...]) + times(
        rows[my_seq ^ (1 + my_core), :, columns], near[...]
    )
    here = half_of(my_core, across.shape[0])
    total[:, here] += times(rows[my_seq ^ 3, :, columns], across[...])


def project_rest_kernel(meta, far, across, rows, most, total):
    my_core, my_seq = meta[0], meta[1]
    step = pl.program_id(0)
    width = far.shape[1]

    @pl.when(step == 0)
    def _():
        total[...] = most[...]

    columns = pl.ds(pl.multiple_of(step * width, LANES), width)
    total[...] += times(rows[my_seq ^ (2 - my_core), :, columns], far[...])
    here = half_of(1 - my_core, across.shape[0])
    total[:, here] += times(rows[my_seq ^ 3, :, columns], across[...])


def stacked(matrix, heads):
    return jnp.concatenate(
        [matrix[:, h * HEAD_DIM : (h + 1) * HEAD_DIM] for h in range(heads)], axis=0
    )


def distances(core):
    return 0, 2 - core, 1 + core, 3


def four(pair, pair_x, pair_y):
    count = pair.shape[0]
    return pair[...], pair_x[...], pair_y[0:count], pair_y[count:]


def forward_kernel(meta, query, pair, pair_x, pair_y, probs, attn_out):
    my_seq = meta[1]
    tok_rows = query.shape[0]
    v0, v1, v2, v3 = four(pair, pair_x, pair_y)
    kv_count = v0.shape[1] // (2 * HEAD_DIM)
    group = query.shape[1] // (kv_count * HEAD_DIM)
    rows = group * tok_rows
    position = lax.rem(iota((rows, tok_rows), 0), tok_rows)
    key_at = iota((rows, tok_rows), 1)
    allowed = jnp.concatenate(
        [
            key_at + ((my_seq ^ k) - my_seq) * tok_rows <= position
            for k in distances(meta[0])
        ],
        axis=1,
    )
    for kv in range(kv_count):
        heads = stacked(query[:, kv * group * HEAD_DIM : (kv + 1) * group * HEAD_DIM], group)
        key_cols = slice(kv * HEAD_DIM, (kv + 1) * HEAD_DIM)
        value_cols = slice((kv_count + kv) * HEAD_DIM, (kv_count + kv + 1) * HEAD_DIM)
        keys = jnp.concatenate([v[:, key_cols] for v in (v0, v1, v2, v3)], axis=0)
        values = jnp.concatenate([v[:, value_cols] for v in (v0, v1, v2, v3)], axis=0)
        scores = lax.dot_general(heads, keys, NT, preferred_element_type=jnp.float32) * (
            HEAD_DIM ** (-0.5)
        )
        row_max = jnp.max(jnp.where(allowed, scores, NEG_FILL), axis=1, keepdims=True)
        weights = jnp.exp(jnp.where(allowed, scores - row_max, NEG_FILL))
        row_total = jnp.sum(weights, axis=1, keepdims=True)
        mixed = (
            jnp.dot(weights.astype(jnp.bfloat16), values, preferred_element_type=jnp.float32)
            / row_total
        )
        log_norm = row_max + jnp.log(row_total)
        probs[kv] = jnp.exp(jnp.where(allowed, scores - log_norm, NEG_FILL))
        for h in range(group):
            at = (kv * group + h) * HEAD_DIM
            attn_out[:, at : at + HEAD_DIM] = mixed[h * tok_rows : (h + 1) * tok_rows]


def backward_kernel(
    meta, columns, projected, router_a, router_b, query, probs, attn_out, pair, pair_x,
    pair_y, dquery, router, d0, d1, d2, d3,
):
    tok_rows = query.shape[0]
    v0, v1, v2, v3 = four(pair, pair_x, pair_y)
    kv_count = v0.shape[1] // (2 * HEAD_DIM)
    group = query.shape[1] // (kv_count * HEAD_DIM)
    wide = group * HEAD_DIM
    score_scale = HEAD_DIM ** (-0.5)
    cols = columns[...]
    weights = [column(cols, e) for e in range(EXPERTS_ROW)]
    along = column(cols, EXPERTS_ROW)
    for kv in range(kv_count):
        here = slice(kv * wide, (kv + 1) * wide)
        attn_grad = projected[0:tok_rows, here] - along * projected[tok_rows : 2 * tok_rows, here]
        for e in range(EXPERTS_ROW):
            attn_grad = attn_grad + weights[e] * projected[2 * tok_rows + e : 2 * tok_rows + e + 1, here]
        grads = stacked(attn_grad.astype(jnp.bfloat16), group)
        heads = stacked(query[:, here], group)
        mixed = stacked(attn_out[:, here], group)
        key_cols = slice(kv * HEAD_DIM, (kv + 1) * HEAD_DIM)
        value_cols = slice((kv_count + kv) * HEAD_DIM, (kv_count + kv + 1) * HEAD_DIM)
        keys = jnp.concatenate([v[:, key_cols] for v in (v0, v1, v2, v3)], axis=0)
        values = jnp.concatenate([v[:, value_cols] for v in (v0, v1, v2, v3)], axis=0)
        delta = jnp.sum(grads.astype(jnp.float32) * mixed, axis=1, keepdims=True)
        dprobs = lax.dot_general(grads, values, NT, preferred_element_type=jnp.float32)
        chances = probs[kv]
        dscores = (chances * (dprobs - delta)).astype(jnp.bfloat16)
        dheads = (
            jnp.dot(dscores, keys, preferred_element_type=jnp.float32) * score_scale
        ).astype(jnp.bfloat16)
        for h in range(group):
            at = (kv * group + h) * HEAD_DIM
            dquery[:, at : at + HEAD_DIM] = dheads[h * tok_rows : (h + 1) * tok_rows]
        dkeys = lax.dot_general(dscores, heads, TN, preferred_element_type=jnp.float32) * score_scale
        dvalues = lax.dot_general(
            chances.astype(jnp.bfloat16), grads, TN, preferred_element_type=jnp.float32
        )
        for k, out in enumerate((d0, d1, d2, d3)):
            part = slice(k * tok_rows, (k + 1) * tok_rows)
            out[0:tok_rows, key_cols] = dkeys[part].astype(out.dtype)
            out[0:tok_rows, value_cols] = dvalues[part].astype(out.dtype)
    halves = paired(router_a[...] + router_b[...], router.shape[1])
    router[...] = halves
    for out in (d1, d2, d3):
        out[tok_rows:] = halves


def paired(part, width):
    high = part.astype(jnp.bfloat16).astype(jnp.float32)
    pieces = [
        half[0:EXPERTS_ROW, at : at + width]
        for half in (high, part - high)
        for at in range(0, part.shape[1], width)
    ]
    return jnp.concatenate(pieces, axis=0).astype(jnp.bfloat16)


def finish_kernel(meta, router, own, t1, t2, t3, key_grad, value_grad, router_grad):
    tok_rows, kv_width = key_grad.shape
    total = own[...]
    for part in (t1, t2, t3):
        total = total + part[0:tok_rows].astype(jnp.float32)
    total = total.astype(jnp.bfloat16)
    key_grad[...] = total[:, 0:kv_width]
    value_grad[...] = total[:, kv_width:]
    sums = []
    for rows in (router[...], t1[tok_rows:], t2[tok_rows:], t3[tok_rows:]):
        rows = rows.astype(jnp.float32)
        count = rows.shape[0] // 2
        sums.append(rows[0:count] + rows[count:])
    first = meta[0] == 0
    one, two = jnp.where(first, sums[2], sums[1]), jnp.where(first, sums[1], sums[2])
    total = (sums[0] + one) + (two + sums[3])
    width = total.shape[1]
    for piece in range(total.shape[0] // EXPERTS_ROW):
        router_grad[:, piece * width : (piece + 1) * width] = total[
            piece * EXPERTS_ROW : (piece + 1) * EXPERTS_ROW
        ]


EXPERTS_ROW = 4
ROW_TILE = 16


def call(kernel, meta, args, outs):
    shapes = [jax.ShapeDtypeStruct(s, t) for s, t in outs]
    return pl.pallas_call(
        kernel,
        out_shape=shapes,
        in_specs=[pl.BlockSpec(memory_space=pltpu.SMEM)]
        + [pl.BlockSpec(memory_space=pltpu.VMEM)] * len(args),
        out_specs=[pl.BlockSpec(memory_space=pltpu.VMEM)] * len(shapes),
        compiler_params=params(),
    )(meta, *args)


def local_fast(
    query_in, key_in, value_in, resid_in, out_grad, o_weight, router_weight, route_ids, expert_out
):
    query = query_in[0]
    resid = resid_in[0]
    grad = out_grad[0]
    route = route_ids[0]
    saved = expert_out[0]
    tok_rows, feats = resid.shape
    capacity, width = saved.shape
    seq_n, expert_n, dp_n = lax.axis_size("seq"), lax.axis_size("expert"), lax.axis_size("dp")
    core = lax.axis_index("dp")
    meta = jnp.stack([core, lax.axis_index("seq"), lax.axis_index("expert")]).astype(jnp.int32)
    f32, bf16 = jnp.float32, jnp.bfloat16

    def over_expert(array):
        return [array] + [partner(array, "expert", expert_n, k) for k in range(1, expert_n)]

    def over_seq(array):
        return [partner(array, "seq", seq_n, k) for k in range(1, seq_n)]

    def over_both(array, step):
        pairs = [
            (c * seq_n + i, c * seq_n + (i ^ step(c))) for c in range(dp_n) for i in range(seq_n)
        ]
        return lax.ppermute(array, ("dp", "seq"), pairs)

    half_rows = o_weight.shape[0] // dp_n
    router_rows = jnp.pad(router_weight.T, ((0, ROW_TILE - EXPERTS_ROW), (0, 0)))
    grads = over_expert(grad)
    pair = jnp.concatenate([key_in[0], value_in[0]], axis=1)
    pair_x = over_both(pair, lambda c: distances(c)[1])
    weight_near = over_both(o_weight, lambda c: 1 + c)
    router_pad = jnp.pad(router_weight, ((0, 0), (0, LANES - router_weight.shape[1])))
    rows, place, saved_tok = call(
        prepare_kernel,
        meta,
        (route, router_pad, resid, saved),
        (
            ((8, tok_rows), f32),
            ((tok_rows, capacity), bf16),
            ((tok_rows, width), bf16),
        ),
    )
    grads[1:], weight_near, rows, place, saved_tok, pair_x = lax.optimization_barrier(
        (grads[1:], weight_near, rows, place, saved_tok, pair_x)
    )
    (own_rows,) = call(
        gate_grad_kernel,
        meta,
        (route, rows, saved_tok, resid, router_rows, *grads),
        (((tok_rows + ROW_TILE, feats), bf16),),
    )
    resids = over_expert(own_rows)
    pair_y = over_both(jnp.concatenate([pair, pair_x], axis=0), lambda c: distances(c)[2])
    pairs = (pair, pair_x, pair_y)
    across = lax.dynamic_slice_in_dim(weight_near, core * half_rows, half_rows, axis=0)
    across_mine = over_both(across, lambda c: 2 - c)

    kv_width = key_in.shape[2]
    kv_count = kv_width // HEAD_DIM
    group = query.shape[1] // kv_width
    probs, attn_out = call(
        forward_kernel,
        meta,
        (query, *pairs),
        (
            ((kv_count, group * tok_rows, seq_n * tok_rows), f32),
            (query.shape, f32),
        ),
    )
    steps = 4
    model_rows = o_weight.shape[0]
    all_rows = 2 * tok_rows + ROW_TILE
    across_mine, resids[1:], probs, attn_out, weight_near = lax.optimization_barrier(
        (across_mine, resids[1:], probs, attn_out, weight_near)
    )
    weight_far = partner(weight_near, "dp", dp_n, 1)
    across_other = partner(across_mine, "dp", dp_n, 1)
    all_shape = (all_rows, model_rows)
    rows_shape = (expert_n, all_rows, feats)

    def project(kernel, weights, in_place, shapes):
        return pl.pallas_call(
            kernel,
            out_shape=shapes,
            grid_spec=pltpu.PrefetchScalarGridSpec(
                num_scalar_prefetch=1,
                grid=(steps,),
                in_specs=[
                    pl.BlockSpec((w.shape[0], feats // steps), lambda i, m: (0, i)) for w in weights
                ]
                + [pl.BlockSpec(memory_space=pltpu.VMEM)] * len(in_place),
                out_specs=[whole(s.shape) for s in shapes],
            ),
            compiler_params=params(),
        )(meta, *weights, *in_place)

    most, staged = project(
        project_kernel,
        (o_weight, weight_near, across_mine),
        (*grads, *resids),
        [jax.ShapeDtypeStruct(all_shape, f32), jax.ShapeDtypeStruct(rows_shape, bf16)],
    )
    (projected,) = project(
        project_rest_kernel,
        (weight_far, across_other),
        (staged, most),
        [jax.ShapeDtypeStruct(all_shape, f32)],
    )
    total_tokens = dp_n * seq_n * tok_rows
    columns, router_part = call(
        lambda meta, *refs: router_kernel(meta, total_tokens, *refs),
        meta,
        (route, *resids),
        (((tok_rows, LANES), f32), ((8, feats), f32)),
    )
    term_width = 2 * kv_width
    router_rows = 2 * EXPERTS_ROW * feats // term_width
    term = (tok_rows + router_rows, term_width)
    router_other = partner(router_part, "dp", dp_n, 1)
    query_grad, router_term, own, *key_terms = call(
        backward_kernel,
        meta,
        (columns, projected, router_part, router_other, query, probs, attn_out, *pairs),
        (
            (query.shape, bf16),
            ((router_rows, term_width), bf16),
            ((tok_rows, term_width), f32),
            *(((term, bf16),) * 3),
        ),
    )
    back = [
        over_both(term, lambda c: distances(c)[at]) for at, term in enumerate(key_terms, start=1)
    ]
    columns, own = lax.optimization_barrier((columns, own))
    (expert_grad,) = call(
        expert_grad_kernel, meta, (columns, place, *grads), (((capacity, width), bf16),)
    )
    key_grad, value_grad, router_grad = call(
        finish_kernel,
        meta,
        (router_term, own, *back),
        (
            ((tok_rows, kv_width), bf16),
            ((tok_rows, kv_width), bf16),
            ((EXPERTS_ROW, feats), f32),
        ),
    )
    router_grad = router_grad.T
    return (query_grad[None], key_grad[None], value_grad[None], router_grad, expert_grad[None])


def solution(mesh):
    placed = (
        P("dp", "seq", "expert"),
        P("dp", "seq", "expert"),
        P("dp", "seq", "expert"),
        P("dp", "seq", "expert"),
        P("dp", "seq", "expert"),
        P("expert", "seq"),
        P("expert", None),
        P("dp", "seq", None),
        P("dp", ("seq", "expert"), None),
    )
    four = mesh.shape["dp"] == 2 and mesh.shape["seq"] == 4 and mesh.shape["expert"] == 4
    return jax.shard_map(
        local_fast if four else local,
        mesh=mesh,
        in_specs=placed,
        out_specs=(
            P("dp", "seq", "expert"),
            P("dp", "seq", "expert"),
            P("dp", "seq", "expert"),
            P("expert", None),
            P("dp", ("seq", "expert"), None),
        ),
        check_vma=False,
    )
```

```python
import math

import jax
import jax.numpy as jnp
from jax import lax
from jax.experimental import pallas as pl
from jax.experimental.pallas import tpu as pltpu
from jax.sharding import PartitionSpec as P

HEADS = 32
KV_HEADS = 8
HEAD_DIM = 128
D = 4096


NEG_FILL = -1e30
NORM_EPS = 1e-05


def head_rows(matrix, kv_count):
    tok_rows = matrix.shape[0]
    group_size = HEADS // KV_HEADS
    split_view = matrix.reshape(tok_rows, kv_count, group_size, HEAD_DIM)
    return jnp.transpose(split_view, (1, 2, 0, 3)).reshape(
        kv_count, group_size * tok_rows, HEAD_DIM
    )


def token_cols(matrix, tok_rows):
    kv_count = matrix.shape[0]
    group_size = matrix.shape[1] // tok_rows
    split_view = matrix.reshape(kv_count, group_size, tok_rows, HEAD_DIM)
    return jnp.transpose(split_view, (2, 0, 1, 3)).reshape(
        tok_rows, kv_count * group_size * HEAD_DIM
    )


def key_blocks(key_part, value_part):
    key_count = key_part.shape[0]
    block_len = math.gcd(key_count, 512)
    kv_count = key_part.shape[1] // HEAD_DIM
    steps_count = key_count // block_len
    key_stack = key_part.reshape(steps_count, block_len, kv_count, HEAD_DIM)
    value_stack = value_part.reshape(steps_count, block_len, kv_count, HEAD_DIM)
    offsets = block_len * jnp.arange(steps_count, dtype=jnp.int32)
    return (key_stack, value_stack, offsets, block_len)


def forward_fold(query_heads, query_pos):
    score_scale = HEAD_DIM ** (-0.5)

    def forward_fold_keys(carry_in, key_piece, start_row):
        key_stack, value_stack, offsets, block_len = key_blocks(key_piece[0], key_piece[1])

        def forward_one_block(carry_state, blocks):
            run_max, run_sum, run_out = carry_state
            key_block, value_block, block_start = blocks
            scores = (
                jnp.einsum(
                    "hrd,khd->hrk", query_heads, key_block, preferred_element_type=jnp.float32
                )
                * score_scale
            )
            key_pos = block_start + jnp.arange(block_len, dtype=jnp.int32)
            allowed = (key_pos[None, :] <= query_pos[:, None])[None]
            row_top = jnp.maximum(run_max, jnp.max(jnp.where(allowed, scores, NEG_FILL), axis=-1))
            weights = jnp.exp(jnp.where(allowed, scores - row_top[..., None], NEG_FILL))
            shrink = jnp.exp(run_max - row_top)
            run_sum = run_sum * shrink + jnp.sum(weights, axis=-1)
            run_out = run_out * shrink[..., None] + jnp.einsum(
                "hrk,khd->hrd",
                weights.astype(jnp.bfloat16),
                value_block,
                preferred_element_type=jnp.float32,
            )
            return ((row_top, run_sum, run_out), None)

        result, _ = lax.scan(forward_one_block, carry_in, (key_stack, value_stack, offsets))
        return result

    return forward_fold_keys


def backward_fold(query_heads, grad_heads, log_norm, delta_row, query_pos):
    score_scale = HEAD_DIM ** (-0.5)

    def backward_fold_keys(carry_in, key_piece, start_row):
        key_stack, value_stack, offsets, block_len = key_blocks(key_piece[0], key_piece[1])

        def backward_one_block(dq_acc, blocks):
            key_block, value_block, block_start = blocks
            scores = (
                jnp.einsum(
                    "hrd,khd->hrk", query_heads, key_block, preferred_element_type=jnp.float32
                )
                * score_scale
            )
            key_pos = block_start + jnp.arange(block_len, dtype=jnp.int32)
            allowed = (key_pos[None, :] <= query_pos[:, None])[None]
            probs = jnp.exp(jnp.where(allowed, scores - log_norm[..., None], NEG_FILL))
            dprobs = jnp.einsum(
                "hrd,khd->hrk", grad_heads, value_block, preferred_element_type=jnp.float32
            )
            dscores = (probs * (dprobs - delta_row[..., None])).astype(jnp.bfloat16)
            dq_acc = (
                dq_acc
                + jnp.einsum("hrk,khd->hrd", dscores, key_block, preferred_element_type=jnp.float32)
                * score_scale
            )
            dk_block = (
                jnp.einsum("hrk,hrd->khd", dscores, query_heads, preferred_element_type=jnp.float32)
                * score_scale
            )
            dv_block = jnp.einsum(
                "hrk,hrd->khd",
                probs.astype(jnp.bfloat16),
                grad_heads,
                preferred_element_type=jnp.float32,
            )
            return (dq_acc, (dk_block, dv_block))

        dq_acc, key_terms = lax.scan(
            backward_one_block, carry_in[0], (key_stack, value_stack, offsets)
        )
        key_count = key_piece[0].shape[0]
        dk_rows = key_terms[0].reshape(key_count, -1)
        dv_rows = key_terms[1].reshape(key_count, -1)
        return (dq_acc, dk_rows, dv_rows)

    return backward_fold_keys


def local(
    query_in, key_in, value_in, resid_in, out_grad, o_weight, router_weight, route_ids, expert_out
):
    query_loc = query_in[0]
    key_loc = key_in[0]
    value_loc = value_in[0]
    resid_loc = resid_in[0]
    grad_in = out_grad[0]
    route_loc = route_ids[0]
    tok_rows = query_loc.shape[0]
    expert_count = router_weight.shape[1]
    capacity = expert_out.shape[1]
    my_expert = lax.axis_index("expert")
    resid_f32 = resid_loc.astype(jnp.float32)
    raw_part = jnp.dot(resid_loc, router_weight, preferred_element_type=jnp.float32)
    square_part = jnp.sum(resid_f32 * resid_f32, axis=1)
    raw_logits, square_sums = lax.psum((raw_part, square_part), "expert")
    inv_rms = lax.rsqrt(square_sums / D + NORM_EPS)
    logits = inv_rms[:, None] * raw_logits
    expert_iota = jnp.arange(expert_count, dtype=jnp.int32)
    first_mask = route_loc[:, 0:1] == expert_iota[None, :]
    second_mask = route_loc[:, 1:2] == expert_iota[None, :]
    choose_a = first_mask.astype(jnp.float32)
    choose_b = second_mask.astype(jnp.float32)
    logit_a = jnp.sum(logits * choose_a, axis=1)
    logit_b = jnp.sum(logits * choose_b, axis=1)
    gate_a = jax.nn.sigmoid(logit_a - logit_b)
    gate_b = jax.nn.sigmoid(logit_b - logit_a)
    gate_table = gate_a[:, None] * choose_a + gate_b[:, None] * choose_b
    member = (first_mask | second_mask).astype(jnp.int32)
    slot_index = jnp.cumsum(member, axis=0) - member
    slot_iota = jnp.arange(capacity, dtype=jnp.int32)
    dispatch_mask = (member.T[:, None, :] == 1) & (
        slot_index.T[:, None, :] == slot_iota[None, :, None]
    )
    dispatch_f32 = dispatch_mask.astype(jnp.float32)
    outgoing = jnp.einsum(
        "ect,td->ecd",
        dispatch_mask.astype(jnp.bfloat16),
        grad_in,
        preferred_element_type=jnp.float32,
    ).astype(jnp.bfloat16)
    arrived = lax.all_to_all(outgoing, "expert", split_axis=0, concat_axis=2, tiled=True)
    slot_grads = arrived[0]
    saved_rows = expert_out[0]
    dgate_mine = jnp.einsum("cd,cd->c", slot_grads, saved_rows, preferred_element_type=jnp.float32)
    onehot_mine = (expert_iota == my_expert).astype(jnp.float32)
    place_mine = jnp.sum(dispatch_f32 * onehot_mine[:, None, None], axis=0)
    gate_column = jnp.sum(gate_table * onehot_mine[None, :], axis=1)
    gate_slot = jnp.sum(place_mine * gate_column[None, :], axis=1)
    expert_grad = (gate_slot[:, None] * slot_grads.astype(jnp.float32)).astype(jnp.bfloat16)
    dgate_all = lax.all_gather(dgate_mine, "expert", axis=0, tiled=True)
    dgate_tok = jnp.einsum(
        "ect,ec->te",
        dispatch_f32,
        dgate_all.reshape(expert_count, capacity),
        precision=lax.Precision.HIGHEST,
    )
    dgate_a = jnp.sum(dgate_tok * choose_a, axis=1)
    dgate_b = jnp.sum(dgate_tok * choose_b, axis=1)
    dlogit_a = gate_a * gate_b * (dgate_a - dgate_b)
    dlogits = dlogit_a[:, None] * (choose_a - choose_b)
    back_proj = jnp.dot(
        dlogits, router_weight.astype(jnp.float32).T, precision=lax.Precision.HIGHEST
    )
    along_raw = jnp.sum(raw_logits * dlogits, axis=1)
    resid_grad = (
        grad_in.astype(jnp.float32)
        + inv_rms[:, None] * back_proj
        - (along_raw * inv_rms**3 / D)[:, None] * resid_f32
    )
    resid_grad = resid_grad.astype(jnp.bfloat16)
    token_total = lax.axis_size("dp") * lax.axis_size("seq") * tok_rows
    router_part = (
        jnp.dot(resid_f32.T, inv_rms[:, None] * dlogits, precision=lax.Precision.HIGHEST)
        / token_total
    )
    router_grad = lax.psum(router_part, ("dp", "seq"))
    resid_whole = lax.all_gather(resid_grad, "expert", axis=1, tiled=True)
    attn_grad = lax.dot_general(
        resid_whole,
        lax.all_gather(o_weight, "seq", axis=1, tiled=True),
        (((1,), (1,)), ((), ())),
        preferred_element_type=jnp.float32,
    ).astype(jnp.bfloat16)
    kv_count = key_loc.shape[1] // HEAD_DIM
    group_size = HEADS // KV_HEADS
    query_heads = head_rows(query_loc, kv_count)
    grad_heads = head_rows(attn_grad, kv_count)
    seq_base = lax.axis_index("seq") * tok_rows
    query_pos = jnp.tile(seq_base + jnp.arange(tok_rows, dtype=jnp.int32), group_size)
    head_count = group_size * tok_rows
    initial = (
        jnp.full((kv_count, head_count), NEG_FILL, jnp.float32),
        jnp.zeros((kv_count, head_count), jnp.float32),
        jnp.zeros((kv_count, head_count, HEAD_DIM), jnp.float32),
    )
    fold_forward = forward_fold(query_heads, query_pos)
    every_key, every_value = (
        lax.all_gather(key_loc, "seq", axis=0, tiled=True),
        lax.all_gather(value_loc, "seq", axis=0, tiled=True),
    )
    run_max, run_sum, run_out = fold_forward(initial, (every_key, every_value), jnp.int32(0))
    log_norm = run_max + jnp.log(run_sum)
    attn_out = run_out / run_sum[..., None]
    delta_row = jnp.sum(grad_heads.astype(jnp.float32) * attn_out, axis=-1)
    zero_dq = jnp.zeros((kv_count, head_count, HEAD_DIM), jnp.float32)
    full_len = tok_rows * lax.axis_size("seq")
    zero_terms = jnp.zeros((full_len, kv_count * HEAD_DIM), jnp.float32)
    back_init = (zero_dq, zero_terms, zero_terms)
    fold_backward = backward_fold(query_heads, grad_heads, log_norm, delta_row, query_pos)
    back_out = fold_backward(back_init, (every_key, every_value), jnp.int32(0))
    query_grad = token_cols(back_out[0], tok_rows).astype(jnp.bfloat16)
    dk_rows, dv_rows = (
        lax.psum_scatter(back_out[1], "seq", scatter_dimension=0, tiled=True),
        lax.psum_scatter(back_out[2], "seq", scatter_dimension=0, tiled=True),
    )
    key_grad = dk_rows.astype(jnp.bfloat16)
    value_grad = dv_rows.astype(jnp.bfloat16)
    return (query_grad[None], key_grad[None], value_grad[None], router_grad, expert_grad[None])


VMEM_LIMIT = 24 * 1024 * 1024
NT = (((1,), (1,)), ((), ()))
TN = (((0,), (0,)), ((), ()))
LANES = 128


def params():
    return pltpu.CompilerParams(vmem_limit_bytes=VMEM_LIMIT)


def partner(array, axis, count, distance):
    return lax.ppermute(array, axis, [(i, i ^ distance) for i in range(count)])


def iota(shape, axis):
    return lax.broadcasted_iota(jnp.int32, shape, axis)


def whole(shape):
    return pl.BlockSpec(shape, lambda *_: (0,) * len(shape))


def column(matrix, lane):
    lanes = iota(matrix.shape, 1)
    return jnp.sum(jnp.where(lanes == lane, matrix, 0.0), axis=1, keepdims=True)


def as_rows(matrix):
    return jnp.transpose(matrix)[0:8]


def as_columns(rows):
    count = rows.shape[1]
    return jnp.transpose(
        jnp.concatenate([rows, jnp.zeros((LANES - rows.shape[0], count), rows.dtype)], axis=0)
    )


def prepare_kernel(meta, route, router_pad, resid, saved, rows, place, saved_tok):
    my_expert = meta[2]
    tok_rows = resid.shape[0]
    capacity = saved.shape[0]
    member = (route[:, 0:1] == my_expert) | (route[:, 1:2] == my_expert)
    earlier = (iota((tok_rows, tok_rows), 1) < iota((tok_rows, tok_rows), 0)).astype(
        jnp.float32
    ).astype(jnp.bfloat16)
    member_wide = jnp.broadcast_to(member.astype(jnp.float32), (tok_rows, capacity))
    slot = jnp.dot(earlier, member_wide.astype(jnp.bfloat16), preferred_element_type=jnp.float32)
    slot_lane = iota((tok_rows, capacity), 1).astype(jnp.float32)
    placed = jnp.where(slot == slot_lane, member_wide, 0.0).astype(jnp.bfloat16)
    place[...] = placed
    saved_tok[...] = jnp.dot(placed, saved[...], preferred_element_type=jnp.float32).astype(
        jnp.bfloat16
    )
    resid_f32 = resid[...].astype(jnp.float32)
    raw = jnp.dot(resid[...], router_pad[...], preferred_element_type=jnp.float32)
    square = jnp.sum(resid_f32 * resid_f32, axis=1, keepdims=True)
    lanes = iota(raw.shape, 1)
    rows[...] = as_rows(jnp.where(lanes == EXPERTS_ROW, square, raw))


def spread(my_expert, refs, rows):
    for k, ref in enumerate(refs):
        yield my_expert ^ k, lambda ref=ref: ref[rows].astype(jnp.float32)


def flat(rows):
    return jnp.concatenate([rows[q : q + 1] for q in range(rows.shape[0])], axis=1)


def gate_grad_kernel(meta, route, rows, saved_tok, resid, router_rows, *refs):
    blocks, message = refs[:-1], refs[-1]
    my_expert = meta[2]
    tok_rows = route.shape[0]
    feats = blocks[0].shape[1]
    total = jnp.zeros((tok_rows, 1), jnp.float32)
    for index, grad in spread(my_expert, blocks, slice(0, tok_rows)):
        start = pl.multiple_of(index * feats, LANES)
        saved = saved_tok[:, pl.ds(start, feats)].astype(jnp.float32)
        total = total + jnp.sum(grad() * saved, axis=1, keepdims=True)
    first = (route[:, 0:1] == my_expert).astype(jnp.float32)
    second = (route[:, 1:2] == my_expert).astype(jnp.float32)
    signed = as_rows(jnp.broadcast_to((first - second) * total, (tok_rows, LANES)))
    rest = flat(jnp.where(iota(signed.shape, 0) == EXPERTS_ROW + 1, signed, rows[...]))
    tile = router_rows[...].astype(jnp.float32)
    at = iota(tile.shape, 0)
    for piece in range(3):
        part = rest.astype(jnp.bfloat16).astype(jnp.float32)
        tile = jnp.where(at == EXPERTS_ROW + piece, part, tile)
        rest = rest - part
    message[0:tok_rows] = resid[...]
    message[tok_rows:] = tile.astype(jnp.bfloat16)


def told(message):
    tok_rows = message.shape[0] - ROW_TILE
    tile = message[tok_rows:].astype(jnp.float32)
    one, two, three = (tile[EXPERTS_ROW + p : EXPERTS_ROW + p + 1] for p in range(3))
    line = (one + two) + three
    return jnp.concatenate(
        [line[:, at : at + tok_rows] for at in range(0, 8 * tok_rows, tok_rows)], axis=0
    )


def router_kernel(meta, total_tokens, route, m0, m1, m2, m3, columns, router_part):
    my_expert = meta[2]
    experts = EXPERTS_ROW
    sums = as_columns((told(m0) + told(m1)) + (told(m2) + told(m3)))
    resid = m0[0 : route.shape[0]]
    lanes = iota(sums.shape, 1)
    inv_rms = lax.rsqrt(column(sums, experts) / D + NORM_EPS)
    delta = column(sums, experts + 1)
    raw = jnp.where(lanes < experts, sums, 0.0)
    logits = raw * inv_rms
    first = route[:, 0:1]
    second = route[:, 1:2]
    logit_a = jnp.sum(jnp.where(lanes == first, logits, 0.0), axis=1, keepdims=True)
    logit_b = jnp.sum(jnp.where(lanes == second, logits, 0.0), axis=1, keepdims=True)
    gate_a = jax.nn.sigmoid(logit_a - logit_b)
    gate_b = jax.nn.sigmoid(logit_b - logit_a)
    gate = jnp.where(first == my_expert, gate_a, 0.0) + jnp.where(second == my_expert, gate_b, 0.0)
    dlogit_a = gate_a * gate_b * delta
    dlogits = jnp.where(lanes == first, dlogit_a, 0.0) - jnp.where(lanes == second, dlogit_a, 0.0)
    along_raw = jnp.sum(raw * dlogits, axis=1, keepdims=True)
    scaled = inv_rms * dlogits
    along = along_raw * inv_rms * inv_rms * inv_rms / D
    columns[...] = jnp.where(
        lanes < experts, scaled, jnp.where(lanes == experts, along, gate)
    )
    router_part[...] = (
        jnp.dot(
            as_rows(scaled),
            resid.astype(jnp.float32),
            precision=lax.Precision.HIGHEST,
            preferred_element_type=jnp.float32,
        )
        / total_tokens
    )


def expert_grad_kernel(meta, columns, place, *refs):
    blocks, expert_grad = refs[:-1], refs[-1]
    tok_rows = place.shape[0]
    feats = blocks[0].shape[1]
    gate = column(columns[...], EXPERTS_ROW + 1)
    for index, grad in spread(meta[2], blocks, slice(0, tok_rows)):
        start = pl.multiple_of(index * feats, LANES)
        value = (gate * grad()).astype(jnp.bfloat16)
        expert_grad[:, pl.ds(start, feats)] = lax.dot_general(
            place[...], value, TN, preferred_element_type=jnp.float32
        ).astype(jnp.bfloat16)


def times(rows, weight):
    return lax.dot_general(rows, weight, NT, preferred_element_type=jnp.float32)


def half_of(part, half):
    return pl.ds(pl.multiple_of(part * half, LANES), half)


def project_kernel(meta, own, near, across, *refs):
    grads, resids, total, rows = refs[0:4], refs[4:8], refs[8], refs[9]
    my_core, my_seq, my_expert = meta[0], meta[1], meta[2]
    tok_rows = grads[0].shape[0]
    for k in range(4):
        rows[my_expert ^ k, 0:tok_rows] = grads[k][...]
        rows[my_expert ^ k, tok_rows:] = resids[k][...]
    total[...] = times(rows[my_seq], own[...]) + times(rows[my_seq ^ (1 + my_core)], near[...])
    total[:, half_of(my_core, across.shape[0])] += times(rows[my_seq ^ 3], across[...])


def project_rest_kernel(meta, far, across, rows, most, total):
    my_core, my_seq = meta[0], meta[1]
    total[...] = most[...] + times(rows[my_seq ^ (2 - my_core)], far[...])
    total[:, half_of(1 - my_core, across.shape[0])] += times(rows[my_seq ^ 3], across[...])


def stacked(matrix, heads):
    return jnp.concatenate(
        [matrix[:, h * HEAD_DIM : (h + 1) * HEAD_DIM] for h in range(heads)], axis=0
    )


def distances(core):
    return 0, 2 - core, 1 + core, 3


def four(pair, pair_x, pair_y):
    count = pair.shape[0]
    return pair[...], pair_x[...], pair_y[0:count], pair_y[count:]


def forward_kernel(meta, query, pair, pair_x, pair_y, probs, attn_out):
    my_seq = meta[1]
    tok_rows = query.shape[0]
    v0, v1, v2, v3 = four(pair, pair_x, pair_y)
    kv_count = v0.shape[1] // (2 * HEAD_DIM)
    group = query.shape[1] // (kv_count * HEAD_DIM)
    rows = group * tok_rows
    position = lax.rem(iota((rows, tok_rows), 0), tok_rows)
    key_at = iota((rows, tok_rows), 1)
    allowed = jnp.concatenate(
        [
            key_at + ((my_seq ^ k) - my_seq) * tok_rows <= position
            for k in distances(meta[0])
        ],
        axis=1,
    )
    for kv in range(kv_count):
        heads = stacked(query[:, kv * group * HEAD_DIM : (kv + 1) * group * HEAD_DIM], group)
        key_cols = slice(kv * HEAD_DIM, (kv + 1) * HEAD_DIM)
        value_cols = slice((kv_count + kv) * HEAD_DIM, (kv_count + kv + 1) * HEAD_DIM)
        keys = jnp.concatenate([v[:, key_cols] for v in (v0, v1, v2, v3)], axis=0)
        values = jnp.concatenate([v[:, value_cols] for v in (v0, v1, v2, v3)], axis=0)
        scores = lax.dot_general(heads, keys, NT, preferred_element_type=jnp.float32) * (
            HEAD_DIM ** (-0.5)
        )
        row_max = jnp.max(jnp.where(allowed, scores, NEG_FILL), axis=1, keepdims=True)
        weights = jnp.exp(jnp.where(allowed, scores - row_max, NEG_FILL))
        row_total = jnp.sum(weights, axis=1, keepdims=True)
        mixed = (
            jnp.dot(weights.astype(jnp.bfloat16), values, preferred_element_type=jnp.float32)
            / row_total
        )
        log_norm = row_max + jnp.log(row_total)
        probs[kv] = jnp.exp(jnp.where(allowed, scores - log_norm, NEG_FILL))
        for h in range(group):
            at = (kv * group + h) * HEAD_DIM
            attn_out[:, at : at + HEAD_DIM] = mixed[h * tok_rows : (h + 1) * tok_rows]


def backward_kernel(
    meta, columns, projected, router_a, router_b, query, probs, attn_out, pair, pair_x,
    pair_y, dquery, router, d0, d1, d2, d3,
):
    tok_rows = query.shape[0]
    v0, v1, v2, v3 = four(pair, pair_x, pair_y)
    kv_count = v0.shape[1] // (2 * HEAD_DIM)
    group = query.shape[1] // (kv_count * HEAD_DIM)
    wide = group * HEAD_DIM
    score_scale = HEAD_DIM ** (-0.5)
    cols = columns[...]
    weights = [column(cols, e) for e in range(EXPERTS_ROW)]
    along = column(cols, EXPERTS_ROW)
    for kv in range(kv_count):
        here = slice(kv * wide, (kv + 1) * wide)
        attn_grad = projected[0:tok_rows, here] - along * projected[tok_rows : 2 * tok_rows, here]
        for e in range(EXPERTS_ROW):
            attn_grad = attn_grad + weights[e] * projected[2 * tok_rows + e : 2 * tok_rows + e + 1, here]
        grads = stacked(attn_grad.astype(jnp.bfloat16), group)
        heads = stacked(query[:, here], group)
        mixed = stacked(attn_out[:, here], group)
        key_cols = slice(kv * HEAD_DIM, (kv + 1) * HEAD_DIM)
        value_cols = slice((kv_count + kv) * HEAD_DIM, (kv_count + kv + 1) * HEAD_DIM)
        keys = jnp.concatenate([v[:, key_cols] for v in (v0, v1, v2, v3)], axis=0)
        values = jnp.concatenate([v[:, value_cols] for v in (v0, v1, v2, v3)], axis=0)
        delta = jnp.sum(grads.astype(jnp.float32) * mixed, axis=1, keepdims=True)
        dprobs = lax.dot_general(grads, values, NT, preferred_element_type=jnp.float32)
        chances = probs[kv]
        dscores = (chances * (dprobs - delta)).astype(jnp.bfloat16)
        dheads = (
            jnp.dot(dscores, keys, preferred_element_type=jnp.float32) * score_scale
        ).astype(jnp.bfloat16)
        for h in range(group):
            at = (kv * group + h) * HEAD_DIM
            dquery[:, at : at + HEAD_DIM] = dheads[h * tok_rows : (h + 1) * tok_rows]
        dkeys = lax.dot_general(dscores, heads, TN, preferred_element_type=jnp.float32) * score_scale
        dvalues = lax.dot_general(
            chances.astype(jnp.bfloat16), grads, TN, preferred_element_type=jnp.float32
        )
        for k, out in enumerate((d0, d1, d2, d3)):
            part = slice(k * tok_rows, (k + 1) * tok_rows)
            out[0:tok_rows, key_cols] = dkeys[part].astype(out.dtype)
            out[0:tok_rows, value_cols] = dvalues[part].astype(out.dtype)
    halves = paired(router_a[...] + router_b[...], router.shape[1])
    router[...] = halves
    for out in (d1, d2, d3):
        out[tok_rows:] = halves


def paired(part, width):
    high = part.astype(jnp.bfloat16).astype(jnp.float32)
    pieces = [
        half[0:EXPERTS_ROW, at : at + width]
        for half in (high, part - high)
        for at in range(0, part.shape[1], width)
    ]
    return jnp.concatenate(pieces, axis=0).astype(jnp.bfloat16)


def finish_kernel(meta, router, own, t1, t2, t3, key_grad, value_grad, router_grad):
    tok_rows, kv_width = key_grad.shape
    total = own[...]
    for part in (t1, t2, t3):
        total = total + part[0:tok_rows].astype(jnp.float32)
    total = total.astype(jnp.bfloat16)
    key_grad[...] = total[:, 0:kv_width]
    value_grad[...] = total[:, kv_width:]
    sums = []
    for rows in (router[...], t1[tok_rows:], t2[tok_rows:], t3[tok_rows:]):
        rows = rows.astype(jnp.float32)
        count = rows.shape[0] // 2
        sums.append(rows[0:count] + rows[count:])
    first = meta[0] == 0
    one, two = jnp.where(first, sums[2], sums[1]), jnp.where(first, sums[1], sums[2])
    total = (sums[0] + one) + (two + sums[3])
    width = total.shape[1]
    for piece in range(total.shape[0] // EXPERTS_ROW):
        router_grad[:, piece * width : (piece + 1) * width] = total[
            piece * EXPERTS_ROW : (piece + 1) * EXPERTS_ROW
        ]


EXPERTS_ROW = 4
ROW_TILE = 16


def call(kernel, meta, args, outs):
    shapes = [jax.ShapeDtypeStruct(s, t) for s, t in outs]
    return pl.pallas_call(
        kernel,
        out_shape=shapes,
        in_specs=[pl.BlockSpec(memory_space=pltpu.SMEM)]
        + [pl.BlockSpec(memory_space=pltpu.VMEM)] * len(args),
        out_specs=[pl.BlockSpec(memory_space=pltpu.VMEM)] * len(shapes),
        compiler_params=params(),
    )(meta, *args)


def local_fast(
    query_in, key_in, value_in, resid_in, out_grad, o_weight, router_weight, route_ids, expert_out
):
    query = query_in[0]
    resid = resid_in[0]
    grad = out_grad[0]
    route = route_ids[0]
    saved = expert_out[0]
    tok_rows, feats = resid.shape
    capacity, width = saved.shape
    seq_n, expert_n, dp_n = lax.axis_size("seq"), lax.axis_size("expert"), lax.axis_size("dp")
    core = lax.axis_index("dp")
    meta = jnp.stack([core, lax.axis_index("seq"), lax.axis_index("expert")]).astype(jnp.int32)
    f32, bf16 = jnp.float32, jnp.bfloat16

    def over_expert(array):
        return [array] + [partner(array, "expert", expert_n, k) for k in range(1, expert_n)]

    def over_seq(array):
        return [partner(array, "seq", seq_n, k) for k in range(1, seq_n)]

    def over_both(array, step):
        pairs = [
            (c * seq_n + i, c * seq_n + (i ^ step(c))) for c in range(dp_n) for i in range(seq_n)
        ]
        return lax.ppermute(array, ("dp", "seq"), pairs)

    half_rows = o_weight.shape[0] // dp_n
    router_rows = jnp.pad(router_weight.T, ((0, ROW_TILE - EXPERTS_ROW), (0, 0)))
    grads = over_expert(grad)
    pair = jnp.concatenate([key_in[0], value_in[0]], axis=1)
    pair_x = over_both(pair, lambda c: distances(c)[1])
    weight_near = over_both(o_weight, lambda c: 1 + c)
    router_pad = jnp.pad(router_weight, ((0, 0), (0, LANES - router_weight.shape[1])))
    rows, place, saved_tok = call(
        prepare_kernel,
        meta,
        (route, router_pad, resid, saved),
        (
            ((8, tok_rows), f32),
            ((tok_rows, capacity), bf16),
            ((tok_rows, width), bf16),
        ),
    )
    grads[1:], weight_near, rows, place, saved_tok, pair_x = lax.optimization_barrier(
        (grads[1:], weight_near, rows, place, saved_tok, pair_x)
    )
    (own_rows,) = call(
        gate_grad_kernel,
        meta,
        (route, rows, saved_tok, resid, router_rows, *grads),
        (((tok_rows + ROW_TILE, feats), bf16),),
    )
    resids = over_expert(own_rows)
    pair_y = over_both(jnp.concatenate([pair, pair_x], axis=0), lambda c: distances(c)[2])
    pairs = (pair, pair_x, pair_y)
    across = lax.dynamic_slice_in_dim(weight_near, core * half_rows, half_rows, axis=0)
    across_mine = over_both(across, lambda c: 2 - c)

    kv_width = key_in.shape[2]
    kv_count = kv_width // HEAD_DIM
    group = query.shape[1] // kv_width
    probs, attn_out = call(
        forward_kernel,
        meta,
        (query, *pairs),
        (
            ((kv_count, group * tok_rows, seq_n * tok_rows), f32),
            (query.shape, f32),
        ),
    )
    model_rows = o_weight.shape[0]
    all_rows = 2 * tok_rows + ROW_TILE
    across_mine, resids[1:], probs, attn_out, weight_near = lax.optimization_barrier(
        (across_mine, resids[1:], probs, attn_out, weight_near)
    )
    weight_far = partner(weight_near, "dp", dp_n, 1)
    across_other = partner(across_mine, "dp", dp_n, 1)
    all_shape = (all_rows, model_rows)
    most, staged = call(
        project_kernel,
        meta,
        (o_weight, weight_near, across_mine, *grads, *resids),
        ((all_shape, f32), ((expert_n, all_rows, feats), bf16)),
    )
    (projected,) = call(
        project_rest_kernel,
        meta,
        (weight_far, across_other, staged, most),
        ((all_shape, f32),),
    )
    total_tokens = dp_n * seq_n * tok_rows
    columns, router_part = call(
        lambda meta, *refs: router_kernel(meta, total_tokens, *refs),
        meta,
        (route, *resids),
        (((tok_rows, LANES), f32), ((8, feats), f32)),
    )
    term_width = 2 * kv_width
    router_rows = 2 * EXPERTS_ROW * feats // term_width
    term = (tok_rows + router_rows, term_width)
    router_other = partner(router_part, "dp", dp_n, 1)
    query_grad, router_term, own, *key_terms = call(
        backward_kernel,
        meta,
        (columns, projected, router_part, router_other, query, probs, attn_out, *pairs),
        (
            (query.shape, bf16),
            ((router_rows, term_width), bf16),
            ((tok_rows, term_width), f32),
            *(((term, bf16),) * 3),
        ),
    )
    back = [
        over_both(term, lambda c: distances(c)[at]) for at, term in enumerate(key_terms, start=1)
    ]
    columns, own = lax.optimization_barrier((columns, own))
    (expert_grad,) = call(
        expert_grad_kernel, meta, (columns, place, *grads), (((capacity, width), bf16),)
    )
    key_grad, value_grad, router_grad = call(
        finish_kernel,
        meta,
        (router_term, own, *back),
        (
            ((tok_rows, kv_width), bf16),
            ((tok_rows, kv_width), bf16),
            ((EXPERTS_ROW, feats), f32),
        ),
    )
    router_grad = router_grad.T
    return (query_grad[None], key_grad[None], value_grad[None], router_grad, expert_grad[None])


def solution(mesh):
    placed = (
        P("dp", "seq", "expert"),
        P("dp", "seq", "expert"),
        P("dp", "seq", "expert"),
        P("dp", "seq", "expert"),
        P("dp", "seq", "expert"),
        P("expert", "seq"),
        P("expert", None),
        P("dp", "seq", None),
        P("dp", ("seq", "expert"), None),
    )
    four = mesh.shape["dp"] == 2 and mesh.shape["seq"] == 4 and mesh.shape["expert"] == 4
    return jax.shard_map(
        local_fast if four else local,
        mesh=mesh,
        in_specs=placed,
        out_specs=(
            P("dp", "seq", "expert"),
            P("dp", "seq", "expert"),
            P("dp", "seq", "expert"),
            P("expert", None),
            P("dp", ("seq", "expert"), None),
        ),
        check_vma=False,
    )
```
